256 devices in a mesh: dp: 32 (over x, z), tile: 8 (over y, core).
Axes of the slice: x: 4, y: 4, z: 8, core: 2. Of those that a mesh axis runs over, the one named last changes fastest.
Arguments:
- queries: bfloat16 [16384, 768], P('dp'), may hold values from -30 to 30
- passages: bfloat16 [262144, 768], P(('dp', 'tile')), may hold values from -30 to 30
- query_cluster: int32 [16384], P('dp'), may hold values from 0 to 127, as said below
- passage_cluster: int32 [262144], P(('dp', 'tile')), may hold values from 0 to 127, as said below
- positive: int32 [16384], P('dp'), may hold values from 0 to 262143, as said below
Outputs:
- query_grad: bfloat16 [16384, 768], P('dp')
- passage_grad: bfloat16 [262144, 768], P(('dp', 'tile'))
The draws below stay inside these ranges and needn't reach their ends.
Inputs may be any that keep to these rules, and one draw needn't show every extreme that they name: `query_cluster`: among the 512 queries of one dp index, at most 32 have clusters of one owner o (clusters o * 4 to o * 4 + 3), and in every draw some owner receives exactly 32 of them. `passage_cluster`: the passages on dp index d belong to clusters d * 4 to d * 4 + 3; every cluster has a passage. passage_cluster[positive[i]] == query_cluster[i].
All inputs are finite; a program needn't handle non-finite values.
Results may differ from the reference program's by a relative error of at most 0.015.
Values may be sent and summed in bfloat16 or wider, within the bound.
A program may use at most 64 MiB of HBM per device.

```python
import math
import jax
import jax.numpy as jnp
from jax import lax

D = 768
Q_DEV = 512
P_DEV = 1024
CL_OWN = 4
CAP = 32
NQ = 16384
NP = 262144
N_DP = 32
N_TILE = 8


def cluster_layout(key):
    key = jax.random.fold_in(key, 11)
    keys = jax.random.split(key, 5)
    owner_rows = P_DEV * N_TILE
    row_ids = jnp.arange(NP, dtype=jnp.int32)
    row_in_owner = row_ids % owner_rows
    row_owner = row_ids // owner_rows
    first_pick = jax.random.randint(keys[0], (NP,), 0, CL_OWN)
    second_pick = jax.random.randint(keys[1], (NP,), 0, CL_OWN)
    local_cluster = jnp.where(row_in_owner < CL_OWN, row_in_owner, jnp.minimum(first_pick, second_pick))
    passage_cluster = (row_owner * CL_OWN + local_cluster).astype(jnp.int32)
    slot_count = 2 * Q_DEV
    slot_owner = jnp.arange(slot_count, dtype=jnp.int32) // CAP
    full_owner = jax.random.randint(keys[2], (N_DP,), 0, N_DP)
    source_keys = jax.random.split(keys[3], N_DP)

    def one_source(source_key, favoured):
        split_keys = jax.random.split(source_key, 2)
        ranking = jax.random.permutation(split_keys[0], slot_count).astype(jnp.int32)
        ranking = jnp.where(slot_owner == favoured, slot_count + jnp.arange(slot_count, dtype=jnp.int32), ranking)
        chosen_slots = jnp.argsort(ranking, stable=True)[:Q_DEV - CAP]
        owners = jnp.concatenate([slot_owner[chosen_slots], jnp.full((CAP,), favoured, jnp.int32)])
        return owners[jax.random.permutation(split_keys[1], Q_DEV)]
    query_owner = jax.vmap(one_source)(source_keys, full_owner).reshape(NQ)
    offsets_in_owner = jax.random.randint(keys[4], (NQ,), 0, owner_rows)
    positive = (query_owner * owner_rows + offsets_in_owner).astype(jnp.int32)
    query_cluster = passage_cluster[positive]
    return (passage_cluster, query_cluster, positive)


def draw_passage_cluster(key, part):
    return cluster_layout(key)[0]


def draw_query_cluster(key, part):
    return cluster_layout(key)[1]


def draw_positive(key, part):
    return cluster_layout(key)[2]


def draw_queries(key, part):
    key = jax.random.fold_in(key, 3)
    noise_key = jax.random.fold_in(key, 0)
    noise = jnp.clip(jax.random.normal(noise_key, (NQ, D), jnp.float32), -6.0, 6.0)
    return noise.astype(jnp.bfloat16)


def draw_passages(key, part):
    key = jax.random.fold_in(key, 5)
    noise_key = jax.random.fold_in(key, 0)
    noise = jnp.clip(jax.random.normal(noise_key, (NP, D), jnp.float32), -6.0, 6.0)
    return noise.astype(jnp.bfloat16)


def setup_inputs(seed: int = 0) -> dict:
    seeds = jax.random.split(jax.random.key(seed), 6)
    return {
        "queries": draw_queries(jax.random.fold_in(seeds[5], 71), 0),
        "passages": draw_passages(jax.random.fold_in(seeds[5], 71), 0),
        "query_cluster": draw_query_cluster(jax.random.fold_in(seeds[5], 71), 0),
        "passage_cluster": draw_passage_cluster(jax.random.fold_in(seeds[5], 71), 0),
        "positive": draw_positive(jax.random.fold_in(seeds[5], 71), 0),
    }


NEGATIVE = -1e+30
SOFTMAX_TEMP = 2.0

def prefix_ends(width):
    twelfth = width // 12
    return [twelfth, 2 * twelfth, 4 * twelfth, 8 * twelfth, width]

def reference(queries, passages, query_cluster, passage_cluster, positive):
    prefix_limits = prefix_ends(D)
    starts = [0] + prefix_limits[:-1]
    query_count = queries.shape[0]
    slab = N_DP * CAP
    owner_rows = P_DEV * N_TILE
    owners = (query_cluster // CL_OWN).astype(jnp.int32)
    order = jnp.argsort(owners, stable=True).astype(jnp.int32)
    owner_ids = jnp.arange(N_DP, dtype=jnp.int32)
    counts = lax.optimization_barrier(jnp.sum((owners[:, None] == owner_ids[None, :]).astype(jnp.int32), axis=0)).astype(jnp.int32)
    offsets = (jnp.cumsum(counts) - counts).astype(jnp.int32)
    padded = jnp.concatenate([order, jnp.zeros((slab,), jnp.int32)])
    slot_ids = jnp.arange(slab, dtype=jnp.int32)
    column_ids = jnp.arange(owner_rows, dtype=jnp.int32)

    def one_owner(owner_index):
        picked = lax.dynamic_slice_in_dim(padded, offsets[owner_index], slab)
        valid = slot_ids < counts[owner_index]
        query_block = queries[picked]
        clusters = jnp.where(valid, query_cluster[picked], -1).astype(jnp.int32)
        first_row = (owner_index * owner_rows).astype(jnp.int32)
        passage_block = lax.dynamic_slice_in_dim(passages, first_row, owner_rows, 0)
        block_cluster = lax.dynamic_slice_in_dim(passage_cluster, first_row, owner_rows)
        targets = jnp.where(valid, positive[picked] - first_row, -1).astype(jnp.int32)
        member = clusters[:, None] == block_cluster[None, :]
        target_indicator = (targets[:, None] == column_ids[None, :]).astype(jnp.float32)
        full_scores = jnp.dot(query_block, passage_block.T, preferred_element_type=jnp.float32)
        logit_deltas = []
        for final_column in prefix_limits:
            if final_column == D:
                unscaled_scores = full_scores
            else:
                unscaled_scores = jnp.dot(query_block[:, :final_column], passage_block[:, :final_column].T, preferred_element_type=jnp.float32)
            scaled_scores = unscaled_scores * (SOFTMAX_TEMP / math.sqrt(final_column))
            highest = lax.optimization_barrier(jnp.max(jnp.where(member, scaled_scores, NEGATIVE), axis=1, keepdims=True))
            totals = lax.optimization_barrier(jnp.sum(jnp.where(member, jnp.exp(scaled_scores - highest), 0.0), axis=1, keepdims=True))
            log_total = highest + jnp.log(jnp.where(totals > 0, totals, 1.0))
            probabilities = jnp.where(member, jnp.exp(scaled_scores - log_total), 0.0)
            logit_deltas.append((probabilities - target_indicator) * (SOFTMAX_TEMP / math.sqrt(final_column)))
        weights = [None] * len(prefix_limits)
        running = None
        for target_position in reversed(range(len(prefix_limits))):
            running = logit_deltas[target_position] if running is None else running + logit_deltas[target_position]
            weights[target_position] = running.astype(jnp.bfloat16)
        query_parts = []
        passage_parts = []
        for target_position in range(len(prefix_limits)):
            start_col = starts[target_position]
            final_column = prefix_limits[target_position]
            tiled = weights[target_position].astype(jnp.float32).reshape(slab, N_TILE, P_DEV)
            piece = passage_block[:, start_col:final_column].astype(jnp.float32).reshape(N_TILE, P_DEV, final_column - start_col)
            per_tile = jnp.einsum('qtp,tpw->tqw', tiled, piece)
            rounded = lax.optimization_barrier(per_tile.astype(jnp.bfloat16))
            query_parts.append(lax.optimization_barrier(jnp.sum(rounded.astype(jnp.float32), axis=0)))
            passage_parts.append(jnp.dot(weights[target_position].T, query_block[:, start_col:final_column], preferred_element_type=jnp.float32))
        query_rows = jnp.concatenate(query_parts, axis=1).astype(jnp.bfloat16)
        passage_rows = jnp.concatenate(passage_parts, axis=1).astype(jnp.bfloat16)
        flat_index = jnp.where(valid, picked, query_count).astype(jnp.int32)
        return (query_rows, passage_rows, flat_index)
    query_rows, passage_rows, flat_index = lax.map(one_owner, owner_ids)
    query_grad = jnp.zeros((query_count, D), jnp.bfloat16).at[flat_index.reshape(-1)].set(query_rows.reshape(-1, D), mode='drop')
    passage_grad = passage_rows.reshape(-1, D)
    return (query_grad, passage_grad)
```

```python
import functools
import math

import jax
import jax.numpy as jnp
from jax import lax
from jax.experimental import pallas as pl
from jax.experimental.pallas import tpu as pltpu
from jax.sharding import PartitionSpec as P

F32 = jnp.float32
BF16 = jnp.bfloat16
I32 = jnp.int32

NX, NZ, NY, NC = 4, 8, 4, 2
CL_OWN = 4
CAP = 32
NEGATIVE = -1e30
CUTS = (64, 128, 256, 512, 768)
WIDTH = 768
META = 128
ROW = WIDTH + META
SCALES = tuple(2.0 / math.sqrt(k) for k in CUTS)
LOG2E = math.log2(math.e)
BLOCK = 128
PAIR = 2 * BLOCK
SLOTS = 8 * BLOCK
HALF = WIDTH // 2

PLACE = ((0, 0), (0, 1), (1, 0), (3, 0), (1, 1), (3, 1), (2, 0), (2, 1))
MIRROR = tuple(PLACE.index(((NY - dy) % NY, dc)) for dy, dc in PLACE)


def nn(a, b):
    return lax.dot_general(a, b, (((1,), (0,)), ((), ())), preferred_element_type=F32)


def nt(a, b):
    return lax.dot_general(a, b, (((1,), (1,)), ((), ())), preferred_element_type=F32)


def iota(shape, dim):
    return lax.broadcasted_iota(I32, shape, dim)


def onehot(mask):
    return jnp.where(mask, 1.0, 0.0).astype(BF16)


def fold(value, op):
    return op(value.reshape(value.shape[0] // 8, 8, value.shape[1]), axis=0)


def kernel(qc_ref, pos_ref, pc_ref, q_ref, p_hbm, qg_ref, pg_hbm,
           p_ref, p0_ref, p1_ref, pt_ref, xs, xr, zs, agb, q0_ref,
           prob, wt, msc, stat, stat_in, lse_ref, gt, sib, comb, half_in, from_m, from_p,
           zbs, zb, xbs, xb, fg, bsel_ref, fsel_ref, pg_ref,
           ssem, rsem, lsem):
    n_pass = p_ref.shape[0]
    dp = lax.axis_index("dp")
    tile = lax.axis_index("tile")
    x, z = lax.div(dp, NZ), lax.rem(dp, NZ)
    y, core = lax.div(tile, NC), lax.rem(tile, NC)

    def at(dx=0, dz=0, dy=0, dc=0):
        return (lax.rem(x + dx, NX) * NZ + lax.rem(z + dz, NZ),
                lax.rem(y + dy, NY) * NC + lax.rem(core + dc, NC))

    started = []

    def send(src, dst, where):
        i = len(started)
        copy = pltpu.make_async_remote_copy(
            src_ref=src, dst_ref=dst, send_sem=ssem.at[i], recv_sem=rsem.at[i],
            device_id=where, device_id_type=pl.DeviceIdType.MESH)
        copy.start()
        started.append(copy)
        return copy

    load_p = pltpu.make_async_copy(p_hbm, p_ref, lsem.at[0])
    load_p.start()

    barrier = pltpu.get_barrier_semaphore()
    partners = ([at(dx=d) for d in range(1, NX)] + [at(dz=d) for d in range(1, NZ)]
                + [at(dy=dy, dc=dc) for dy, dc in PLACE[1:]])
    for where in partners:
        pl.semaphore_signal(barrier, inc=1, device_id=where, device_id_type=pl.DeviceIdType.MESH)

    nq = q_ref.shape[0]
    cluster = qc_ref[...]
    owner = lax.shift_right_logical(cluster, 2)
    local = lax.bitwise_and(cluster, 3)
    n_owner = NX * NZ
    own = jnp.where(iota((n_owner, nq), 0) == owner, 1.0, 0.0)
    before = onehot(iota((nq, nq), 0) < iota((nq, nq), 1))
    rank = jnp.sum(own * nn(own.astype(BF16), before), axis=0, keepdims=True)
    first = jnp.sum(jnp.where(owner < iota((n_owner, nq), 0), 1.0, 0.0), axis=1, keepdims=True)
    order = (rank + jnp.sum(own * first, axis=0, keepdims=True)).astype(I32)
    rank = rank.astype(I32)
    carrier = lax.bitwise_and(order, 7)
    line = lax.shift_right_logical(order, 3)
    dxs = lax.bitwise_and(lax.shift_right_logical(owner, 3) - x, NX - 1)
    dzs = lax.bitwise_and(lax.bitwise_and(owner, NZ - 1) - z, NZ - 1)
    code = dxs * 32 + dzs * 4 + lax.shift_right_logical(rank, 3)
    mine = carrier == tile
    pick = onehot(iota((BLOCK, nq), 0) == jnp.where(mine, code, -1))
    row = iota((META, nq), 0)
    target = lax.bitwise_and(pos_ref[...], 8 * n_pass - 1)
    high = lax.shift_right_logical(target, 6)
    low = lax.bitwise_and(target, 63)
    digits = jnp.where(row == 69, high, jnp.where(row == 70, low, 0))
    digits = jnp.where((row == local + 64) | (row == 68), 1, digits)
    meta = nt(pick, digits.astype(F32).astype(BF16))
    meta = jnp.where(iota((BLOCK, META), 1) == 68, 1.0 - meta, meta)
    xs[:, :WIDTH] = nn(pick, q_ref[...]).astype(BF16)
    xs[:, WIDTH:] = meta.astype(BF16)

    pl.semaphore_wait(barrier, len(partners))

    x_copies = [send(xs.at[pl.ds(d * 32, 32)], xr.at[pl.ds(d * 32, 32)], at(dx=d)) for d in range(1, NX)]
    xr[pl.ds(0, 32)] = xs[pl.ds(0, 32)]

    clusters = pc_ref[...]
    lane_row = iota((META, n_pass), 0)
    off = jnp.where((lane_row == clusters - CL_OWN * dp + 64) | (lane_row > 68) | (lane_row < 64), 0.0, NEGATIVE)
    eye = onehot(iota((BLOCK, BLOCK), 0) == iota((BLOCK, BLOCK), 1))
    load_p.wait()
    lane = iota((n_pass, 128), 1)
    head = p_ref[:, :128].astype(F32)
    p0_ref[...] = jnp.where(lane < 64, head, off.T).astype(BF16)
    p1_ref[...] = jnp.where(lane < 64, 0.0, head).astype(BF16)

    i, c = iota((BLOCK, BLOCK), 0), iota((BLOCK, BLOCK), 1)
    to_z = onehot(c == lax.bitwise_and(lax.shift_right_logical(i, 2), 3) * 32
                  + lax.shift_right_logical(i, 4) * 4 + lax.bitwise_and(i, 3))
    to_x = onehot(c == lax.bitwise_and(lax.shift_right_logical(i, 2), 7) * 16
                  + lax.shift_right_logical(i, 5) * 4 + lax.bitwise_and(i, 3))
    for copy in x_copies:
        copy.wait_recv()
    zs[...] = nn(to_z, xr[...]).astype(BF16)
    z_copies = [send(zs.at[pl.ds(d * 16, 16)], agb.at[pl.ds(d * 16, 16)], at(dz=d)) for d in range(1, NZ)]
    agb[pl.ds(0, 16)] = zs[pl.ds(0, 16)]

    for b in range(WIDTH // 128):
        pt_ref[pl.ds(b * 128, 128)] = nt(eye, p_ref[:, b * 128:(b + 1) * 128]).astype(BF16)
    lines = nq // 8
    pick_line = onehot(iota((lines, nq), 0) == jnp.where(mine, line, -1))
    bsel_ref[...] = nt(pick_line, pick).astype(BF16)
    cdy = lax.bitwise_and(lax.shift_right_logical(carrier, 1) - y, NY - 1)
    cdc = lax.bitwise_and(carrier - core, 1)
    place = jnp.where(cdy == 0, cdc, jnp.where(cdy == 2, 6 + cdc, jnp.where(cdy == 1, 2, 3) + 2 * cdc))
    spread = onehot(iota((nq, nq), 0) == place * lines + line)
    fsel_ref[...] = nt(onehot(iota((nq, nq), 0) == iota((nq, nq), 1)), spread).astype(BF16)
    stat[...] = jnp.zeros_like(stat)
    lse_ref[...] = jnp.zeros_like(lse_ref)
    for copy in z_copies:
        copy.wait_recv()

    def gather_start(buf, rows):
        blk = lambda s: buf.at[pl.ds(s * rows, rows)]
        return [send(blk(0), blk(1), at(dc=1)), send(blk(0), blk(3), at(dy=1)), send(blk(0), blk(2), at(dy=3))]

    def gather_near(buf, rows, near):
        blk = lambda s: buf.at[pl.ds(s * rows, rows)]
        part = lambda s, h: buf.at[pl.ds(s * rows + h * (rows // 2), rows // 2)]
        near[1].wait_recv()
        near[2].wait_recv()
        return [send(part(3, 0), part(6, 0), at(dy=1)), send(part(2, 1), part(6, 1), at(dy=3)),
                send(blk(2), blk(4), at(dc=1)), send(blk(3), blk(5), at(dc=1))]

    def gather_far(buf, rows, far):
        blk = lambda s: buf.at[pl.ds(s * rows, rows)]
        far[0].wait_recv()
        far[1].wait_recv()
        return send(blk(6), blk(7), at(dc=1))

    stat_copies = [None] * 8

    def first_pass(pair):
        rows = pl.ds(pair * PAIR, PAIR)
        cols = pl.ds(pair * PAIR, PAIR)
        q0_ref[...] = jnp.where(iota((PAIR, 128), 1) < 64, agb[rows, 0:128].astype(F32),
                                agb[rows, WIDTH:ROW].astype(F32)).astype(BF16)
        step = 256

        def scores(j, tops):
            js = pl.ds(pl.multiple_of(j * step, step), step)
            value = nt(p0_ref[js], q0_ref[...])
            prob[0, js, cols] = value
            out = [jnp.maximum(tops[0], fold(value, jnp.max))]
            for m in range(1, 5):
                left = p1_ref[js] if m == 1 else p_ref[js, CUTS[m - 1]:CUTS[m]]
                right = agb[rows, 0:128] if m == 1 else agb[rows, CUTS[m - 1]:CUTS[m]]
                value = value + nt(left, right)
                prob[m, js, cols] = value
                out.append(jnp.maximum(tops[m], fold(value, jnp.max)))
            return tuple(out)

        tops = lax.fori_loop(0, n_pass // step, scores, (jnp.full((8, PAIR), -3e38, F32),) * 5)
        tops = [jnp.max(t, axis=0, keepdims=True) for t in tops]
        small = 64

        def exps(j, sums):
            js = pl.ds(pl.multiple_of(j * small, small), small)
            out = []
            for m in range(5):
                e = jnp.exp2((prob[m, js, cols] - tops[m]) * (SCALES[m] * LOG2E))
                prob[m, js, cols] = e
                out.append(sums[m] + fold(e, jnp.sum))
            return tuple(out)

        sums = lax.fori_loop(0, n_pass // small, exps, (jnp.zeros((8, PAIR), F32),) * 5)
        for m in range(5):
            top = tops[m] * SCALES[m]
            total = jnp.sum(sums[m], axis=0, keepdims=True)
            msc[m:m + 1, cols] = top
            lse = top + jnp.log(total)
            stat[2 * pair, m:m + 1] = lse[:, :BLOCK]
            stat[2 * pair + 1, m:m + 1] = lse[:, BLOCK:]
        for s in (2 * pair, 2 * pair + 1):
            if s:
                dy, dc = PLACE[s]
                stat_copies[s] = send(stat.at[s], stat_in.at[MIRROR[s]], at(dy=dy, dc=dc))

    near = gather_start(agb, BLOCK)
    near[0].wait_recv()
    first_pass(0)
    far = gather_near(agb, BLOCK, near)
    first_pass(1)
    last = gather_far(agb, BLOCK, far)
    far[2].wait_recv()
    far[3].wait_recv()
    first_pass(2)
    last.wait_recv()
    first_pass(3)

    for s in range(1, 8):
        stat_copies[s].wait_recv()
    parts = [stat[0]] + [stat_in[s] for s in range(1, 8)]
    top = functools.reduce(jnp.maximum, parts)
    lse_ref[0] = top + jnp.log(functools.reduce(jnp.add, [jnp.exp(v - top) for v in parts]))
    lse_copies = [None] * 8
    for s in range(7, 0, -1):
        dy, dc = PLACE[s]
        lse_copies[s] = send(lse_ref.at[0], lse_ref.at[MIRROR[s]], at(dy=dy, dc=dc))
    lse_from = {MIRROR[s]: lse_copies[s] for s in range(1, 8)}

    base = tile * n_pass
    pick_digit = jnp.where(iota((8, META), 1) == 69, 64.0,
                           jnp.where(iota((8, META), 1) == 70, 1.0, 0.0)).astype(BF16)

    def second_pass(pair):
        rows = pl.ds(pair * PAIR, PAIR)
        cols = pl.ds(pair * PAIR, PAIR)
        for s in (2 * pair, 2 * pair + 1):
            if s:
                lse_from[s].wait_recv()
        goal = nt(pick_digit, agb[rows, WIDTH:ROW])[0:1].astype(I32) - base
        lse = jnp.concatenate([lse_ref[2 * pair], lse_ref[2 * pair + 1]], axis=1)
        factor = [jnp.exp(msc[m:m + 1, cols] - lse[m:m + 1]) * SCALES[m] for m in range(5)]
        small = 64

        def weigh(j, carry):
            start = pl.multiple_of(j * small, small)
            js = pl.ds(start, small)
            hit = iota((small, PAIR), 0) == goal - start
            running = None
            for m in range(4, -1, -1):
                term = prob[m, js, cols] * factor[m]
                running = term if running is None else running + term
                drop = sum(SCALES[m:])
                wt[m, js, cols] = jnp.where(hit, running - drop, running).astype(BF16)
            return carry

        lax.fori_loop(0, n_pass // small, weigh, 0)
        for m in range(5):
            lo = CUTS[m - 1] if m else 0
            value = nn(pt_ref[lo:CUTS[m]], wt[m, :, cols]).astype(BF16)
            gt[2 * pair, lo:CUTS[m]] = value[:, :BLOCK]
            gt[2 * pair + 1, lo:CUTS[m]] = value[:, BLOCK:]

    def plus(*values):
        return functools.reduce(jnp.add, [v.astype(F32) for v in values])

    part = (pl.ds(0, HALF), pl.ds(HALF, HALF))
    second_pass(3)
    sib_far = send(gt.at[7], sib.at[3], at(dc=1))
    second_pass(2)
    sib_up = send(gt.at[4], sib.at[1], at(dc=1))
    sib_down = send(gt.at[5], sib.at[2], at(dc=1))
    sib_far.wait_recv()
    comb[2] = plus(gt[6], sib[3]).astype(BF16)
    half_up = send(comb.at[2, part[0]], half_in.at[0], at(dy=1))
    half_down = send(comb.at[2, part[1]], half_in.at[1], at(dy=3))
    second_pass(1)
    sib_up.wait_recv()
    sib_down.wait_recv()
    comb[0, part[1]] = plus(gt[2, part[1]], sib[1, part[1]]).astype(BF16)
    up_b = send(comb.at[0, part[1]], from_m.at[part[1]], at(dy=1))
    comb[1, part[0]] = plus(gt[3, part[0]], sib[2, part[0]]).astype(BF16)
    down_a = send(comb.at[1, part[0]], from_p.at[part[0]], at(dy=3))
    second_pass(0)
    sib_own = send(gt.at[1], sib.at[0], at(dc=1))
    half_up.wait_recv()
    half_down.wait_recv()
    comb[0, part[0]] = plus(gt[2, part[0]], sib[1, part[0]], half_in[0]).astype(BF16)
    up_a = send(comb.at[0, part[0]], from_m.at[part[0]], at(dy=1))
    comb[1, part[1]] = plus(gt[3, part[1]], sib[2, part[1]], half_in[1]).astype(BF16)
    down_b = send(comb.at[1, part[1]], from_p.at[part[1]], at(dy=3))

    step = 256

    def passage_part(j, carry):
        js = pl.ds(pl.multiple_of(j * step, step), step)
        low = nn(wt[0, js], agb[:, 0:128])
        high = nn(wt[1, js], agb[:, 0:128])
        pg_ref[js, 0:128] = jnp.where(iota((step, 128), 1) < 64, low, high).astype(BF16)
        for m in range(2, 5):
            pg_ref[js, CUTS[m - 1]:CUTS[m]] = nn(wt[m, js], agb[:, CUTS[m - 1]:CUTS[m]]).astype(BF16)
        return carry

    lax.fori_loop(0, n_pass // step, passage_part, 0)
    store_p = pltpu.make_async_copy(pg_ref, pg_hbm, lsem.at[1])
    store_p.start()

    for copy in (sib_own, up_a, up_b, down_a, down_b):
        copy.wait_recv()
    mine_t = plus(gt[0], sib[0], from_m[...], from_p[...]).astype(BF16)

    zbs[...] = nt(eye, mine_t).astype(BF16)
    z_back = [send(zbs.at[pl.ds(d * 16, 16)], zb.at[pl.ds(d * 16, 16)], at(dz=NZ - d)) for d in range(1, NZ)]
    zb[pl.ds(0, 16)] = zbs[pl.ds(0, 16)]
    for copy in z_back:
        copy.wait_recv()
    xbs[...] = nn(to_x, zb[...]).astype(BF16)
    x_back = [send(xbs.at[pl.ds(d * 32, 32)], xb.at[pl.ds(d * 32, 32)], at(dx=NX - d)) for d in range(1, NX)]
    xb[pl.ds(0, 32)] = xbs[pl.ds(0, 32)]
    for copy in x_back:
        copy.wait_recv()
    fg[pl.ds(0, lines)] = nn(bsel_ref[...], xb[...]).astype(BF16)
    near = gather_start(fg, lines)
    far = gather_near(fg, lines, near)
    last = gather_far(fg, lines, far)
    for copy in (near[0], far[2], far[3], last):
        copy.wait_recv()
    qg_ref[...] = nn(fsel_ref[...], fg[...]).astype(BF16)

    store_p.wait()
    for copy in started:
        copy.wait_send()


def body(queries, passages, query_cluster, passage_cluster, positive):
    nq, width = queries.shape
    n_pass = passages.shape[0]
    vmem = pl.BlockSpec(memory_space=pltpu.VMEM)
    hbm = pl.BlockSpec(memory_space=pl.ANY)
    V = pltpu.VMEM
    return pl.pallas_call(
        kernel,
        out_shape=(jax.ShapeDtypeStruct((nq, width), BF16), jax.ShapeDtypeStruct((n_pass, width), BF16)),
        in_specs=[vmem, vmem, vmem, vmem, hbm],
        out_specs=(vmem, hbm),
        scratch_shapes=[
            V((n_pass, width), BF16), V((n_pass, 128), BF16), V((n_pass, 128), BF16), V((width, n_pass), BF16),
            V((BLOCK, ROW), BF16), V((BLOCK, ROW), BF16), V((BLOCK, ROW), BF16), V((SLOTS, ROW), BF16),
            V((PAIR, 128), BF16),
            V((5, n_pass, SLOTS), F32), V((5, n_pass, SLOTS), BF16), V((8, SLOTS), F32),
            V((8, 8, BLOCK), F32), V((8, 8, BLOCK), F32), V((8, 8, BLOCK), F32),
            V((8, width, BLOCK), BF16), V((4, width, BLOCK), BF16), V((3, width, BLOCK), BF16),
            V((2, HALF, BLOCK), BF16), V((width, BLOCK), BF16), V((width, BLOCK), BF16),
            V((BLOCK, width), BF16), V((BLOCK, width), BF16), V((BLOCK, width), BF16), V((BLOCK, width), BF16),
            V((nq, width), BF16), V((nq // 8, BLOCK), BF16), V((nq, nq), BF16), V((n_pass, width), BF16),
            pltpu.SemaphoreType.DMA((72,)), pltpu.SemaphoreType.DMA((72,)), pltpu.SemaphoreType.DMA((2,)),
        ],
        compiler_params=pltpu.CompilerParams(
            collective_id=0, has_side_effects=True, vmem_limit_bytes=58 * 1024 * 1024),
    )(query_cluster.reshape(1, nq), positive.reshape(1, nq), passage_cluster.reshape(1, n_pass), queries, passages)


def solution(mesh):
    in_specs = (P("dp", None), P(("dp", "tile"), None), P("dp"), P(("dp", "tile")), P("dp"))
    out_specs = (P("dp", None), P(("dp", "tile"), None))
    return jax.shard_map(body, mesh=mesh, in_specs=in_specs, out_specs=out_specs, check_vma=False)
```

```python
import functools
import math

import jax
import jax.numpy as jnp
from jax import lax
from jax.experimental import pallas as pl
from jax.experimental.pallas import tpu as pltpu
from jax.sharding import PartitionSpec as P

F32 = jnp.float32
BF16 = jnp.bfloat16
I32 = jnp.int32

NX, NZ, NY, NC = 4, 8, 4, 2
CL_OWN = 4
CAP = 32
NEGATIVE = -1e30
CUTS = (64, 128, 256, 512, 768)
WIDTH = 768
META = 128
ROW = WIDTH + META
SCALES = tuple(2.0 / math.sqrt(k) for k in CUTS)
LOG2E = math.log2(math.e)
BLOCK = 64
PAIR = 4 * BLOCK
HALF = 8 * BLOCK
SLOTS = 2 * HALF
FAR = NX * NZ
CHUNK = 16
STACK = ROW // 128 * BLOCK

PLACE = ((0, 0), (0, 1), (1, 0), (3, 0), (1, 1), (3, 1), (2, 0), (2, 1))
MIRROR = tuple(PLACE.index(((NY - dy) % NY, dc)) for dy, dc in PLACE)
MESH = pl.DeviceIdType.MESH


def nn(a, b):
    return lax.dot_general(a, b, (((1,), (0,)), ((), ())), preferred_element_type=F32)


def nt(a, b):
    return lax.dot_general(a, b, (((1,), (1,)), ((), ())), preferred_element_type=F32)


def iota(shape, dim):
    return lax.broadcasted_iota(I32, shape, dim)


def onehot(mask):
    return jnp.where(mask, 1.0, 0.0).astype(BF16)


def fold(value, op):
    return op(value.reshape(value.shape[0] // 8, 8, value.shape[1]), axis=0)


def plus(*values):
    return functools.reduce(jnp.add, [v.astype(F32) for v in values])


def shift(a, n):
    return lax.shift_right_logical(a, n)


def kernel(qc_ref, pos_ref, pc_ref, q_ref, p_hbm, qg_ref, pg_hbm,
           p_ref, p0_ref, p1_ref, pt_ref, stack, out_buf, in_buf, back_out, back_in, pack_ref, unpack_ref,
           agb, q0_ref, prob, wt, msc, stat, stat_in, lse_ref, gt, grad, sib, comb, from_y,
           rows_ref, fg, bsel_ref, fsel_ref, pg_ref,
           ssem, rsem, fsem, gsem, lsem):
    n_pass = p_ref.shape[0]
    dp = lax.axis_index("dp")
    tile = lax.axis_index("tile")
    x, z = lax.div(dp, NZ), lax.rem(dp, NZ)
    y, core = lax.div(tile, NC), lax.rem(tile, NC)

    def at(dy=0, dc=0):
        return (dp, lax.rem(y + dy, NY) * NC + lax.rem(core + dc, NC))

    def ahead(i):
        return (lax.rem(x + lax.div(i, NZ), NX) * NZ + lax.rem(z + lax.rem(i, NZ), NZ), tile)

    def behind(i):
        return (lax.rem(x + NX - lax.div(i, NZ), NX) * NZ + lax.rem(z + NZ - lax.rem(i, NZ), NZ), tile)

    started = []

    def send(src, dst, where):
        i = len(started)
        copy = pltpu.make_async_remote_copy(
            src_ref=src, dst_ref=dst, send_sem=ssem.at[i], recv_sem=rsem.at[i],
            device_id=where, device_id_type=MESH)
        copy.start()
        started.append(copy)
        return copy

    def chunk(i, src, dst, lane, where):
        rows = pl.ds(pl.multiple_of(i * CHUNK, CHUNK), CHUNK)
        return pltpu.make_async_remote_copy(
            src_ref=src.at[rows], dst_ref=dst.at[rows], send_sem=fsem.at[lane, i], recv_sem=gsem.at[lane, i],
            device_id=where(i), device_id_type=MESH)

    exchanges = []

    def exchange(src, dst, where):
        args = (src, dst, len(exchanges), where)
        exchanges.append(args)

        def go(i, carry):
            chunk(i, *args).start()
            return carry

        lax.fori_loop(1, FAR, go, 0)
        dst[pl.ds(0, CHUNK)] = src[pl.ds(0, CHUNK)]

        def arrived():
            def wait(i, carry):
                chunk(i, *args).wait_recv()
                return carry

            lax.fori_loop(1, FAR, wait, 0)

        return arrived

    load_p = pltpu.make_async_copy(p_hbm, p_ref, lsem.at[0])
    load_p.start()

    barrier = pltpu.get_barrier_semaphore()

    def greet(i, carry):
        pl.semaphore_signal(barrier, inc=1, device_id=ahead(i), device_id_type=MESH)
        return carry

    lax.fori_loop(1, FAR, greet, 0)
    for dy, dc in PLACE[1:]:
        pl.semaphore_signal(barrier, inc=1, device_id=at(dy, dc), device_id_type=MESH)

    nq = q_ref.shape[0]
    cluster = qc_ref[...]
    owner = shift(cluster, 2)
    local = lax.bitwise_and(cluster, 3)
    own = jnp.where(iota((FAR, nq), 0) == owner, 1.0, 0.0)
    before = onehot(iota((nq, nq), 0) < iota((nq, nq), 1))
    rank = jnp.sum(own * nn(own.astype(BF16), before), axis=0, keepdims=True)
    first = jnp.sum(jnp.where(owner < iota((FAR, nq), 0), 1.0, 0.0), axis=1, keepdims=True)
    order = (rank + jnp.sum(own * first, axis=0, keepdims=True)).astype(I32)
    rank = rank.astype(I32)
    carrier = lax.bitwise_and(order, 7)
    line = shift(order, 3)
    dxs = lax.bitwise_and(shift(owner, 3) - x, NX - 1)
    dzs = lax.bitwise_and(lax.bitwise_and(owner, NZ - 1) - z, NZ - 1)
    code = shift(rank, 4) * BLOCK + (dxs * NZ + dzs) * 2 + lax.bitwise_and(shift(rank, 3), 1)
    mine = carrier == tile
    pick = onehot(iota((2 * BLOCK, nq), 0) == jnp.where(mine, code, -1))
    row = iota((META, nq), 0)
    target = lax.bitwise_and(pos_ref[...], 8 * n_pass - 1)
    digits = jnp.where(row == 69, shift(target, 6), jnp.where(row == 70, lax.bitwise_and(target, 63), 0))
    digits = jnp.where((row == local + 64) | (row == 68), 1, digits)
    meta = nt(pick, digits.astype(F32).astype(BF16))
    meta = jnp.where(iota((2 * BLOCK, META), 1) == 68, 1.0 - meta, meta).astype(BF16)
    sent = nn(pick, q_ref[...]).astype(BF16)
    r, c = iota((HALF, STACK), 0), iota((HALF, STACK), 1)
    pack_ref[...] = onehot((shift(lax.bitwise_and(r, CHUNK - 1), 1) == shift(c, 6))
                           & (lax.bitwise_and(c, BLOCK - 1) == shift(r, 4) * 2 + lax.bitwise_and(r, 1)))
    c, r = iota((STACK, HALF), 0), iota((STACK, HALF), 1)
    unpack_ref[...] = onehot((shift(lax.bitwise_and(r, CHUNK - 1), 1) == shift(c, 6))
                             & (lax.bitwise_and(c, BLOCK - 1) == shift(r, 4) * 2 + lax.bitwise_and(r, 1)))
    for h in range(2):
        for b in range(WIDTH // 128):
            stack[pl.ds(b * BLOCK, BLOCK)] = sent[h * BLOCK:(h + 1) * BLOCK, b * 128:(b + 1) * 128]
        stack[pl.ds(STACK - BLOCK, BLOCK)] = meta[h * BLOCK:(h + 1) * BLOCK]
        out_buf[h] = nn(pack_ref[...], stack[...]).astype(BF16)

    pl.semaphore_wait(barrier, FAR - 1 + 7)

    arrived = [exchange(out_buf.at[h], in_buf.at[h], ahead) for h in range(2)]

    clusters = pc_ref[...]
    lane_row = iota((META, n_pass), 0)
    off = jnp.where((lane_row == clusters - CL_OWN * dp + 64) | (lane_row > 68) | (lane_row < 64), 0.0, NEGATIVE)
    load_p.wait()
    lane = iota((n_pass, 128), 1)
    head = p_ref[:, :128].astype(F32)
    p0_ref[...] = jnp.where(lane < 64, head, off.T).astype(BF16)
    p1_ref[...] = jnp.where(lane < 64, 0.0, head).astype(BF16)
    eye = onehot(iota((PAIR, PAIR), 0) == iota((PAIR, PAIR), 1))
    for b in range(WIDTH // PAIR):
        pt_ref[pl.ds(b * PAIR, PAIR)] = nt(eye, p_ref[:, b * PAIR:(b + 1) * PAIR]).astype(BF16)
    lines = nq // 8
    pick_line = onehot(iota((lines, nq), 0) == jnp.where(mine, line, -1))
    bsel_ref[...] = nt(pick_line, pick).astype(BF16)
    cdy = lax.bitwise_and(shift(carrier, 1) - y, NY - 1)
    cdc = lax.bitwise_and(carrier - core, 1)
    place = jnp.where(cdy == 0, cdc, jnp.where(cdy == 2, 6 + cdc, jnp.where(cdy == 1, 2, 3) + 2 * cdc))
    spread = onehot(iota((nq, nq), 0) == place * lines + line)
    fsel_ref[...] = nt(onehot(iota((nq, nq), 0) == iota((nq, nq), 1)), spread).astype(BF16)
    stat[...] = jnp.zeros_like(stat)
    lse_ref[...] = jnp.zeros_like(lse_ref)

    def gather_start(buf, base, rows):
        blk = lambda s: buf.at[pl.ds(base + s * rows, rows)]
        return {1: send(blk(0), blk(1), at(dc=1)), 3: send(blk(0), blk(3), at(dy=1)),
                2: send(blk(0), blk(2), at(dy=3)), 6: send(blk(0), blk(6), at(dy=2))}

    def gather_pass(buf, base, rows, got, s):
        blk = lambda s: buf.at[pl.ds(base + s * rows, rows)]
        got[s].wait_recv()
        on = {2: 4, 3: 5, 6: 7}[s]
        got[on] = send(blk(s), blk(on), at(dc=1))

    got = []
    for h in range(2):
        arrived[h]()
        rows = nn(unpack_ref[...], in_buf[h]).astype(BF16)
        for b in range(ROW // 128):
            agb[pl.ds(h * HALF, BLOCK), b * 128:(b + 1) * 128] = rows[b * BLOCK:(b + 1) * BLOCK]
        got.append(gather_start(agb, h * HALF, BLOCK))

    stat_copies = {}

    def first_pass(u):
        h, q = u // 2, u % 2
        rows = pl.ds(u * PAIR, PAIR)
        cols = pl.ds(u * PAIR, PAIR)
        q0_ref[...] = jnp.where(iota((PAIR, 128), 1) < 64, agb[rows, 0:128].astype(F32),
                                agb[rows, WIDTH:ROW].astype(F32)).astype(BF16)
        value, tops = None, []
        for m in range(5):
            left = (p0_ref[...], p1_ref[...])[m] if m < 2 else p_ref[:, CUTS[m - 1]:CUTS[m]]
            right = (q0_ref[...], agb[rows, 0:128])[m] if m < 2 else agb[rows, CUTS[m - 1]:CUTS[m]]
            part = nt(left, right)
            value = part if value is None else value + part
            prob[m, :, cols] = value
            tops.append(jnp.max(fold(value, jnp.max), axis=0, keepdims=True))
        small = 128

        def exps(j, sums):
            js = pl.ds(pl.multiple_of(j * small, small), small)
            out = []
            for m in range(5):
                e = jnp.exp2((prob[m, js, cols] - tops[m]) * (SCALES[m] * LOG2E))
                prob[m, js, cols] = e
                out.append(sums[m] + fold(e, jnp.sum))
            return tuple(out)

        sums = lax.fori_loop(0, n_pass // small, exps, (jnp.zeros((8, PAIR), F32),) * 5)
        for m in range(5):
            top = tops[m] * SCALES[m]
            total = jnp.sum(sums[m], axis=0, keepdims=True)
            msc[m:m + 1, cols] = top
            lse = top + jnp.log(total)
            for s in range(4):
                stat[h, 4 * q + s, m:m + 1] = lse[:, s // 2 * 128:s // 2 * 128 + 128]
        for s in range(4 * q, 4 * q + 4):
            if s:
                stat_copies[h, s] = send(stat.at[h, s], stat_in.at[h, MIRROR[s]], at(*PLACE[s]))

    lse_from = {}

    def totals(h):
        parts = [stat[h, 0]]
        for s in range(1, 8):
            stat_copies[h, s].wait_recv()
        for s in range(1, 8):
            value = stat_in[h, MIRROR[s]]
            parts.append(pltpu.roll(value, BLOCK, 1) if s % 2 else value)
        top = functools.reduce(jnp.maximum, parts)
        lse = top + jnp.log(functools.reduce(jnp.add, [jnp.exp(v - top) for v in parts]))
        lse_ref[h, 0] = jnp.where(iota((8, 128), 1) < BLOCK, lse, pltpu.roll(lse, BLOCK, 1))
        for s in range(7, 0, -1):
            lse_from[h, MIRROR[s]] = send(lse_ref.at[h, 0], lse_ref.at[h, MIRROR[s]], at(*PLACE[s]))

    base = tile * n_pass
    pick_digit = jnp.where(iota((8, META), 1) == 69, 64.0,
                           jnp.where(iota((8, META), 1) == 70, 1.0, 0.0)).astype(BF16)

    def second_pass(u, between=None):
        h, q = u // 2, u % 2
        rows = pl.ds(u * PAIR, PAIR)
        cols = pl.ds(u * PAIR, PAIR)
        for s in range(4 * q, 4 * q + 4):
            if s:
                lse_from[h, s].wait_recv()
        goal = nt(pick_digit, agb[rows, WIDTH:ROW])[0:1].astype(I32) - base
        lower = iota((8, 128), 1) < BLOCK
        lse = jnp.concatenate([jnp.where(lower, lse_ref[h, 4 * q + s], lse_ref[h, 4 * q + s + 1]) for s in (0, 2)],
                              axis=1)
        factor = [jnp.exp(msc[m:m + 1, cols] - lse[m:m + 1]) * SCALES[m] for m in range(5)]
        small = 64

        def weigh(j, carry):
            start = pl.multiple_of(j * small, small)
            js = pl.ds(start, small)
            hit = iota((small, PAIR), 0) == goal - start
            running = None
            for m in range(4, -1, -1):
                term = prob[m, js, cols] * factor[m]
                running = term if running is None else running + term
                wt[m, js, cols] = jnp.where(hit, running - sum(SCALES[m:]), running).astype(BF16)
            return carry

        lax.fori_loop(0, n_pass // small, weigh, 0)
        if between is not None:
            between()
        for m in range(5):
            lo = CUTS[m - 1] if m else 0
            gt[lo:CUTS[m]] = nn(pt_ref[lo:CUTS[m]], wt[m, :, cols]).astype(BF16)
        grad[rows] = nt(eye, gt[...]).astype(BF16)

    sums_in = {}

    def block(h, s):
        return grad.at[pl.ds(h * HALF + s * BLOCK, BLOCK)]

    def to_core(h, s):
        i = {1: 0, 4: 1, 5: 2, 7: 3}[s]
        sums_in[h, i] = send(block(h, s), sib.at[h, i], at(dc=1))

    def to_chip(h, s):
        i = {2: 1, 3: 2, 6: 3}[s]
        sums_in[h, i].wait_recv()
        comb[h, i] = plus(block(h, s)[...], sib[h, i]).astype(BF16)
        sums_in[h, s, s] = send(comb.at[h, i], from_y.at[h, i], at(dy=PLACE[s][0]))

    def go_back(h):
        sums_in[h, 0].wait_recv()
        for s in (2, 3, 6):
            sums_in[h, s, s].wait_recv()
        total = plus(block(h, 0)[...], sib[h, 0], from_y[h, 1], from_y[h, 2], from_y[h, 3]).astype(BF16)
        for b in range(WIDTH // 128):
            stack[pl.ds(b * BLOCK, BLOCK)] = total[:, b * 128:(b + 1) * 128]
        used = WIDTH // 128 * BLOCK
        back_out[h] = nn(pack_ref[:, :used], stack[pl.ds(0, used)]).astype(BF16)
        return exchange(back_out.at[h], back_in.at[h], behind)

    wide = n_pass // 2

    def passage_part(j):
        js = slice(j * wide, (j + 1) * wide)
        low = nn(wt[0, js], agb[:, 0:128])
        high = nn(wt[1, js], agb[:, 0:128])
        pg_ref[js, 0:128] = jnp.where(iota((wide, 128), 1) < 64, low, high).astype(BF16)
        for m in range(2, 5):
            pg_ref[js, CUTS[m - 1]:CUTS[m]] = nn(wt[m, js], agb[:, CUTS[m - 1]:CUTS[m]]).astype(BF16)
        store = pltpu.make_async_copy(pg_ref.at[js], pg_hbm.at[js], lsem.at[1 + j])
        store.start()
        return store

    def gather_near(h):
        gather_pass(agb, h * HALF, BLOCK, got[h], 2)
        gather_pass(agb, h * HALF, BLOCK, got[h], 3)
        got[h][1].wait_recv()

    def gather_rest(h):
        gather_pass(agb, h * HALF, BLOCK, got[h], 6)
        for s in (4, 5, 7):
            got[h][s].wait_recv()

    gather_near(0)
    first_pass(0)
    gather_rest(0)
    first_pass(1)
    gather_near(1)
    first_pass(2)
    totals(0)
    gather_rest(1)
    first_pass(3)

    second_pass(1)
    for s in (7, 4, 5):
        to_core(0, s)
    totals(1)
    second_pass(0, lambda: to_chip(0, 6))
    to_core(0, 1)
    to_chip(0, 2)
    to_chip(0, 3)
    second_pass(3)
    for s in (7, 4, 5):
        to_core(1, s)
    second_pass(2, lambda: to_chip(1, 6))
    to_core(1, 1)
    to_chip(1, 2)
    to_chip(1, 3)
    home = [go_back(0)]
    stores = [passage_part(0)]
    home.append(go_back(1))
    stores.append(passage_part(1))

    for h in range(2):
        home[h]()
        used = WIDTH // 128 * BLOCK
        rows = nn(unpack_ref[:used], back_in[h]).astype(BF16)
        for b in range(WIDTH // 128):
            rows_ref[pl.ds(h * BLOCK, BLOCK), b * 128:(b + 1) * 128] = rows[b * BLOCK:(b + 1) * BLOCK]
    fg[pl.ds(0, lines)] = nn(bsel_ref[...], rows_ref[...]).astype(BF16)
    last = gather_start(fg, 0, lines)
    for s in (2, 3, 6):
        gather_pass(fg, 0, lines, last, s)
    for s in (1, 4, 5, 7):
        last[s].wait_recv()
    qg_ref[...] = nn(fsel_ref[...], fg[...]).astype(BF16)

    for store in stores:
        store.wait()
    for copy in started:
        copy.wait_send()
    for args in exchanges:
        def sent_all(i, carry, args=args):
            chunk(i, *args).wait_send()
            return carry

        lax.fori_loop(1, FAR, sent_all, 0)


def body(queries, passages, query_cluster, passage_cluster, positive):
    nq, width = queries.shape
    n_pass = passages.shape[0]
    vmem = pl.BlockSpec(memory_space=pltpu.VMEM)
    hbm = pl.BlockSpec(memory_space=pl.ANY)
    V = pltpu.VMEM
    return pl.pallas_call(
        kernel,
        out_shape=(jax.ShapeDtypeStruct((nq, width), BF16), jax.ShapeDtypeStruct((n_pass, width), BF16)),
        in_specs=[vmem, vmem, vmem, vmem, hbm],
        out_specs=(vmem, hbm),
        scratch_shapes=[
            V((n_pass, width), BF16), V((n_pass, 128), BF16), V((n_pass, 128), BF16), V((width, n_pass), BF16),
            V((STACK, 128), BF16), *[V((2, HALF, 128), BF16)] * 4, V((HALF, STACK), BF16), V((STACK, HALF), BF16),
            V((SLOTS, ROW), BF16), V((PAIR, 128), BF16),
            V((5, n_pass, SLOTS), F32), V((5, n_pass, SLOTS), BF16), V((8, SLOTS), F32),
            V((2, 8, 8, 128), F32), V((2, 8, 8, 128), F32), V((2, 8, 8, 128), F32),
            V((width, PAIR), BF16), V((SLOTS, width), BF16),
            V((2, 4, BLOCK, width), BF16), V((2, 4, BLOCK, width), BF16), V((2, 4, BLOCK, width), BF16),
            V((2 * BLOCK, width), BF16), V((nq, width), BF16), V((nq // 8, 2 * BLOCK), BF16), V((nq, nq), BF16),
            V((n_pass, width), BF16),
            pltpu.SemaphoreType.DMA((72,)), pltpu.SemaphoreType.DMA((72,)),
            pltpu.SemaphoreType.DMA((4, FAR)), pltpu.SemaphoreType.DMA((4, FAR)), pltpu.SemaphoreType.DMA((3,)),
        ],
        compiler_params=pltpu.CompilerParams(
            collective_id=0, has_side_effects=True, vmem_limit_bytes=58 * 1024 * 1024),
    )(query_cluster.reshape(1, nq), positive.reshape(1, nq), passage_cluster.reshape(1, n_pass), queries, passages)


def solution(mesh):
    in_specs = (P("dp", None), P(("dp", "tile"), None), P("dp"), P(("dp", "tile")), P("dp"))
    out_specs = (P("dp", None), P(("dp", "tile"), None))
    return jax.shard_map(body, mesh=mesh, in_specs=in_specs, out_specs=out_specs, check_vma=False)
```

```python
import functools
import math

import jax
import jax.numpy as jnp
from jax import lax
from jax.experimental import pallas as pl
from jax.experimental.pallas import tpu as pltpu
from jax.sharding import PartitionSpec as P

F32 = jnp.float32
BF16 = jnp.bfloat16
I32 = jnp.int32

NX, NZ, NY, NC = 4, 8, 4, 2
CL_OWN = 4
CAP = 32
NEGATIVE = -1e30
CUTS = (64, 128, 256, 512, 768)
WIDTH = 768
META = 128
ROW = WIDTH + META
SCALES = tuple(2.0 / math.sqrt(k) for k in CUTS)
LOG2E = math.log2(math.e)
BLOCK = 64
PAIR = 4 * BLOCK
HALF = 8 * BLOCK
SLOTS = 2 * HALF
FAR = NX * NZ
CHUNK = 16
STACK = ROW // 128 * BLOCK

PLACE = ((0, 0), (0, 1), (1, 0), (3, 0), (1, 1), (3, 1), (2, 0), (2, 1))
MIRROR = tuple(PLACE.index(((NY - dy) % NY, dc)) for dy, dc in PLACE)
MESH = pl.DeviceIdType.MESH
PARTS = 4


def nn(a, b):
    return lax.dot_general(a, b, (((1,), (0,)), ((), ())), preferred_element_type=F32)


def nt(a, b):
    return lax.dot_general(a, b, (((1,), (1,)), ((), ())), preferred_element_type=F32)


def iota(shape, dim):
    return lax.broadcasted_iota(I32, shape, dim)


def onehot(mask):
    return jnp.where(mask, 1.0, 0.0).astype(BF16)


def fold(value, op):
    return op(value.reshape(value.shape[0] // 8, 8, value.shape[1]), axis=0)


def plus(*values):
    return functools.reduce(jnp.add, [v.astype(F32) for v in values])


def shift(a, n):
    return lax.shift_right_logical(a, n)


def kernel(qc_ref, pos_ref, pc_ref, q_hbm, p_hbm, fg_hbm, fsel_hbm, pg_hbm,
           q_ref, p_ref, p0_ref, p1_ref, pt_ref, stack, out_buf, in_buf, back_out, back_in, pack_ref, unpack_ref,
           agb, q0_ref, prob, wt, msc, stat, stat_in, lse_ref, gt, grad, sib, comb, from_y,
           rows_ref, fg, bsel_ref, fsel_ref, pg_ref,
           ssem, rsem, lsem):
    n_pass = p_ref.shape[0]
    dp = lax.axis_index("dp")
    tile = lax.axis_index("tile")
    x, z = lax.div(dp, NZ), lax.rem(dp, NZ)
    y, core = lax.div(tile, NC), lax.rem(tile, NC)

    def at(dy=0, dc=0):
        return (dp, lax.rem(y + dy, NY) * NC + lax.rem(core + dc, NC))

    def ahead(i):
        return (lax.rem(x + lax.div(i, NZ), NX) * NZ + lax.rem(z + lax.rem(i, NZ), NZ), tile)

    def behind(i):
        return (lax.rem(x + NX - lax.div(i, NZ), NX) * NZ + lax.rem(z + NZ - lax.rem(i, NZ), NZ), tile)

    groups, received = [], []

    def group(all_sent):
        groups.append(all_sent)
        return len(groups) - 1

    def arrival():
        received.append(None)
        return len(received) - 1

    def remote(src, dst, g, i, where):
        return pltpu.make_async_remote_copy(
            src_ref=src, dst_ref=dst, send_sem=ssem.at[g], recv_sem=rsem.at[i], device_id=where, device_id_type=MESH)

    def send(src, dst, where, g, i=None):
        copy = remote(src, dst, g, arrival() if i is None else i, where)
        copy.start()
        return copy

    def exchange(src, dst, where):
        rest = pl.ds(CHUNK, (FAR - 1) * CHUNK)
        g, n = group(src.at[rest]), arrival()

        def go(i, carry):
            rows = pl.ds(pl.multiple_of(i * CHUNK, CHUNK), CHUNK)
            remote(src.at[rows], dst.at[rows], g, n, where(i)).start()
            return carry

        lax.fori_loop(1, FAR, go, 0)
        dst[pl.ds(0, CHUNK)] = src[pl.ds(0, CHUNK)]
        return remote(src.at[rest], dst.at[rest], g, n, where(1)).wait_recv

    barrier = pltpu.get_barrier_semaphore()
    for dx, dz in sorted(((i // NZ, i % NZ) for i in range(1, FAR)), key=lambda d: abs(d[1] - NZ // 2)):
        there = lax.rem(x + dx, NX) * NZ + lax.rem(z + dz, NZ)
        pl.semaphore_signal(barrier, inc=1, device_id=(there, tile), device_id_type=MESH)
    for dy, dc in PLACE[1:]:
        pl.semaphore_signal(barrier, inc=1, device_id=at(dy, dc), device_id_type=MESH)
    load_q = pltpu.make_async_copy(q_hbm, q_ref, lsem.at[3])
    load_q.start()
    load_p = pltpu.make_async_copy(p_hbm, p_ref, lsem.at[0])
    load_p.start()

    nq = q_ref.shape[0]
    cluster = qc_ref[...]
    owner = shift(cluster, 2)
    local = lax.bitwise_and(cluster, 3)
    own = jnp.where(iota((FAR, nq), 0) == owner, 1.0, 0.0)
    before = onehot(iota((nq, nq), 0) < iota((nq, nq), 1))
    rank = jnp.sum(own * nn(own.astype(BF16), before), axis=0, keepdims=True)
    first = jnp.sum(jnp.where(owner < iota((FAR, nq), 0), 1.0, 0.0), axis=1, keepdims=True)
    order = (rank + jnp.sum(own * first, axis=0, keepdims=True)).astype(I32)
    rank = rank.astype(I32)
    carrier = lax.bitwise_and(order, 7)
    line = shift(order, 3)
    dxs = lax.bitwise_and(shift(owner, 3) - x, NX - 1)
    dzs = lax.bitwise_and(lax.bitwise_and(owner, NZ - 1) - z, NZ - 1)
    code = shift(rank, 4) * BLOCK + (dxs * NZ + dzs) * 2 + lax.bitwise_and(shift(rank, 3), 1)
    mine = carrier == tile
    pick = onehot(iota((2 * BLOCK, nq), 0) == jnp.where(mine, code, -1))
    row = iota((META, nq), 0)
    target = lax.bitwise_and(pos_ref[...], 8 * n_pass - 1)
    digits = jnp.where(row == 69, shift(target, 6), jnp.where(row == 70, lax.bitwise_and(target, 63), 0))
    digits = jnp.where((row == local + 64) | (row == 68), 1, digits)
    meta = nt(pick, digits.astype(F32).astype(BF16))
    meta = jnp.where(iota((2 * BLOCK, META), 1) == 68, 1.0 - meta, meta).astype(BF16)
    load_q.wait()
    sent = nn(pick, q_ref[...]).astype(BF16)
    r, c = iota((HALF, STACK), 0), iota((HALF, STACK), 1)
    pack_ref[...] = onehot((shift(lax.bitwise_and(r, CHUNK - 1), 1) == shift(c, 6))
                           & (lax.bitwise_and(c, BLOCK - 1) == shift(r, 4) * 2 + lax.bitwise_and(r, 1)))
    c, r = iota((STACK, HALF), 0), iota((STACK, HALF), 1)
    unpack_ref[...] = onehot((shift(lax.bitwise_and(r, CHUNK - 1), 1) == shift(c, 6))
                             & (lax.bitwise_and(c, BLOCK - 1) == shift(r, 4) * 2 + lax.bitwise_and(r, 1)))
    for h in range(2):
        for b in range(WIDTH // 128):
            stack[pl.ds(b * BLOCK, BLOCK)] = sent[h * BLOCK:(h + 1) * BLOCK, b * 128:(b + 1) * 128]
        stack[pl.ds(STACK - BLOCK, BLOCK)] = meta[h * BLOCK:(h + 1) * BLOCK]
        out_buf[h] = nn(pack_ref[...], stack[...]).astype(BF16)

    pl.semaphore_wait(barrier, FAR - 1 + 7)

    arrived = [exchange(out_buf.at[h], in_buf.at[h], ahead) for h in range(2)]

    clusters = pc_ref[...]
    lane_row = iota((META, n_pass), 0)
    off = jnp.where((lane_row == clusters - CL_OWN * dp + 64) | (lane_row > 68) | (lane_row < 64), 0.0, NEGATIVE)
    load_p.wait()
    lane = iota((n_pass, 128), 1)
    head = p_ref[:, :128].astype(F32)
    p0_ref[...] = jnp.where(lane < 64, head, off.T).astype(BF16)
    p1_ref[...] = jnp.where(lane < 64, 0.0, head).astype(BF16)
    eye = onehot(iota((PAIR, PAIR), 0) == iota((PAIR, PAIR), 1))
    for b in range(WIDTH // PAIR):
        pt_ref[pl.ds(b * PAIR, PAIR)] = nt(eye, p_ref[:, b * PAIR:(b + 1) * PAIR]).astype(BF16)
    lines = nq // 8
    pick_line = onehot(iota((lines, nq), 0) == jnp.where(mine, line, -1))
    bsel_ref[...] = nt(pick_line, pick).astype(BF16)
    cdy = lax.bitwise_and(shift(carrier, 1) - y, NY - 1)
    cdc = lax.bitwise_and(carrier - core, 1)
    place = jnp.where(cdy == 0, cdc, jnp.where(cdy == 2, 6 + cdc, jnp.where(cdy == 1, 2, 3) + 2 * cdc))
    spread = onehot(iota((nq, nq), 0) == place * lines + line)
    fsel_ref[...] = nt(onehot(iota((nq, nq), 0) == iota((nq, nq), 1)), spread).astype(BF16)
    stores = [pltpu.make_async_copy(fsel_ref, fsel_hbm, lsem.at[4])]
    stores[0].start()
    stat[...] = jnp.zeros_like(stat)
    lse_ref[...] = jnp.zeros_like(lse_ref)

    def gather_start(buf, base, rows):
        blk = lambda s: buf.at[pl.ds(base + s * rows, rows)]
        g = group(buf.at[pl.ds(base, 7 * rows)])
        return {0: g, 1: send(blk(0), blk(1), at(dc=1), g), 3: send(blk(0), blk(3), at(dy=1), g),
                2: send(blk(0), blk(2), at(dy=3), g), 6: send(blk(0), blk(6), at(dy=2), g)}

    def gather_pass(buf, base, rows, got, s):
        blk = lambda s: buf.at[pl.ds(base + s * rows, rows)]
        got[s].wait_recv()
        on = {2: 4, 3: 5, 6: 7}[s]
        got[on] = send(blk(s), blk(on), at(dc=1), got[0])

    got = []
    for h in range(2):
        arrived[h]()
        rows = nn(unpack_ref[...], in_buf[h]).astype(BF16)
        for b in range(ROW // 128):
            agb[pl.ds(h * HALF, BLOCK), b * 128:(b + 1) * 128] = rows[b * BLOCK:(b + 1) * BLOCK]
        got.append(gather_start(agb, h * HALF, BLOCK))

    others = pl.ds(1, 7)
    stat_group = [group(stat.at[h, others]) for h in range(2)]
    stat_come = [arrival() for h in range(2)]
    lse_group = [group(lse_ref.at[h, others]) for h in range(2)]
    lse_come = [arrival() for h in range(2)]

    def first_pass(u):
        h, q = u // 2, u % 2
        rows = pl.ds(u * PAIR, PAIR)
        cols = pl.ds(u * PAIR, PAIR)
        q0_ref[...] = jnp.where(iota((PAIR, 128), 1) < 64, agb[rows, 0:128].astype(F32),
                                agb[rows, WIDTH:ROW].astype(F32)).astype(BF16)
        value, tops = None, []
        for m in range(5):
            left = (p0_ref[...], p1_ref[...])[m] if m < 2 else p_ref[:, CUTS[m - 1]:CUTS[m]]
            right = (q0_ref[...], agb[rows, 0:128])[m] if m < 2 else agb[rows, CUTS[m - 1]:CUTS[m]]
            part = nt(left, right)
            value = part if value is None else value + part
            prob[m, :, cols] = value
            tops.append(jnp.max(fold(value, jnp.max), axis=0, keepdims=True))
        small = 128

        def exps(j, sums):
            js = pl.ds(pl.multiple_of(j * small, small), small)
            out = []
            for m in range(5):
                e = jnp.exp2((prob[m, js, cols] - tops[m]) * (SCALES[m] * LOG2E))
                prob[m, js, cols] = e
                out.append(sums[m] + fold(e, jnp.sum))
            return tuple(out)

        sums = lax.fori_loop(0, n_pass // small, exps, (jnp.zeros((8, PAIR), F32),) * 5)
        for m in range(5):
            top = tops[m] * SCALES[m]
            total = jnp.sum(sums[m], axis=0, keepdims=True)
            msc[m:m + 1, cols] = top
            lse = top + jnp.log(total)
            for s in range(4):
                stat[h, 4 * q + s, m:m + 1] = lse[:, s // 2 * 128:s // 2 * 128 + 128]
        for s in range(4 * q, 4 * q + 4):
            if s:
                send(stat.at[h, s], stat_in.at[h, MIRROR[s]], at(*PLACE[s]), stat_group[h], stat_come[h])

    def totals(h):
        parts = [stat[h, 0]]
        remote(stat.at[h, others], stat_in.at[h, others], stat_group[h], stat_come[h], at(dc=1)).wait_recv()
        for s in range(1, 8):
            value = stat_in[h, MIRROR[s]]
            parts.append(pltpu.roll(value, BLOCK, 1) if s % 2 else value)
        top = functools.reduce(jnp.maximum, parts)
        lse = top + jnp.log(functools.reduce(jnp.add, [jnp.exp(v - top) for v in parts]))
        lse_ref[h, 0] = jnp.where(iota((8, 128), 1) < BLOCK, lse, pltpu.roll(lse, BLOCK, 1))
        for s in range(7, 0, -1):
            send(lse_ref.at[h, 0], lse_ref.at[h, MIRROR[s]], at(*PLACE[s]), lse_group[h], lse_come[h])

    base = tile * n_pass
    pick_digit = jnp.where(iota((8, META), 1) == 69, 64.0,
                           jnp.where(iota((8, META), 1) == 70, 1.0, 0.0)).astype(BF16)

    def second_pass(u, between=None):
        h, q = u // 2, u % 2
        rows = pl.ds(u * PAIR, PAIR)
        cols = pl.ds(u * PAIR, PAIR)
        if q == 1:
            remote(lse_ref.at[h, others], lse_ref.at[h, others], lse_group[h], lse_come[h], at(dc=1)).wait_recv()
        goal = nt(pick_digit, agb[rows, WIDTH:ROW])[0:1].astype(I32) - base
        lower = iota((8, 128), 1) < BLOCK
        lse = jnp.concatenate([jnp.where(lower, lse_ref[h, 4 * q + s], lse_ref[h, 4 * q + s + 1]) for s in (0, 2)],
                              axis=1)
        factor = [jnp.exp(msc[m:m + 1, cols] - lse[m:m + 1]) * SCALES[m] for m in range(5)]
        small = 64

        def weigh(j, carry):
            start = pl.multiple_of(j * small, small)
            js = pl.ds(start, small)
            hit = iota((small, PAIR), 0) == goal - start
            running = None
            for m in range(4, -1, -1):
                term = prob[m, js, cols] * factor[m]
                running = term if running is None else running + term
                wt[m, js, cols] = jnp.where(hit, running - sum(SCALES[m:]), running).astype(BF16)
            return carry

        lax.fori_loop(0, n_pass // small, weigh, 0)
        if between is not None:
            between()
        for m in range(5):
            lo = CUTS[m - 1] if m else 0
            gt[lo:CUTS[m]] = nn(pt_ref[lo:CUTS[m]], wt[m, :, cols]).astype(BF16)
        grad[rows] = nt(eye, gt[...]).astype(BF16)

    sums_in = {}
    sum_group = [group(grad.at[pl.ds(h * HALF, 7 * BLOCK)]) for h in range(2)]

    def block(h, s):
        return grad.at[pl.ds(h * HALF + s * BLOCK, BLOCK)]

    def to_core(h, s):
        i = {1: 0, 4: 1, 5: 2, 7: 3}[s]
        sums_in[h, i] = send(block(h, s), sib.at[h, i], at(dc=1), sum_group[h])

    def to_chip(h, s):
        i = {2: 1, 3: 2, 6: 3}[s]
        sums_in[h, i].wait_recv()
        comb[h, i] = plus(block(h, s)[...], sib[h, i]).astype(BF16)
        sums_in[h, s, s] = send(comb.at[h, i], from_y.at[h, i], at(dy=PLACE[s][0]), sum_group[h])

    def go_back(h):
        sums_in[h, 0].wait_recv()
        for s in (2, 3, 6):
            sums_in[h, s, s].wait_recv()
        total = plus(block(h, 0)[...], sib[h, 0], from_y[h, 1], from_y[h, 2], from_y[h, 3]).astype(BF16)
        for b in range(WIDTH // 128):
            stack[pl.ds(b * BLOCK, BLOCK)] = total[:, b * 128:(b + 1) * 128]
        used = WIDTH // 128 * BLOCK
        back_out[h] = nn(pack_ref[:, :used], stack[pl.ds(0, used)]).astype(BF16)
        return exchange(back_out.at[h], back_in.at[h], behind)

    wide = n_pass // 2

    def passage_part(j):
        js = slice(j * wide, (j + 1) * wide)
        low = nn(wt[0, js], agb[:, 0:128])
        high = nn(wt[1, js], agb[:, 0:128])
        pg_ref[js, 0:128] = jnp.where(iota((wide, 128), 1) < 64, low, high).astype(BF16)
        for m in range(2, 5):
            pg_ref[js, CUTS[m - 1]:CUTS[m]] = nn(wt[m, js], agb[:, CUTS[m - 1]:CUTS[m]]).astype(BF16)
        store = pltpu.make_async_copy(pg_ref.at[js], pg_hbm.at[js], lsem.at[1 + j])
        store.start()
        return store

    def gather_near(h):
        gather_pass(agb, h * HALF, BLOCK, got[h], 2)
        gather_pass(agb, h * HALF, BLOCK, got[h], 3)
        got[h][1].wait_recv()

    def gather_rest(h):
        gather_pass(agb, h * HALF, BLOCK, got[h], 6)
        for s in (4, 5, 7):
            got[h][s].wait_recv()

    gather_near(0)
    first_pass(0)
    gather_rest(0)
    first_pass(1)
    gather_near(1)
    first_pass(2)
    totals(0)
    gather_rest(1)
    first_pass(3)

    second_pass(1)
    for s in (7, 4, 5):
        to_core(0, s)
    totals(1)
    second_pass(0, lambda: to_chip(0, 6))
    to_core(0, 1)
    to_chip(0, 2)
    to_chip(0, 3)
    second_pass(3)
    for s in (7, 4, 5):
        to_core(1, s)
    second_pass(2, lambda: to_chip(1, 6))
    to_core(1, 1)
    to_chip(1, 2)
    to_chip(1, 3)
    home = [go_back(0)]
    stores.append(passage_part(0))
    home.append(go_back(1))
    stores.append(passage_part(1))

    for h in range(2):
        home[h]()
        used = WIDTH // 128 * BLOCK
        rows = nn(unpack_ref[:used], back_in[h]).astype(BF16)
        for b in range(WIDTH // 128):
            rows_ref[pl.ds(h * BLOCK, BLOCK), b * 128:(b + 1) * 128] = rows[b * BLOCK:(b + 1) * BLOCK]
    fg[pl.ds(0, lines)] = nn(bsel_ref[...], rows_ref[...]).astype(BF16)
    last = gather_start(fg, 0, lines)
    for s in (2, 3, 6):
        gather_pass(fg, 0, lines, last, s)
    for s in (1, 4, 5, 7):
        last[s].wait_recv()
    assert len(groups) == ssem.shape[0] and len(received) == rsem.shape[0]
    write = pltpu.make_async_copy(fg, fg_hbm, lsem.at[3])
    write.start()
    write.wait()
    for store in stores:
        store.wait()
    for g, all_sent in enumerate(groups):
        remote(all_sent, all_sent, g, 0, at(dc=1)).wait_send()


def finish(fsel_hbm, fg_hbm, pg_hbm, qg_hbm, out_hbm, fsel_ref, fg_ref, qg_ref, pg_ref, sems):
    loads = [pltpu.make_async_copy(fsel_hbm, fsel_ref, sems.at[0]), pltpu.make_async_copy(fg_hbm, fg_ref, sems.at[1])]
    for load in loads:
        load.start()
    rows = pg_hbm.shape[0] // PARTS
    parts = [pl.ds(i * rows, rows) for i in range(PARTS)]
    reads = [pltpu.make_async_copy(pg_hbm.at[r], pg_ref.at[r], sems.at[2 + i]) for i, r in enumerate(parts)]
    writes = [pltpu.make_async_copy(pg_ref.at[r], out_hbm.at[r], sems.at[2 + PARTS + i]) for i, r in enumerate(parts)]
    for read in reads:
        read.start()
    for load in loads:
        load.wait()
    for read, write in zip(reads, writes):
        read.wait()
        write.start()
    some = qg_ref.shape[0] // 2
    for i in range(2):
        r = pl.ds(i * some, some)
        qg_ref[r] = nn(fsel_ref[r], fg_ref[...]).astype(BF16)
        write = pltpu.make_async_copy(qg_ref.at[r], qg_hbm.at[r], sems.at[2 + 2 * PARTS + i])
        write.start()
        writes.append(write)
    for write in writes:
        write.wait()


def body(queries, passages, query_cluster, passage_cluster, positive):
    nq, width = queries.shape
    n_pass = passages.shape[0]
    vmem = pl.BlockSpec(memory_space=pltpu.VMEM)
    hbm = pl.BlockSpec(memory_space=pl.ANY)
    V = pltpu.VMEM
    fg, fsel, pg = pl.pallas_call(
        kernel,
        out_shape=(jax.ShapeDtypeStruct((nq, width), BF16), jax.ShapeDtypeStruct((nq, nq), BF16),
                   jax.ShapeDtypeStruct((n_pass, width), BF16)),
        in_specs=[vmem, vmem, vmem, hbm, hbm],
        out_specs=(hbm, hbm, hbm),
        scratch_shapes=[
            V((nq, width), BF16),
            V((n_pass, width), BF16), V((n_pass, 128), BF16), V((n_pass, 128), BF16), V((width, n_pass), BF16),
            V((STACK, 128), BF16), *[V((2, HALF, 128), BF16)] * 4, V((HALF, STACK), BF16), V((STACK, HALF), BF16),
            V((SLOTS, ROW), BF16), V((PAIR, 128), BF16),
            V((5, n_pass, SLOTS), F32), V((5, n_pass, SLOTS), BF16), V((8, SLOTS), F32),
            V((2, 8, 8, 128), F32), V((2, 8, 8, 128), F32), V((2, 8, 8, 128), F32),
            V((width, PAIR), BF16), V((SLOTS, width), BF16),
            V((2, 4, BLOCK, width), BF16), V((2, 4, BLOCK, width), BF16), V((2, 4, BLOCK, width), BF16),
            V((2 * BLOCK, width), BF16), V((nq, width), BF16), V((nq // 8, 2 * BLOCK), BF16), V((nq, nq), BF16),
            V((n_pass, width), BF16),
            pltpu.SemaphoreType.DMA((13,)), pltpu.SemaphoreType.DMA((43,)), pltpu.SemaphoreType.DMA((5,)),
        ],
        compiler_params=pltpu.CompilerParams(
            collective_id=0, has_side_effects=True, vmem_limit_bytes=58 * 1024 * 1024),
    )(query_cluster.reshape(1, nq), positive.reshape(1, nq), passage_cluster.reshape(1, n_pass), queries, passages)
    return pl.pallas_call(
        finish,
        out_shape=(jax.ShapeDtypeStruct((nq, width), BF16), jax.ShapeDtypeStruct((n_pass, width), BF16)),
        in_specs=[hbm, hbm, hbm],
        out_specs=(hbm, hbm),
        scratch_shapes=[V((nq, nq), BF16), V((nq, width), BF16), V((nq, width), BF16), V((n_pass, width), BF16),
                        pltpu.SemaphoreType.DMA((4 + 2 * PARTS,))],
        compiler_params=pltpu.CompilerParams(vmem_limit_bytes=58 * 1024 * 1024),
    )(fsel, fg, pg)


def solution(mesh):
    in_specs = (P("dp", None), P(("dp", "tile"), None), P("dp"), P(("dp", "tile")), P("dp"))
    out_specs = (P("dp", None), P(("dp", "tile"), None))
    return jax.shard_map(body, mesh=mesh, in_specs=in_specs, out_specs=out_specs, check_vma=False)
```

```python
import functools
import math

import jax
import jax.numpy as jnp
from jax import lax
from jax.experimental import pallas as pl
from jax.experimental.pallas import tpu as pltpu
from jax.sharding import PartitionSpec as P

F32 = jnp.float32
BF16 = jnp.bfloat16
I32 = jnp.int32

NX, NZ, NY, NC = 4, 8, 4, 2
CL_OWN = 4
CAP = 32
NEGATIVE = -1e30
CUTS = (64, 128, 256, 512, 768)
WIDTH = 768
META = 128
ROW = WIDTH + META
SCALES = tuple(2.0 / math.sqrt(k) for k in CUTS)
LOG2E = math.log2(math.e)
BLOCK = 64
PAIR = 4 * BLOCK
HALF = 8 * BLOCK
SLOTS = 2 * HALF
FAR = NX * NZ
CHUNK = 16
STACK = ROW // 128 * BLOCK

PLACE = ((0, 0), (0, 1), (1, 0), (3, 0), (1, 1), (3, 1), (2, 0), (2, 1))
MIRROR = tuple(PLACE.index(((NY - dy) % NY, dc)) for dy, dc in PLACE)
MESH = pl.DeviceIdType.MESH
PARTS = 4


def nn(a, b):
    return lax.dot_general(a, b, (((1,), (0,)), ((), ())), preferred_element_type=F32)


def nt(a, b):
    return lax.dot_general(a, b, (((1,), (1,)), ((), ())), preferred_element_type=F32)


def iota(shape, dim):
    return lax.broadcasted_iota(I32, shape, dim)


def onehot(mask):
    return jnp.where(mask, 1.0, 0.0).astype(BF16)


def fold(value, op):
    return op(value.reshape(value.shape[0] // 8, 8, value.shape[1]), axis=0)


def plus(*values):
    return functools.reduce(jnp.add, [v.astype(F32) for v in values])


def shift(a, n):
    return lax.shift_right_logical(a, n)


def kernel(qc_ref, pos_ref, pc_ref, q_hbm, p_hbm, fg_hbm, fsel_hbm, pg_hbm,
           q_ref, p_ref, p0_ref, p1_ref, pt_ref, stack, out_buf, in_buf, back_out, back_in, pack_ref, unpack_ref,
           agb, notes, spread_ref, q0_ref, prob, wt, msc, stat, stat_in, lse_ref, gt, grad, sib, comb, from_y,
           rows_ref, fg, bsel_ref, fsel_ref, pg_ref,
           ssem, rsem, lsem):
    n_pass = p_ref.shape[0]
    dp = lax.axis_index("dp")
    tile = lax.axis_index("tile")
    x, z = lax.div(dp, NZ), lax.rem(dp, NZ)
    y, core = lax.div(tile, NC), lax.rem(tile, NC)

    def at(dy=0, dc=0):
        return (dp, lax.rem(y + dy, NY) * NC + lax.rem(core + dc, NC))

    def ahead(i):
        return (lax.rem(x + lax.div(i, NZ), NX) * NZ + lax.rem(z + lax.rem(i, NZ), NZ), tile)

    def behind(i):
        return (lax.rem(x + NX - lax.div(i, NZ), NX) * NZ + lax.rem(z + NZ - lax.rem(i, NZ), NZ), tile)

    groups, received = [], []

    def group(all_sent):
        groups.append(all_sent)
        return len(groups) - 1

    def arrival():
        received.append(None)
        return len(received) - 1

    def remote(src, dst, g, i, where):
        return pltpu.make_async_remote_copy(
            src_ref=src, dst_ref=dst, send_sem=ssem.at[g], recv_sem=rsem.at[i], device_id=where, device_id_type=MESH)

    def send(src, dst, where, g, i=None):
        copy = remote(src, dst, g, arrival() if i is None else i, where)
        copy.start()
        return copy

    def exchange(src, dst, where):
        rest = pl.ds(CHUNK, (FAR - 1) * CHUNK)
        g, n = group(src.at[rest]), arrival()

        def go(i, carry):
            rows = pl.ds(pl.multiple_of(i * CHUNK, CHUNK), CHUNK)
            remote(src.at[rows], dst.at[rows], g, n, where(i)).start()
            return carry

        lax.fori_loop(1, FAR, go, 0)
        dst[pl.ds(0, CHUNK)] = src[pl.ds(0, CHUNK)]
        return remote(src.at[rest], dst.at[rest], g, n, where(1)).wait_recv

    barrier = pltpu.get_barrier_semaphore()
    for dx, dz in sorted(((i // NZ, i % NZ) for i in range(1, FAR)), key=lambda d: abs(d[1] - NZ // 2)):
        there = lax.rem(x + dx, NX) * NZ + lax.rem(z + dz, NZ)
        pl.semaphore_signal(barrier, inc=1, device_id=(there, tile), device_id_type=MESH)
    for dy, dc in PLACE[1:]:
        pl.semaphore_signal(barrier, inc=1, device_id=at(dy, dc), device_id_type=MESH)
    load_q = pltpu.make_async_copy(q_hbm, q_ref, lsem.at[3])
    load_q.start()
    load_p = pltpu.make_async_copy(p_hbm, p_ref, lsem.at[0])
    load_p.start()

    nq = q_ref.shape[0]
    cluster = qc_ref[...]
    owner = shift(cluster, 2)
    local = lax.bitwise_and(cluster, 3)
    own = jnp.where(iota((FAR, nq), 0) == owner, 1.0, 0.0)
    before = onehot(iota((nq, nq), 0) < iota((nq, nq), 1))
    rank = jnp.sum(own * nn(own.astype(BF16), before), axis=0, keepdims=True)
    first = jnp.sum(jnp.where(owner < iota((FAR, nq), 0), 1.0, 0.0), axis=1, keepdims=True)
    order = (rank + jnp.sum(own * first, axis=0, keepdims=True)).astype(I32)
    rank = rank.astype(I32)
    carrier = lax.bitwise_and(order, 7)
    line = shift(order, 3)
    dxs = lax.bitwise_and(shift(owner, 3) - x, NX - 1)
    dzs = lax.bitwise_and(lax.bitwise_and(owner, NZ - 1) - z, NZ - 1)
    code = shift(rank, 4) * BLOCK + (dxs * NZ + dzs) * 2 + lax.bitwise_and(shift(rank, 3), 1)
    mine = carrier == tile
    pick = onehot(iota((2 * BLOCK, nq), 0) == jnp.where(mine, code, -1))
    row = iota((META, nq), 0)
    target = lax.bitwise_and(pos_ref[...], 8 * n_pass - 1)
    digits = jnp.where(row == 69, shift(target, 6), jnp.where(row == 70, lax.bitwise_and(target, 63), 0))
    digits = jnp.where((row == local + 64) | (row == 68), 1, digits)
    meta = nt(pick, digits.astype(F32).astype(BF16))
    meta = jnp.where(iota((2 * BLOCK, META), 1) == 68, 1.0 - meta, meta).astype(BF16)
    load_q.wait()
    sent = nn(pick, q_ref[...]).astype(BF16)
    r, c = iota((HALF, STACK), 0), iota((HALF, STACK), 1)
    pack_ref[...] = onehot((shift(lax.bitwise_and(r, CHUNK - 1), 1) == shift(c, 6))
                           & (lax.bitwise_and(c, BLOCK - 1) == shift(r, 4) * 2 + lax.bitwise_and(r, 1)))
    c, r = iota((STACK, HALF), 0), iota((STACK, HALF), 1)
    unpack_ref[...] = onehot((shift(lax.bitwise_and(r, CHUNK - 1), 1) == shift(c, 6))
                             & (lax.bitwise_and(c, BLOCK - 1) == shift(r, 4) * 2 + lax.bitwise_and(r, 1)))
    for h in range(2):
        for b in range(WIDTH // 128):
            stack[pl.ds(b * BLOCK, BLOCK)] = sent[h * BLOCK:(h + 1) * BLOCK, b * 128:(b + 1) * 128]
        stack[pl.ds(STACK - BLOCK, BLOCK)] = meta[h * BLOCK:(h + 1) * BLOCK]
        out_buf[h] = nn(pack_ref[...], stack[...]).astype(BF16)

    pl.semaphore_wait(barrier, FAR - 1 + 7)

    arrived = [exchange(out_buf.at[h], in_buf.at[h], ahead) for h in range(2)]

    clusters = pc_ref[...]
    lane_row = iota((META, n_pass), 0)
    off = jnp.where((lane_row == clusters - CL_OWN * dp + 64) | (lane_row > 68) | (lane_row < 64), 0.0, NEGATIVE)
    load_p.wait()
    lane = iota((n_pass, 128), 1)
    head = p_ref[:, :128].astype(F32)
    p0_ref[...] = jnp.where(lane < 64, head, off.T).astype(BF16)
    p1_ref[...] = jnp.where(lane < 64, 0.0, head).astype(BF16)
    eye = onehot(iota((PAIR, PAIR), 0) == iota((PAIR, PAIR), 1))
    for b in range(WIDTH // PAIR):
        pt_ref[pl.ds(b * PAIR, PAIR)] = nt(eye, p_ref[:, b * PAIR:(b + 1) * PAIR]).astype(BF16)
    lines = nq // 8
    pick_line = onehot(iota((lines, nq), 0) == jnp.where(mine, line, -1))
    bsel_ref[...] = nt(pick_line, pick).astype(BF16)
    cdy = lax.bitwise_and(shift(carrier, 1) - y, NY - 1)
    cdc = lax.bitwise_and(carrier - core, 1)
    place = jnp.where(cdy == 0, cdc, jnp.where(cdy == 2, 6 + cdc, jnp.where(cdy == 1, 2, 3) + 2 * cdc))
    spread = onehot(iota((nq, nq), 0) == place * lines + line)
    fsel_ref[...] = nt(onehot(iota((nq, nq), 0) == iota((nq, nq), 1)), spread).astype(BF16)
    stores = [pltpu.make_async_copy(fsel_ref, fsel_hbm, lsem.at[4])]
    stores[0].start()
    stat[...] = jnp.zeros_like(stat)
    spread_ref[...] = jnp.zeros_like(spread_ref)
    lse_ref[...] = jnp.zeros_like(lse_ref)

    def gather_start(buf, base, rows):
        blk = lambda s: buf.at[pl.ds(base + s * rows, rows)]
        g = group(buf.at[pl.ds(base, 7 * rows)])
        return {0: g, 1: send(blk(0), blk(1), at(dc=1), g), 3: send(blk(0), blk(3), at(dy=1), g),
                2: send(blk(0), blk(2), at(dy=3), g), 6: send(blk(0), blk(6), at(dy=2), g)}

    def gather_pass(buf, base, rows, got, s):
        blk = lambda s: buf.at[pl.ds(base + s * rows, rows)]
        got[s].wait_recv()
        on = {2: 4, 3: 5, 6: 7}[s]
        got[on] = send(blk(s), blk(on), at(dc=1), got[0])

    others = pl.ds(1, 7)
    note_row = onehot(iota((16, META), 1) == iota((16, META), 0) + 64)
    note_group = [group(notes.at[h, others]) for h in range(2)]
    note_come = [arrival() for h in range(2)]
    got = []
    for h in range(2):
        arrived[h]()
        rows = nn(unpack_ref[...], in_buf[h]).astype(BF16)
        note = rows[STACK - BLOCK:]
        notes[h, 0] = nt(note_row, jnp.concatenate([note, note], axis=0)).astype(BF16)
        for s in range(7, 0, -1):
            send(notes.at[h, 0], notes.at[h, MIRROR[s]], at(*PLACE[s]), note_group[h], note_come[h])
        for b in range(WIDTH // 128):
            agb[pl.ds(h * HALF, BLOCK), b * 128:(b + 1) * 128] = rows[b * BLOCK:(b + 1) * BLOCK]
        got.append(gather_start(agb, h * HALF, BLOCK))

    stat_group = [group(stat.at[h, others]) for h in range(2)]
    stat_come = [arrival() for h in range(2)]
    lse_group = [group(lse_ref.at[h, others]) for h in range(2)]
    lse_come = [arrival() for h in range(2)]

    def unit_notes(u):
        lower = iota((16, 128), 1) < BLOCK
        note = [notes[u // 2, u % 2 * 4 + s].astype(F32) for s in range(4)]
        return jnp.concatenate([jnp.where(lower, note[0], note[1]), jnp.where(lower, note[2], note[3])], axis=1)

    def first_pass(u):
        h, q = u // 2, u % 2
        rows = pl.ds(u * PAIR, PAIR)
        cols = pl.ds(u * PAIR, PAIR)
        spread_ref[64:80] = unit_notes(u).astype(BF16)
        q0_ref[...] = jnp.where(iota((PAIR, 128), 1) < 64, agb[rows, 0:128].astype(F32),
                                nt(eye, spread_ref[...])).astype(BF16)
        value, tops = None, []
        for m in range(5):
            left = (p0_ref[...], p1_ref[...])[m] if m < 2 else p_ref[:, CUTS[m - 1]:CUTS[m]]
            right = (q0_ref[...], agb[rows, 0:128])[m] if m < 2 else agb[rows, CUTS[m - 1]:CUTS[m]]
            part = nt(left, right)
            value = part if value is None else value + part
            prob[m, :, cols] = value
            tops.append(jnp.max(fold(value, jnp.max), axis=0, keepdims=True))
        small = 128

        def exps(j, sums):
            js = pl.ds(pl.multiple_of(j * small, small), small)
            out = []
            for m in range(5):
                e = jnp.exp2((prob[m, js, cols] - tops[m]) * (SCALES[m] * LOG2E))
                prob[m, js, cols] = e
                out.append(sums[m] + fold(e, jnp.sum))
            return tuple(out)

        sums = lax.fori_loop(0, n_pass // small, exps, (jnp.zeros((8, PAIR), F32),) * 5)
        for m in range(5):
            top = tops[m] * SCALES[m]
            total = jnp.sum(sums[m], axis=0, keepdims=True)
            msc[m:m + 1, cols] = top
            lse = top + jnp.log(total)
            for s in range(4):
                stat[h, 4 * q + s, m:m + 1] = lse[:, s // 2 * 128:s // 2 * 128 + 128]
        for s in range(4 * q, 4 * q + 4):
            if s:
                send(stat.at[h, s], stat_in.at[h, MIRROR[s]], at(*PLACE[s]), stat_group[h], stat_come[h])

    def totals(h):
        parts = [stat[h, 0]]
        remote(stat.at[h, others], stat_in.at[h, others], stat_group[h], stat_come[h], at(dc=1)).wait_recv()
        for s in range(1, 8):
            value = stat_in[h, MIRROR[s]]
            parts.append(pltpu.roll(value, BLOCK, 1) if s % 2 else value)
        top = functools.reduce(jnp.maximum, parts)
        lse = top + jnp.log(functools.reduce(jnp.add, [jnp.exp(v - top) for v in parts]))
        lse_ref[h, 0] = jnp.where(iota((8, 128), 1) < BLOCK, lse, pltpu.roll(lse, BLOCK, 1))
        for s in range(7, 0, -1):
            send(lse_ref.at[h, 0], lse_ref.at[h, MIRROR[s]], at(*PLACE[s]), lse_group[h], lse_come[h])

    base = tile * n_pass

    def second_pass(u, between=None):
        h, q = u // 2, u % 2
        rows = pl.ds(u * PAIR, PAIR)
        cols = pl.ds(u * PAIR, PAIR)
        if q == 1:
            remote(lse_ref.at[h, others], lse_ref.at[h, others], lse_group[h], lse_come[h], at(dc=1)).wait_recv()
        note = unit_notes(u)
        goal = (note[5:6] * 64.0 + note[6:7]).astype(I32) - base
        lower = iota((8, 128), 1) < BLOCK
        lse = jnp.concatenate([jnp.where(lower, lse_ref[h, 4 * q + s], lse_ref[h, 4 * q + s + 1]) for s in (0, 2)],
                              axis=1)
        factor = [jnp.exp(msc[m:m + 1, cols] - lse[m:m + 1]) * SCALES[m] for m in range(5)]
        small = 64

        def weigh(j, carry):
            start = pl.multiple_of(j * small, small)
            js = pl.ds(start, small)
            hit = iota((small, PAIR), 0) == goal - start
            running = None
            for m in range(4, -1, -1):
                term = prob[m, js, cols] * factor[m]
                running = term if running is None else running + term
                wt[m, js, cols] = jnp.where(hit, running - sum(SCALES[m:]), running).astype(BF16)
            return carry

        lax.fori_loop(0, n_pass // small, weigh, 0)
        if between is not None:
            between()
        for m in range(5):
            lo = CUTS[m - 1] if m else 0
            gt[lo:CUTS[m]] = nn(pt_ref[lo:CUTS[m]], wt[m, :, cols]).astype(BF16)
        grad[rows] = nt(eye, gt[...]).astype(BF16)

    sums_in = {}
    sum_group = [group(grad.at[pl.ds(h * HALF, 7 * BLOCK)]) for h in range(2)]

    def block(h, s):
        return grad.at[pl.ds(h * HALF + s * BLOCK, BLOCK)]

    def to_core(h, s):
        i = {1: 0, 4: 1, 5: 2, 7: 3}[s]
        sums_in[h, i] = send(block(h, s), sib.at[h, i], at(dc=1), sum_group[h])

    def to_chip(h, s):
        i = {2: 1, 3: 2, 6: 3}[s]
        sums_in[h, i].wait_recv()
        comb[h, i] = plus(block(h, s)[...], sib[h, i]).astype(BF16)
        sums_in[h, s, s] = send(comb.at[h, i], from_y.at[h, i], at(dy=PLACE[s][0]), sum_group[h])

    def go_back(h):
        sums_in[h, 0].wait_recv()
        for s in (2, 3, 6):
            sums_in[h, s, s].wait_recv()
        total = plus(block(h, 0)[...], sib[h, 0], from_y[h, 1], from_y[h, 2], from_y[h, 3]).astype(BF16)
        for b in range(WIDTH // 128):
            stack[pl.ds(b * BLOCK, BLOCK)] = total[:, b * 128:(b + 1) * 128]
        used = WIDTH // 128 * BLOCK
        back_out[h] = nn(pack_ref[:, :used], stack[pl.ds(0, used)]).astype(BF16)
        return exchange(back_out.at[h], back_in.at[h], behind)

    wide = n_pass // 2

    def passage_part(j):
        js = slice(j * wide, (j + 1) * wide)
        low = nn(wt[0, js], agb[:, 0:128])
        high = nn(wt[1, js], agb[:, 0:128])
        pg_ref[js, 0:128] = jnp.where(iota((wide, 128), 1) < 64, low, high).astype(BF16)
        for m in range(2, 5):
            pg_ref[js, CUTS[m - 1]:CUTS[m]] = nn(wt[m, js], agb[:, CUTS[m - 1]:CUTS[m]]).astype(BF16)
        store = pltpu.make_async_copy(pg_ref.at[js], pg_hbm.at[js], lsem.at[1 + j])
        store.start()
        return store

    def gather_near(h):
        remote(notes.at[h, others], notes.at[h, others], note_group[h], note_come[h], at(dc=1)).wait_recv()
        gather_pass(agb, h * HALF, BLOCK, got[h], 2)
        gather_pass(agb, h * HALF, BLOCK, got[h], 3)
        got[h][1].wait_recv()

    def gather_rest(h):
        gather_pass(agb, h * HALF, BLOCK, got[h], 6)
        for s in (4, 5, 7):
            got[h][s].wait_recv()

    gather_near(0)
    first_pass(0)
    gather_rest(0)
    first_pass(1)
    gather_near(1)
    first_pass(2)
    totals(0)
    gather_rest(1)
    first_pass(3)

    second_pass(1)
    for s in (7, 4, 5):
        to_core(0, s)
    totals(1)
    second_pass(0, lambda: to_chip(0, 6))
    to_core(0, 1)
    to_chip(0, 2)
    to_chip(0, 3)
    second_pass(3)
    for s in (7, 4, 5):
        to_core(1, s)
    second_pass(2, lambda: to_chip(1, 6))
    to_core(1, 1)
    to_chip(1, 2)
    to_chip(1, 3)
    home = [go_back(0)]
    stores.append(passage_part(0))
    home.append(go_back(1))
    stores.append(passage_part(1))

    for h in range(2):
        home[h]()
        used = WIDTH // 128 * BLOCK
        rows = nn(unpack_ref[:used], back_in[h]).astype(BF16)
        for b in range(WIDTH // 128):
            rows_ref[pl.ds(h * BLOCK, BLOCK), b * 128:(b + 1) * 128] = rows[b * BLOCK:(b + 1) * BLOCK]
    fg[pl.ds(0, lines)] = nn(bsel_ref[...], rows_ref[...]).astype(BF16)
    last = gather_start(fg, 0, lines)
    for s in (2, 3, 6):
        gather_pass(fg, 0, lines, last, s)
    for s in (1, 4, 5, 7):
        last[s].wait_recv()
    assert len(groups) == ssem.shape[0] and len(received) == rsem.shape[0]
    write = pltpu.make_async_copy(fg, fg_hbm, lsem.at[3])
    write.start()
    write.wait()
    for store in stores:
        store.wait()
    for g, all_sent in enumerate(groups):
        remote(all_sent, all_sent, g, 0, at(dc=1)).wait_send()


def finish(fsel_hbm, fg_hbm, pg_hbm, qg_hbm, out_hbm, fsel_ref, fg_ref, qg_ref, pg_ref, sems):
    loads = [pltpu.make_async_copy(fsel_hbm, fsel_ref, sems.at[0]), pltpu.make_async_copy(fg_hbm, fg_ref, sems.at[1])]
    for load in loads:
        load.start()
    rows = pg_hbm.shape[0] // PARTS
    parts = [pl.ds(i * rows, rows) for i in range(PARTS)]
    reads = [pltpu.make_async_copy(pg_hbm.at[r], pg_ref.at[r], sems.at[2 + i]) for i, r in enumerate(parts)]
    writes = [pltpu.make_async_copy(pg_ref.at[r], out_hbm.at[r], sems.at[2 + PARTS + i]) for i, r in enumerate(parts)]
    for read in reads:
        read.start()
    for load in loads:
        load.wait()
    for read, write in zip(reads, writes):
        read.wait()
        write.start()
    some = qg_ref.shape[0] // 2
    for i in range(2):
        r = pl.ds(i * some, some)
        qg_ref[r] = nn(fsel_ref[r], fg_ref[...]).astype(BF16)
        write = pltpu.make_async_copy(qg_ref.at[r], qg_hbm.at[r], sems.at[2 + 2 * PARTS + i])
        write.start()
        writes.append(write)
    for write in writes:
        write.wait()


def body(queries, passages, query_cluster, passage_cluster, positive):
    nq, width = queries.shape
    n_pass = passages.shape[0]
    vmem = pl.BlockSpec(memory_space=pltpu.VMEM)
    hbm = pl.BlockSpec(memory_space=pl.ANY)
    V = pltpu.VMEM
    fg, fsel, pg = pl.pallas_call(
        kernel,
        out_shape=(jax.ShapeDtypeStruct((nq, width), BF16), jax.ShapeDtypeStruct((nq, nq), BF16),
                   jax.ShapeDtypeStruct((n_pass, width), BF16)),
        in_specs=[vmem, vmem, vmem, hbm, hbm],
        out_specs=(hbm, hbm, hbm),
        scratch_shapes=[
            V((nq, width), BF16),
            V((n_pass, width), BF16), V((n_pass, 128), BF16), V((n_pass, 128), BF16), V((width, n_pass), BF16),
            V((STACK, 128), BF16), *[V((2, HALF, 128), BF16)] * 4, V((HALF, STACK), BF16), V((STACK, HALF), BF16),
            V((SLOTS, width), BF16), V((2, 8, 16, 128), BF16), V((META, PAIR), BF16), V((PAIR, 128), BF16),
            V((5, n_pass, SLOTS), F32), V((5, n_pass, SLOTS), BF16), V((8, SLOTS), F32),
            V((2, 8, 8, 128), F32), V((2, 8, 8, 128), F32), V((2, 8, 8, 128), F32),
            V((width, PAIR), BF16), V((SLOTS, width), BF16),
            V((2, 4, BLOCK, width), BF16), V((2, 4, BLOCK, width), BF16), V((2, 4, BLOCK, width), BF16),
            V((2 * BLOCK, width), BF16), V((nq, width), BF16), V((nq // 8, 2 * BLOCK), BF16), V((nq, nq), BF16),
            V((n_pass, width), BF16),
            pltpu.SemaphoreType.DMA((15,)), pltpu.SemaphoreType.DMA((45,)), pltpu.SemaphoreType.DMA((5,)),
        ],
        compiler_params=pltpu.CompilerParams(
            collective_id=0, has_side_effects=True, vmem_limit_bytes=58 * 1024 * 1024),
    )(query_cluster.reshape(1, nq), positive.reshape(1, nq), passage_cluster.reshape(1, n_pass), queries, passages)
    return pl.pallas_call(
        finish,
        out_shape=(jax.ShapeDtypeStruct((nq, width), BF16), jax.ShapeDtypeStruct((n_pass, width), BF16)),
        in_specs=[hbm, hbm, hbm],
        out_specs=(hbm, hbm),
        scratch_shapes=[V((nq, nq), BF16), V((nq, width), BF16), V((nq, width), BF16), V((n_pass, width), BF16),
                        pltpu.SemaphoreType.DMA((4 + 2 * PARTS,))],
        compiler_params=pltpu.CompilerParams(vmem_limit_bytes=58 * 1024 * 1024),
    )(fsel, fg, pg)


def solution(mesh):
    in_specs = (P("dp", None), P(("dp", "tile"), None), P("dp"), P(("dp", "tile")), P("dp"))
    out_specs = (P("dp", None), P(("dp", "tile"), None))
    return jax.shard_map(body, mesh=mesh, in_specs=in_specs, out_specs=out_specs, check_vma=False)
```

```python
import functools
import math

import jax
import jax.numpy as jnp
from jax import lax
from jax.experimental import pallas as pl
from jax.experimental.pallas import tpu as pltpu
from jax.sharding import PartitionSpec as P

F32 = jnp.float32
BF16 = jnp.bfloat16
I32 = jnp.int32

NX, NZ, NY, NC = 4, 8, 4, 2
CL_OWN = 4
CAP = 32
NEGATIVE = -1e30
CUTS = (64, 128, 256, 512, 768)
WIDTH = 768
META = 128
ROW = WIDTH + META
SCALES = tuple(2.0 / math.sqrt(k) for k in CUTS)
LOG2E = math.log2(math.e)
BLOCK = 64
PAIR = 4 * BLOCK
HALF = 8 * BLOCK
SLOTS = 2 * HALF
FAR = NX * NZ
CHUNK = 16
STACK = ROW // 128 * BLOCK

PLACE = ((0, 0), (0, 1), (1, 0), (3, 0), (1, 1), (3, 1), (2, 0), (2, 1))
CHIPS = (0, 1, 3, 2)
MESH = pl.DeviceIdType.MESH
PARTS = 4


def nn(a, b):
    return lax.dot_general(a, b, (((1,), (0,)), ((), ())), preferred_element_type=F32)


def nt(a, b):
    return lax.dot_general(a, b, (((1,), (1,)), ((), ())), preferred_element_type=F32)


def iota(shape, dim):
    return lax.broadcasted_iota(I32, shape, dim)


def onehot(mask):
    return jnp.where(mask, 1.0, 0.0).astype(BF16)


def fold(value, op):
    return op(value.reshape(value.shape[0] // 8, 8, value.shape[1]), axis=0)


def plus(*values):
    return functools.reduce(jnp.add, [v.astype(F32) for v in values])


def shift(a, n):
    return lax.shift_right_logical(a, n)


def kernel(qc_ref, pos_ref, pc_ref, q_hbm, p_hbm, fg_hbm, fsel_hbm, pg_hbm,
           q_ref, p_ref, p0_ref, p1_ref, pt_ref, stack, out_buf, in_buf, back_out, back_in, pack_ref, unpack_ref,
           agb, q0_ref, prob, wt, msc, stat, core_out, core_in, chip_out, chip_in, lse_ref, gt, grad, sib, comb, from_y,
           rows_ref, fg, bsel_ref, fsel_ref, pg_ref,
           ssem, rsem, lsem):
    n_pass = p_ref.shape[0]
    dp = lax.axis_index("dp")
    tile = lax.axis_index("tile")
    x, z = lax.div(dp, NZ), lax.rem(dp, NZ)
    y, core = lax.div(tile, NC), lax.rem(tile, NC)

    def at(dy=0, dc=0):
        return (dp, lax.rem(y + dy, NY) * NC + lax.rem(core + dc, NC))

    places = sorted(((dx, dz) for dx in range(NX) for dz in range(NZ) if dx or dz), key=lambda d: abs(d[1] - NZ // 2))
    x_at = [lax.rem(x + d, NX) * NZ for d in range(NX)]
    z_at = [lax.rem(z + d, NZ) for d in range(NZ)]

    def ahead(dx, dz):
        return (x_at[dx] + z_at[dz], tile)

    def behind(dx, dz):
        return ahead((NX - dx) % NX, (NZ - dz) % NZ)

    groups, received = [], []

    def group(all_sent):
        groups.append(all_sent)
        return len(groups) - 1

    def arrival():
        received.append(None)
        return len(received) - 1

    def remote(src, dst, g, i, where):
        return pltpu.make_async_remote_copy(
            src_ref=src, dst_ref=dst, send_sem=ssem.at[g], recv_sem=rsem.at[i], device_id=where, device_id_type=MESH)

    def send(src, dst, where, g, i=None):
        copy = remote(src, dst, g, arrival() if i is None else i, where)
        copy.start()
        return copy

    def exchange(src, dst, where):
        rest = pl.ds(CHUNK, (FAR - 1) * CHUNK)
        g, n = group(src.at[rest]), arrival()

        for dx, dz in places:
            rows = pl.ds((dx * NZ + dz) * CHUNK, CHUNK)
            remote(src.at[rows], dst.at[rows], g, n, where(dx, dz)).start()
        dst[pl.ds(0, CHUNK)] = src[pl.ds(0, CHUNK)]
        return remote(src.at[rest], dst.at[rest], g, n, at(dc=1)).wait_recv

    barrier = pltpu.get_barrier_semaphore()
    for dx, dz in places:
        pl.semaphore_signal(barrier, inc=1, device_id=ahead(dx, dz), device_id_type=MESH)
    for dy, dc in PLACE[1:]:
        pl.semaphore_signal(barrier, inc=1, device_id=at(dy, dc), device_id_type=MESH)
    load_q = pltpu.make_async_copy(q_hbm, q_ref, lsem.at[3])
    load_q.start()
    load_p = pltpu.make_async_copy(p_hbm, p_ref, lsem.at[0])
    load_p.start()

    nq = q_ref.shape[0]
    cluster = qc_ref[...]
    owner = shift(cluster, 2)
    local = lax.bitwise_and(cluster, 3)
    own = jnp.where(iota((FAR, nq), 0) == owner, 1.0, 0.0)
    before = onehot(iota((nq, nq), 0) < iota((nq, nq), 1))
    rank = jnp.sum(own * nn(own.astype(BF16), before), axis=0, keepdims=True)
    first = jnp.sum(jnp.where(owner < iota((FAR, nq), 0), 1.0, 0.0), axis=1, keepdims=True)
    order = (rank + jnp.sum(own * first, axis=0, keepdims=True)).astype(I32)
    rank = rank.astype(I32)
    carrier = lax.bitwise_and(order, 7)
    line = shift(order, 3)
    dxs = lax.bitwise_and(shift(owner, 3) - x, NX - 1)
    dzs = lax.bitwise_and(lax.bitwise_and(owner, NZ - 1) - z, NZ - 1)
    code = shift(rank, 4) * BLOCK + (dxs * NZ + dzs) * 2 + lax.bitwise_and(shift(rank, 3), 1)
    mine = carrier == tile
    pick = onehot(iota((2 * BLOCK, nq), 0) == jnp.where(mine, code, -1))
    row = iota((META, nq), 0)
    target = lax.bitwise_and(pos_ref[...], 8 * n_pass - 1)
    digits = jnp.where(row == 69, shift(target, 6), jnp.where(row == 70, lax.bitwise_and(target, 63), 0))
    digits = jnp.where((row == local + 64) | (row == 68), 1, digits)
    meta = nt(pick, digits.astype(F32).astype(BF16))
    meta = jnp.where(iota((2 * BLOCK, META), 1) == 68, 1.0 - meta, meta).astype(BF16)
    load_q.wait()
    sent = nn(pick, q_ref[...]).astype(BF16)
    r, c = iota((HALF, STACK), 0), iota((HALF, STACK), 1)
    pack_ref[...] = onehot((shift(lax.bitwise_and(r, CHUNK - 1), 1) == shift(c, 6))
                           & (lax.bitwise_and(c, BLOCK - 1) == shift(r, 4) * 2 + lax.bitwise_and(r, 1)))
    c, r = iota((STACK, HALF), 0), iota((STACK, HALF), 1)
    unpack_ref[...] = onehot((shift(lax.bitwise_and(r, CHUNK - 1), 1) == shift(c, 6))
                             & (lax.bitwise_and(c, BLOCK - 1) == shift(r, 4) * 2 + lax.bitwise_and(r, 1)))
    for h in range(2):
        for b in range(WIDTH // 128):
            stack[pl.ds(b * BLOCK, BLOCK)] = sent[h * BLOCK:(h + 1) * BLOCK, b * 128:(b + 1) * 128]
        stack[pl.ds(STACK - BLOCK, BLOCK)] = meta[h * BLOCK:(h + 1) * BLOCK]
        out_buf[h] = nn(pack_ref[...], stack[...]).astype(BF16)

    pl.semaphore_wait(barrier, FAR - 1 + 7)

    arrived = [exchange(out_buf.at[h], in_buf.at[h], ahead) for h in range(2)]

    clusters = pc_ref[...]
    lane_row = iota((META, n_pass), 0)
    off = jnp.where((lane_row == clusters - CL_OWN * dp + 64) | (lane_row > 68) | (lane_row < 64), 0.0, NEGATIVE)
    load_p.wait()
    lane = iota((n_pass, 128), 1)
    head = p_ref[:, :128].astype(F32)
    p0_ref[...] = jnp.where(lane < 64, head, off.T).astype(BF16)
    p1_ref[...] = jnp.where(lane < 64, 0.0, head).astype(BF16)
    eye = onehot(iota((PAIR, PAIR), 0) == iota((PAIR, PAIR), 1))
    for b in range(WIDTH // PAIR):
        pt_ref[pl.ds(b * PAIR, PAIR)] = nt(eye, p_ref[:, b * PAIR:(b + 1) * PAIR]).astype(BF16)
    lines = nq // 8
    pick_line = onehot(iota((lines, nq), 0) == jnp.where(mine, line, -1))
    bsel_ref[...] = nt(pick_line, pick).astype(BF16)
    cdy = lax.bitwise_and(shift(carrier, 1) - y, NY - 1)
    cdc = lax.bitwise_and(carrier - core, 1)
    place = jnp.where(cdy == 0, cdc, jnp.where(cdy == 2, 6 + cdc, jnp.where(cdy == 1, 2, 3) + 2 * cdc))
    spread = onehot(iota((nq, nq), 0) == place * lines + line)
    fsel_ref[...] = nt(onehot(iota((nq, nq), 0) == iota((nq, nq), 1)), spread).astype(BF16)
    stores = [pltpu.make_async_copy(fsel_ref, fsel_hbm, lsem.at[4])]
    stores[0].start()
    stat[...] = jnp.zeros_like(stat)

    def gather_start(buf, base, rows):
        blk = lambda s: buf.at[pl.ds(base + s * rows, rows)]
        g = group(buf.at[pl.ds(base, 7 * rows)])
        return {0: g, 1: send(blk(0), blk(1), at(dc=1), g), 3: send(blk(0), blk(3), at(dy=1), g),
                2: send(blk(0), blk(2), at(dy=3), g), 6: send(blk(0), blk(6), at(dy=2), g)}

    def gather_pass(buf, base, rows, got, s):
        blk = lambda s: buf.at[pl.ds(base + s * rows, rows)]
        got[s].wait_recv()
        on = {2: 4, 3: 5, 6: 7}[s]
        got[on] = send(blk(s), blk(on), at(dc=1), got[0])

    got = []
    for h in range(2):
        arrived[h]()
        rows = nn(unpack_ref[...], in_buf[h]).astype(BF16)
        for b in range(ROW // 128):
            agb[pl.ds(h * HALF, BLOCK), b * 128:(b + 1) * 128] = rows[b * BLOCK:(b + 1) * BLOCK]
        got.append(gather_start(agb, h * HALF, BLOCK))

    core_group = [group(core_out.at[h]) for h in range(2)]
    core_come = [arrival() for h in range(2)]
    chip_group = [group(chip_in.at[h]) for h in range(2)]
    chip_come = [arrival() for h in range(2)]

    def first_pass(u):
        h, q = u // 2, u % 2
        rows = pl.ds(u * PAIR, PAIR)
        cols = pl.ds(u * PAIR, PAIR)
        q0_ref[...] = jnp.where(iota((PAIR, 128), 1) < 64, agb[rows, 0:128].astype(F32),
                                agb[rows, WIDTH:ROW].astype(F32)).astype(BF16)
        value, tops = None, []
        for m in range(5):
            left = (p0_ref[...], p1_ref[...])[m] if m < 2 else p_ref[:, CUTS[m - 1]:CUTS[m]]
            right = (q0_ref[...], agb[rows, 0:128])[m] if m < 2 else agb[rows, CUTS[m - 1]:CUTS[m]]
            part = nt(left, right)
            value = part if value is None else value + part
            prob[m, :, cols] = value
            tops.append(jnp.max(fold(value, jnp.max), axis=0, keepdims=True))
        small = 128

        def exps(j, sums):
            js = pl.ds(pl.multiple_of(j * small, small), small)
            out = []
            for m in range(5):
                e = jnp.exp2((prob[m, js, cols] - tops[m]) * (SCALES[m] * LOG2E))
                prob[m, js, cols] = e
                out.append(sums[m] + fold(e, jnp.sum))
            return tuple(out)

        sums = lax.fori_loop(0, n_pass // small, exps, (jnp.zeros((8, PAIR), F32),) * 5)
        for m in range(5):
            top = tops[m] * SCALES[m]
            total = jnp.sum(sums[m], axis=0, keepdims=True)
            msc[m:m + 1, cols] = top
            lse = top + jnp.log(total)
            for t in range(2):
                stat[h, 2 * q + t, m:m + 1] = lse[:, t * 128:(t + 1) * 128]

    lower = iota((8, 128), 1) < BLOCK

    def turn(value):
        return pltpu.roll(value, BLOCK, 1)

    def by_chip(a, b):
        return jnp.where(lower, a, turn(b)), jnp.where(lower, turn(a), b)

    def join(values):
        top = functools.reduce(jnp.maximum, values)
        return top + jnp.log(functools.reduce(jnp.add, [jnp.exp(v - top) for v in values]))

    def totals_to_core(h):
        core_out[h, 0] = stat[h, 0]
        core_out[h, 1], core_out[h, 2] = by_chip(stat[h, 1], stat[h, 2])
        core_out[h, 3] = stat[h, 3]
        send(core_out.at[h], core_in.at[h], at(dc=1), core_group[h], core_come[h])

    def totals_to_chips(h):
        remote(core_out.at[h], core_in.at[h], core_group[h], core_come[h], at(dc=1)).wait_recv()
        for t in range(4):
            chip_out[h, t] = join([core_out[h, t], turn(core_in[h, t])])
        for t in (3, 1, 2):
            send(chip_out.at[h], chip_in.at[h, t - 1], at(dy=CHIPS[t]), chip_group[h], chip_come[h])

    def totals(h):
        remote(chip_in.at[h], chip_in.at[h], chip_group[h], chip_come[h], at(dc=1)).wait_recv()
        tiles = []
        for t in range(4):
            values = [chip_out[h, t]]
            for f in (1, 2, 3):
                values.append(chip_in[h, f - 1, CHIPS.index((CHIPS[t] + CHIPS[f]) % NY)])
            tiles.append(join(values))
        lse_ref[h, 0] = tiles[0]
        lse_ref[h, 1], lse_ref[h, 2] = by_chip(tiles[1], tiles[2])
        lse_ref[h, 3] = tiles[3]

    base = tile * n_pass
    pick_digit = jnp.where(iota((8, META), 1) == 69, 64.0,
                           jnp.where(iota((8, META), 1) == 70, 1.0, 0.0)).astype(BF16)

    def second_pass(u, between=None):
        h, q = u // 2, u % 2
        rows = pl.ds(u * PAIR, PAIR)
        cols = pl.ds(u * PAIR, PAIR)
        goal = nt(pick_digit, agb[rows, WIDTH:ROW])[0:1].astype(I32) - base
        lse = jnp.concatenate([lse_ref[h, 2 * q], lse_ref[h, 2 * q + 1]], axis=1)
        factor = [jnp.exp(msc[m:m + 1, cols] - lse[m:m + 1]) * SCALES[m] for m in range(5)]
        small = 64

        def weigh(j, carry):
            start = pl.multiple_of(j * small, small)
            js = pl.ds(start, small)
            hit = iota((small, PAIR), 0) == goal - start
            running = None
            for m in range(4, -1, -1):
                term = prob[m, js, cols] * factor[m]
                running = term if running is None else running + term
                wt[m, js, cols] = jnp.where(hit, running - sum(SCALES[m:]), running).astype(BF16)
            return carry

        lax.fori_loop(0, n_pass // small, weigh, 0)
        if between is not None:
            between()
        for m in range(5):
            lo = CUTS[m - 1] if m else 0
            gt[lo:CUTS[m]] = nn(pt_ref[lo:CUTS[m]], wt[m, :, cols]).astype(BF16)
        grad[rows] = nt(eye, gt[...]).astype(BF16)

    sums_in = {}
    sum_group = [group(grad.at[pl.ds(h * HALF, 7 * BLOCK)]) for h in range(2)]

    def block(h, s):
        return grad.at[pl.ds(h * HALF + s * BLOCK, BLOCK)]

    def to_core(h, s):
        i = {1: 0, 4: 1, 5: 2, 7: 3}[s]
        sums_in[h, i] = send(block(h, s), sib.at[h, i], at(dc=1), sum_group[h])

    def to_chip(h, s):
        i = {2: 1, 3: 2, 6: 3}[s]
        sums_in[h, i].wait_recv()
        comb[h, i] = plus(block(h, s)[...], sib[h, i]).astype(BF16)
        sums_in[h, s, s] = send(comb.at[h, i], from_y.at[h, i], at(dy=PLACE[s][0]), sum_group[h])

    def go_back(h):
        sums_in[h, 0].wait_recv()
        for s in (2, 3, 6):
            sums_in[h, s, s].wait_recv()
        total = plus(block(h, 0)[...], sib[h, 0], from_y[h, 1], from_y[h, 2], from_y[h, 3]).astype(BF16)
        for b in range(WIDTH // 128):
            stack[pl.ds(b * BLOCK, BLOCK)] = total[:, b * 128:(b + 1) * 128]
        used = WIDTH // 128 * BLOCK
        back_out[h] = nn(pack_ref[:, :used], stack[pl.ds(0, used)]).astype(BF16)
        return exchange(back_out.at[h], back_in.at[h], behind)

    wide = n_pass // 2

    def passage_part(j):
        js = slice(j * wide, (j + 1) * wide)
        low = nn(wt[0, js], agb[:, 0:128])
        high = nn(wt[1, js], agb[:, 0:128])
        pg_ref[js, 0:128] = jnp.where(iota((wide, 128), 1) < 64, low, high).astype(BF16)
        for m in range(2, 5):
            pg_ref[js, CUTS[m - 1]:CUTS[m]] = nn(wt[m, js], agb[:, CUTS[m - 1]:CUTS[m]]).astype(BF16)
        store = pltpu.make_async_copy(pg_ref.at[js], pg_hbm.at[js], lsem.at[1 + j])
        store.start()
        return store

    def gather_near(h):
        gather_pass(agb, h * HALF, BLOCK, got[h], 2)
        gather_pass(agb, h * HALF, BLOCK, got[h], 3)
        got[h][1].wait_recv()

    def gather_rest(h):
        gather_pass(agb, h * HALF, BLOCK, got[h], 6)
        for s in (4, 5, 7):
            got[h][s].wait_recv()

    gather_near(0)
    first_pass(0)
    gather_rest(0)
    first_pass(1)
    totals_to_core(0)
    gather_near(1)
    first_pass(2)
    totals_to_chips(0)
    gather_rest(1)
    first_pass(3)
    totals_to_core(1)
    totals(0)
    totals_to_chips(1)

    second_pass(1)
    for s in (7, 4, 5):
        to_core(0, s)
    second_pass(0, lambda: to_chip(0, 6))
    to_core(0, 1)
    to_chip(0, 2)
    to_chip(0, 3)
    totals(1)
    second_pass(3)
    for s in (7, 4, 5):
        to_core(1, s)
    second_pass(2, lambda: to_chip(1, 6))
    to_core(1, 1)
    to_chip(1, 2)
    to_chip(1, 3)
    home = [go_back(0)]
    stores.append(passage_part(0))
    home.append(go_back(1))
    stores.append(passage_part(1))

    for h in range(2):
        home[h]()
        used = WIDTH // 128 * BLOCK
        rows = nn(unpack_ref[:used], back_in[h]).astype(BF16)
        for b in range(WIDTH // 128):
            rows_ref[pl.ds(h * BLOCK, BLOCK), b * 128:(b + 1) * 128] = rows[b * BLOCK:(b + 1) * BLOCK]
    fg[pl.ds(0, lines)] = nn(bsel_ref[...], rows_ref[...]).astype(BF16)
    last = gather_start(fg, 0, lines)
    for s in (2, 3, 6):
        gather_pass(fg, 0, lines, last, s)
    for s in (1, 4, 5, 7):
        last[s].wait_recv()
    assert len(groups) == ssem.shape[0] and len(received) == rsem.shape[0]
    write = pltpu.make_async_copy(fg, fg_hbm, lsem.at[3])
    write.start()
    write.wait()
    for store in stores:
        store.wait()
    for g, all_sent in enumerate(groups):
        remote(all_sent, all_sent, g, 0, at(dc=1)).wait_send()


def finish(fsel_hbm, fg_hbm, pg_hbm, qg_hbm, out_hbm, fsel_ref, fg_ref, qg_ref, pg_ref, sems):
    loads = [pltpu.make_async_copy(fsel_hbm, fsel_ref, sems.at[0]), pltpu.make_async_copy(fg_hbm, fg_ref, sems.at[1])]
    for load in loads:
        load.start()
    rows = pg_hbm.shape[0] // PARTS
    parts = [pl.ds(i * rows, rows) for i in range(PARTS)]
    reads = [pltpu.make_async_copy(pg_hbm.at[r], pg_ref.at[r], sems.at[2 + i]) for i, r in enumerate(parts)]
    writes = [pltpu.make_async_copy(pg_ref.at[r], out_hbm.at[r], sems.at[2 + PARTS + i]) for i, r in enumerate(parts)]
    for read in reads:
        read.start()
    for load in loads:
        load.wait()
    for read, write in zip(reads, writes):
        read.wait()
        write.start()
    some = qg_ref.shape[0] // 2
    for i in range(2):
        r = pl.ds(i * some, some)
        qg_ref[r] = nn(fsel_ref[r], fg_ref[...]).astype(BF16)
        write = pltpu.make_async_copy(qg_ref.at[r], qg_hbm.at[r], sems.at[2 + 2 * PARTS + i])
        write.start()
        writes.append(write)
    for write in writes:
        write.wait()


def body(queries, passages, query_cluster, passage_cluster, positive):
    nq, width = queries.shape
    n_pass = passages.shape[0]
    vmem = pl.BlockSpec(memory_space=pltpu.VMEM)
    hbm = pl.BlockSpec(memory_space=pl.ANY)
    V = pltpu.VMEM
    fg, fsel, pg = pl.pallas_call(
        kernel,
        out_shape=(jax.ShapeDtypeStruct((nq, width), BF16), jax.ShapeDtypeStruct((nq, nq), BF16),
                   jax.ShapeDtypeStruct((n_pass, width), BF16)),
        in_specs=[vmem, vmem, vmem, hbm, hbm],
        out_specs=(hbm, hbm, hbm),
        scratch_shapes=[
            V((nq, width), BF16),
            V((n_pass, width), BF16), V((n_pass, 128), BF16), V((n_pass, 128), BF16), V((width, n_pass), BF16),
            V((STACK, 128), BF16), *[V((2, HALF, 128), BF16)] * 4, V((HALF, STACK), BF16), V((STACK, HALF), BF16),
            V((SLOTS, ROW), BF16), V((PAIR, 128), BF16),
            V((5, n_pass, SLOTS), F32), V((5, n_pass, SLOTS), BF16), V((8, SLOTS), F32),
            *[V((2, 4, 8, 128), F32)] * 4, V((2, 3, 4, 8, 128), F32), V((2, 4, 8, 128), F32),
            V((width, PAIR), BF16), V((SLOTS, width), BF16),
            V((2, 4, BLOCK, width), BF16), V((2, 4, BLOCK, width), BF16), V((2, 4, BLOCK, width), BF16),
            V((2 * BLOCK, width), BF16), V((nq, width), BF16), V((nq // 8, 2 * BLOCK), BF16), V((nq, nq), BF16),
            V((n_pass, width), BF16),
            pltpu.SemaphoreType.DMA((13,)), pltpu.SemaphoreType.DMA((43,)), pltpu.SemaphoreType.DMA((5,)),
        ],
        compiler_params=pltpu.CompilerParams(
            collective_id=0, has_side_effects=True, vmem_limit_bytes=58 * 1024 * 1024),
    )(query_cluster.reshape(1, nq), positive.reshape(1, nq), passage_cluster.reshape(1, n_pass), queries, passages)
    return pl.pallas_call(
        finish,
        out_shape=(jax.ShapeDtypeStruct((nq, width), BF16), jax.ShapeDtypeStruct((n_pass, width), BF16)),
        in_specs=[hbm, hbm, hbm],
        out_specs=(hbm, hbm),
        scratch_shapes=[V((nq, nq), BF16), V((nq, width), BF16), V((nq, width), BF16), V((n_pass, width), BF16),
                        pltpu.SemaphoreType.DMA((4 + 2 * PARTS,))],
        compiler_params=pltpu.CompilerParams(vmem_limit_bytes=58 * 1024 * 1024),
    )(fsel, fg, pg)


def solution(mesh):
    in_specs = (P("dp", None), P(("dp", "tile"), None), P("dp"), P(("dp", "tile")), P("dp"))
    out_specs = (P("dp", None), P(("dp", "tile"), None))
    return jax.shard_map(body, mesh=mesh, in_specs=in_specs, out_specs=out_specs, check_vma=False)
```

```python
import functools
import math

import jax
import jax.numpy as jnp
from jax import lax
from jax.experimental import pallas as pl
from jax.experimental.pallas import tpu as pltpu
from jax.sharding import PartitionSpec as P

F32 = jnp.float32
BF16 = jnp.bfloat16
I32 = jnp.int32

NX, NZ, NY, NC = 4, 8, 4, 2
CL_OWN = 4
CAP = 32
NEGATIVE = -1e30
CUTS = (64, 128, 256, 512, 768)
WIDTH = 768
META = 128
ROW = WIDTH + META
SCALES = tuple(2.0 / math.sqrt(k) for k in CUTS)
LOG2E = math.log2(math.e)
BLOCK = 64
PAIR = 4 * BLOCK
HALF = 8 * BLOCK
SLOTS = 2 * HALF
FAR = NX * NZ
CHUNK = 16
STACK = ROW // 128 * BLOCK

PLACE = ((0, 0), (0, 1), (1, 0), (3, 0), (1, 1), (3, 1), (2, 0), (2, 1))
CHIPS = (0, 1, 3, 2)
MESH = pl.DeviceIdType.MESH
PARTS = 4


def nn(a, b):
    return lax.dot_general(a, b, (((1,), (0,)), ((), ())), preferred_element_type=F32)


def nt(a, b):
    return lax.dot_general(a, b, (((1,), (1,)), ((), ())), preferred_element_type=F32)


def iota(shape, dim):
    return lax.broadcasted_iota(I32, shape, dim)


def onehot(mask):
    return jnp.where(mask, 1.0, 0.0).astype(BF16)


def fold(value, op):
    return op(value.reshape(value.shape[0] // 8, 8, value.shape[1]), axis=0)


def plus(*values):
    return functools.reduce(jnp.add, [v.astype(F32) for v in values])


def shift(a, n):
    return lax.shift_right_logical(a, n)


def kernel(qc_ref, pos_ref, pc_ref, q_hbm, p_hbm, fg_hbm, fsel_hbm, pg_hbm,
           q_ref, p_ref, p0_ref, p1_ref, pt_ref, stack, out_buf, in_buf, back_out, back_in, pack_ref, unpack_ref,
           agb, q0_ref, prob, wt, msc, stat, core_out, core_in, chip_out, chip_in, lse_ref, gt, grad, sib, comb, from_y,
           rows_ref, fg, bsel_ref, fsel_ref, pg_ref,
           ssem, rsem, lsem):
    n_pass = p_ref.shape[0]
    dp = lax.axis_index("dp")
    tile = lax.axis_index("tile")
    x, z = lax.div(dp, NZ), lax.rem(dp, NZ)
    y, core = lax.div(tile, NC), lax.rem(tile, NC)

    def at(dy=0, dc=0):
        return (dp, lax.rem(y + dy, NY) * NC + lax.rem(core + dc, NC))

    places = sorted(((dx, dz) for dx in range(NX) for dz in range(NZ) if dx or dz), key=lambda d: abs(d[1] - NZ // 2))
    x_at = [lax.rem(x + d, NX) * NZ for d in range(NX)]
    z_at = [lax.rem(z + d, NZ) for d in range(NZ)]

    def ahead(dx, dz):
        return (x_at[dx] + z_at[dz], tile)

    def behind(dx, dz):
        return ahead((NX - dx) % NX, (NZ - dz) % NZ)

    groups, received = [], []

    def group(all_sent):
        groups.append(all_sent)
        return len(groups) - 1

    def arrival():
        received.append(None)
        return len(received) - 1

    def remote(src, dst, g, i, where):
        return pltpu.make_async_remote_copy(
            src_ref=src, dst_ref=dst, send_sem=ssem.at[g], recv_sem=rsem.at[i], device_id=where, device_id_type=MESH)

    def send(src, dst, where, g, i=None):
        copy = remote(src, dst, g, arrival() if i is None else i, where)
        copy.start()
        return copy

    def exchange(src, dst, where):
        rest = pl.ds(CHUNK, (FAR - 1) * CHUNK)
        g, n = group(src.at[rest]), arrival()

        for dx, dz in places:
            rows = pl.ds((dx * NZ + dz) * CHUNK, CHUNK)
            remote(src.at[rows], dst.at[rows], g, n, where(dx, dz)).start()
        dst[pl.ds(0, CHUNK)] = src[pl.ds(0, CHUNK)]
        return remote(src.at[rest], dst.at[rest], g, n, at(dc=1)).wait_recv

    barrier = pltpu.get_barrier_semaphore()
    for dx, dz in places:
        pl.semaphore_signal(barrier, inc=1, device_id=ahead(dx, dz), device_id_type=MESH)
    near_by = [(0, 1), (1, 0), (2, 0), (3, 0)]
    for dy, dc in near_by:
        pl.semaphore_signal(barrier, inc=1, device_id=at(dy, dc), device_id_type=MESH)
    load_q = pltpu.make_async_copy(q_hbm, q_ref, lsem.at[3])
    load_q.start()
    load_p = pltpu.make_async_copy(p_hbm, p_ref, lsem.at[0])
    load_p.start()

    nq = q_ref.shape[0]
    cluster = qc_ref[...]
    owner = shift(cluster, 2)
    local = lax.bitwise_and(cluster, 3)
    own = jnp.where(iota((FAR, nq), 0) == owner, 1.0, 0.0)
    before = onehot(iota((nq, nq), 0) < iota((nq, nq), 1))
    rank = jnp.sum(own * nn(own.astype(BF16), before), axis=0, keepdims=True)
    first = jnp.sum(jnp.where(owner < iota((FAR, nq), 0), 1.0, 0.0), axis=1, keepdims=True)
    order = (rank + jnp.sum(own * first, axis=0, keepdims=True)).astype(I32)
    rank = rank.astype(I32)
    carrier = lax.bitwise_and(order, 7)
    line = shift(order, 3)
    dxs = lax.bitwise_and(shift(owner, 3) - x, NX - 1)
    dzs = lax.bitwise_and(lax.bitwise_and(owner, NZ - 1) - z, NZ - 1)
    code = shift(rank, 4) * BLOCK + (dxs * NZ + dzs) * 2 + lax.bitwise_and(shift(rank, 3), 1)
    mine = carrier == tile
    pick = onehot(iota((2 * BLOCK, nq), 0) == jnp.where(mine, code, -1))
    row = iota((META, nq), 0)
    target = lax.bitwise_and(pos_ref[...], 8 * n_pass - 1)
    digits = jnp.where(row == 69, shift(target, 6), jnp.where(row == 70, lax.bitwise_and(target, 63), 0))
    digits = jnp.where((row == local + 64) | (row == 68), 1, digits)
    meta = nt(pick, digits.astype(F32).astype(BF16))
    meta = jnp.where(iota((2 * BLOCK, META), 1) == 68, 1.0 - meta, meta).astype(BF16)
    load_q.wait()
    sent = nn(pick, q_ref[...]).astype(BF16)
    r, c = iota((HALF, STACK), 0), iota((HALF, STACK), 1)
    pack_ref[...] = onehot((shift(lax.bitwise_and(r, CHUNK - 1), 1) == shift(c, 6))
                           & (lax.bitwise_and(c, BLOCK - 1) == shift(r, 4) * 2 + lax.bitwise_and(r, 1)))
    c, r = iota((STACK, HALF), 0), iota((STACK, HALF), 1)
    unpack_ref[...] = onehot((shift(lax.bitwise_and(r, CHUNK - 1), 1) == shift(c, 6))
                             & (lax.bitwise_and(c, BLOCK - 1) == shift(r, 4) * 2 + lax.bitwise_and(r, 1)))
    for h in range(2):
        for b in range(WIDTH // 128):
            stack[pl.ds(b * BLOCK, BLOCK)] = sent[h * BLOCK:(h + 1) * BLOCK, b * 128:(b + 1) * 128]
        stack[pl.ds(STACK - BLOCK, BLOCK)] = meta[h * BLOCK:(h + 1) * BLOCK]
        out_buf[h] = nn(pack_ref[...], stack[...]).astype(BF16)

    pl.semaphore_wait(barrier, len(places) + len(near_by))

    arrived = [exchange(out_buf.at[h], in_buf.at[h], ahead) for h in range(2)]

    clusters = pc_ref[...]
    lane_row = iota((META, n_pass), 0)
    off = jnp.where((lane_row == clusters - CL_OWN * dp + 64) | (lane_row > 68) | (lane_row < 64), 0.0, NEGATIVE)
    load_p.wait()
    lane = iota((n_pass, 128), 1)
    head = p_ref[:, :128].astype(F32)
    p0_ref[...] = jnp.where(lane < 64, head, off.T).astype(BF16)
    p1_ref[...] = jnp.where(lane < 64, 0.0, head).astype(BF16)
    eye = onehot(iota((PAIR, PAIR), 0) == iota((PAIR, PAIR), 1))
    for b in range(WIDTH // PAIR):
        pt_ref[pl.ds(b * PAIR, PAIR)] = nt(eye, p_ref[:, b * PAIR:(b + 1) * PAIR]).astype(BF16)
    lines = nq // 8
    pick_line = onehot(iota((lines, nq), 0) == jnp.where(mine, line, -1))
    bsel_ref[...] = nt(pick_line, pick).astype(BF16)
    cdy = lax.bitwise_and(shift(carrier, 1) - y, NY - 1)
    cdc = lax.bitwise_and(carrier - core, 1)
    place = jnp.where(cdy == 0, cdc, jnp.where(cdy == 2, 6 + cdc, jnp.where(cdy == 1, 2, 3) + 2 * cdc))
    spread = onehot(iota((nq, nq), 0) == place * lines + line)
    fsel_ref[...] = nt(onehot(iota((nq, nq), 0) == iota((nq, nq), 1)), spread).astype(BF16)
    stores = [pltpu.make_async_copy(fsel_ref, fsel_hbm, lsem.at[4])]
    stores[0].start()
    stat[...] = jnp.zeros_like(stat)

    def gather_start(buf, base, rows):
        blk = lambda s: buf.at[pl.ds(base + s * rows, rows)]
        g = group(buf.at[pl.ds(base, 7 * rows)])
        return {0: g, 1: send(blk(0), blk(1), at(dc=1), g), 3: send(blk(0), blk(3), at(dy=1), g),
                2: send(blk(0), blk(2), at(dy=3), g), 6: send(blk(0), blk(6), at(dy=2), g)}

    def gather_pass(buf, base, rows, got, s):
        blk = lambda s: buf.at[pl.ds(base + s * rows, rows)]
        got[s].wait_recv()
        on = {2: 4, 3: 5, 6: 7}[s]
        got[on] = send(blk(s), blk(on), at(dc=1), got[0])

    got = []
    for h in range(2):
        arrived[h]()
        rows = nn(unpack_ref[...], in_buf[h]).astype(BF16)
        for b in range(ROW // 128):
            agb[pl.ds(h * HALF, BLOCK), b * 128:(b + 1) * 128] = rows[b * BLOCK:(b + 1) * BLOCK]
        got.append(gather_start(agb, h * HALF, BLOCK))

    core_group = [group(core_out.at[h]) for h in range(2)]
    core_come = [arrival() for h in range(2)]
    chip_group = [group(chip_in.at[h]) for h in range(2)]
    chip_come = [arrival() for h in range(2)]

    def first_pass(u):
        h, q = u // 2, u % 2
        rows = pl.ds(u * PAIR, PAIR)
        cols = pl.ds(u * PAIR, PAIR)
        q0_ref[...] = jnp.where(iota((PAIR, 128), 1) < 64, agb[rows, 0:128].astype(F32),
                                agb[rows, WIDTH:ROW].astype(F32)).astype(BF16)
        value, tops = None, []
        for m in range(5):
            left = (p0_ref[...], p1_ref[...])[m] if m < 2 else p_ref[:, CUTS[m - 1]:CUTS[m]]
            right = (q0_ref[...], agb[rows, 0:128])[m] if m < 2 else agb[rows, CUTS[m - 1]:CUTS[m]]
            part = nt(left, right)
            value = part if value is None else value + part
            prob[m, :, cols] = value
            tops.append(jnp.max(fold(value, jnp.max), axis=0, keepdims=True))
        small = 128

        def exps(j, sums):
            js = pl.ds(pl.multiple_of(j * small, small), small)
            out = []
            for m in range(5):
                e = jnp.exp2((prob[m, js, cols] - tops[m]) * (SCALES[m] * LOG2E))
                prob[m, js, cols] = e
                out.append(sums[m] + fold(e, jnp.sum))
            return tuple(out)

        sums = lax.fori_loop(0, n_pass // small, exps, (jnp.zeros((8, PAIR), F32),) * 5)
        for m in range(5):
            top = tops[m] * SCALES[m]
            total = jnp.sum(sums[m], axis=0, keepdims=True)
            msc[m:m + 1, cols] = top
            lse = top + jnp.log(total)
            for t in range(2):
                stat[h, 2 * q + t, m:m + 1] = lse[:, t * 128:(t + 1) * 128]

    lower = iota((8, 128), 1) < BLOCK

    def turn(value):
        return pltpu.roll(value, BLOCK, 1)

    def by_chip(a, b):
        return jnp.where(lower, a, turn(b)), jnp.where(lower, turn(a), b)

    def join(values):
        top = functools.reduce(jnp.maximum, values)
        return top + jnp.log(functools.reduce(jnp.add, [jnp.exp(v - top) for v in values]))

    def totals_to_core(h):
        core_out[h, 0] = stat[h, 0]
        core_out[h, 1], core_out[h, 2] = by_chip(stat[h, 1], stat[h, 2])
        core_out[h, 3] = stat[h, 3]
        send(core_out.at[h], core_in.at[h], at(dc=1), core_group[h], core_come[h])

    def totals_to_chips(h):
        remote(core_out.at[h], core_in.at[h], core_group[h], core_come[h], at(dc=1)).wait_recv()
        for t in range(4):
            chip_out[h, t] = join([core_out[h, t], turn(core_in[h, t])])
        for t in (3, 1, 2):
            send(chip_out.at[h], chip_in.at[h, t - 1], at(dy=CHIPS[t]), chip_group[h], chip_come[h])

    def totals(h):
        remote(chip_in.at[h], chip_in.at[h], chip_group[h], chip_come[h], at(dc=1)).wait_recv()
        tiles = []
        for t in range(4):
            values = [chip_out[h, t]]
            for f in (1, 2, 3):
                values.append(chip_in[h, f - 1, CHIPS.index((CHIPS[t] + CHIPS[f]) % NY)])
            tiles.append(join(values))
        lse_ref[h, 0] = tiles[0]
        lse_ref[h, 1], lse_ref[h, 2] = by_chip(tiles[1], tiles[2])
        lse_ref[h, 3] = tiles[3]

    base = tile * n_pass
    pick_digit = jnp.where(iota((8, META), 1) == 69, 64.0,
                           jnp.where(iota((8, META), 1) == 70, 1.0, 0.0)).astype(BF16)

    def second_pass(u, between=None):
        h, q = u // 2, u % 2
        rows = pl.ds(u * PAIR, PAIR)
        cols = pl.ds(u * PAIR, PAIR)
        goal = nt(pick_digit, agb[rows, WIDTH:ROW])[0:1].astype(I32) - base
        lse = jnp.concatenate([lse_ref[h, 2 * q], lse_ref[h, 2 * q + 1]], axis=1)
        factor = [jnp.exp(msc[m:m + 1, cols] - lse[m:m + 1]) * SCALES[m] for m in range(5)]
        small = 64

        def weigh(j, carry):
            start = pl.multiple_of(j * small, small)
            js = pl.ds(start, small)
            hit = iota((small, PAIR), 0) == goal - start
            running = None
            for m in range(4, -1, -1):
                term = prob[m, js, cols] * factor[m]
                running = term if running is None else running + term
                wt[m, js, cols] = jnp.where(hit, running - sum(SCALES[m:]), running).astype(BF16)
            return carry

        lax.fori_loop(0, n_pass // small, weigh, 0)
        if between is not None:
            between()
        for m in range(5):
            lo = CUTS[m - 1] if m else 0
            gt[lo:CUTS[m]] = nn(pt_ref[lo:CUTS[m]], wt[m, :, cols]).astype(BF16)
        grad[rows] = nt(eye, gt[...]).astype(BF16)

    sums_in = {}
    sum_group = [group(grad.at[pl.ds(h * HALF, 7 * BLOCK)]) for h in range(2)]

    def block(h, s):
        return grad.at[pl.ds(h * HALF + s * BLOCK, BLOCK)]

    def to_core(h, s):
        i = {1: 0, 4: 1, 5: 2, 7: 3}[s]
        sums_in[h, i] = send(block(h, s), sib.at[h, i], at(dc=1), sum_group[h])

    def to_chip(h, s):
        i = {2: 1, 3: 2, 6: 3}[s]
        sums_in[h, i].wait_recv()
        comb[h, i] = plus(block(h, s)[...], sib[h, i]).astype(BF16)
        sums_in[h, s, s] = send(comb.at[h, i], from_y.at[h, i], at(dy=PLACE[s][0]), sum_group[h])

    def go_back(h):
        sums_in[h, 0].wait_recv()
        for s in (2, 3, 6):
            sums_in[h, s, s].wait_recv()
        total = plus(block(h, 0)[...], sib[h, 0], from_y[h, 1], from_y[h, 2], from_y[h, 3]).astype(BF16)
        for b in range(WIDTH // 128):
            stack[pl.ds(b * BLOCK, BLOCK)] = total[:, b * 128:(b + 1) * 128]
        used = WIDTH // 128 * BLOCK
        back_out[h] = nn(pack_ref[:, :used], stack[pl.ds(0, used)]).astype(BF16)
        return exchange(back_out.at[h], back_in.at[h], behind)

    wide = n_pass // 2

    def passage_part(j):
        js = slice(j * wide, (j + 1) * wide)
        low = nn(wt[0, js], agb[:, 0:128])
        high = nn(wt[1, js], agb[:, 0:128])
        pg_ref[js, 0:128] = jnp.where(iota((wide, 128), 1) < 64, low, high).astype(BF16)
        for m in range(2, 5):
            pg_ref[js, CUTS[m - 1]:CUTS[m]] = nn(wt[m, js], agb[:, CUTS[m - 1]:CUTS[m]]).astype(BF16)
        store = pltpu.make_async_copy(pg_ref.at[js], pg_hbm.at[js], lsem.at[1 + j])
        store.start()
        return store

    def gather_near(h):
        gather_pass(agb, h * HALF, BLOCK, got[h], 2)
        gather_pass(agb, h * HALF, BLOCK, got[h], 3)
        got[h][1].wait_recv()

    def gather_rest(h):
        gather_pass(agb, h * HALF, BLOCK, got[h], 6)
        for s in (4, 5, 7):
            got[h][s].wait_recv()

    gather_near(0)
    first_pass(0)
    gather_rest(0)
    first_pass(1)
    totals_to_core(0)
    gather_near(1)
    first_pass(2)
    totals_to_chips(0)
    gather_rest(1)
    first_pass(3)
    totals_to_core(1)
    totals(0)

    second_pass(1, lambda: totals_to_chips(1))
    for s in (7, 4, 5):
        to_core(0, s)
    second_pass(0, lambda: to_chip(0, 6))
    to_core(0, 1)
    to_chip(0, 2)
    to_chip(0, 3)
    totals(1)
    second_pass(3)
    for s in (7, 4, 5):
        to_core(1, s)
    second_pass(2, lambda: to_chip(1, 6))
    to_core(1, 1)
    to_chip(1, 2)
    to_chip(1, 3)
    home = [go_back(0)]
    stores.append(passage_part(0))
    home.append(go_back(1))
    stores.append(passage_part(1))

    for h in range(2):
        home[h]()
        used = WIDTH // 128 * BLOCK
        rows = nn(unpack_ref[:used], back_in[h]).astype(BF16)
        for b in range(WIDTH // 128):
            rows_ref[pl.ds(h * BLOCK, BLOCK), b * 128:(b + 1) * 128] = rows[b * BLOCK:(b + 1) * BLOCK]
    fg[pl.ds(0, lines)] = nn(bsel_ref[...], rows_ref[...]).astype(BF16)
    last = gather_start(fg, 0, lines)

    def write_out(s):
        rows = pl.ds(s * lines, 2 * lines)
        stores.append(pltpu.make_async_copy(fg.at[rows], fg_hbm.at[rows], lsem.at[5 + s // 2]))
        stores[-1].start()

    last[1].wait_recv()
    write_out(0)
    gather_pass(fg, 0, lines, last, 2)
    gather_pass(fg, 0, lines, last, 3)
    write_out(2)
    last[4].wait_recv()
    last[5].wait_recv()
    write_out(4)
    gather_pass(fg, 0, lines, last, 6)
    last[7].wait_recv()
    write_out(6)
    assert len(groups) == ssem.shape[0] and len(received) == rsem.shape[0]
    for store in stores:
        store.wait()
    for g, all_sent in enumerate(groups):
        remote(all_sent, all_sent, g, 0, at(dc=1)).wait_send()


def finish(fsel_hbm, fg_hbm, pg_hbm, qg_hbm, out_hbm, fsel_ref, fg_ref, qg_ref, pg_ref, sems):
    loads = [pltpu.make_async_copy(fsel_hbm, fsel_ref, sems.at[0]), pltpu.make_async_copy(fg_hbm, fg_ref, sems.at[1])]
    for load in loads:
        load.start()
    rows = pg_hbm.shape[0] // PARTS
    parts = [pl.ds(i * rows, rows) for i in range(PARTS)]
    reads = [pltpu.make_async_copy(pg_hbm.at[r], pg_ref.at[r], sems.at[2 + i]) for i, r in enumerate(parts)]
    writes = [pltpu.make_async_copy(pg_ref.at[r], out_hbm.at[r], sems.at[2 + PARTS + i]) for i, r in enumerate(parts)]
    for read in reads:
        read.start()
    for load in loads:
        load.wait()
    for read, write in zip(reads, writes):
        read.wait()
        write.start()
    some = qg_ref.shape[0] // 2
    for i in range(2):
        r = pl.ds(i * some, some)
        qg_ref[r] = nn(fsel_ref[r], fg_ref[...]).astype(BF16)
        write = pltpu.make_async_copy(qg_ref.at[r], qg_hbm.at[r], sems.at[2 + 2 * PARTS + i])
        write.start()
        writes.append(write)
    for write in writes:
        write.wait()


def body(queries, passages, query_cluster, passage_cluster, positive):
    nq, width = queries.shape
    n_pass = passages.shape[0]
    vmem = pl.BlockSpec(memory_space=pltpu.VMEM)
    hbm = pl.BlockSpec(memory_space=pl.ANY)
    V = pltpu.VMEM
    fg, fsel, pg = pl.pallas_call(
        kernel,
        out_shape=(jax.ShapeDtypeStruct((nq, width), BF16), jax.ShapeDtypeStruct((nq, nq), BF16),
                   jax.ShapeDtypeStruct((n_pass, width), BF16)),
        in_specs=[vmem, vmem, vmem, hbm, hbm],
        out_specs=(hbm, hbm, hbm),
        scratch_shapes=[
            V((nq, width), BF16),
            V((n_pass, width), BF16), V((n_pass, 128), BF16), V((n_pass, 128), BF16), V((width, n_pass), BF16),
            V((STACK, 128), BF16), *[V((2, HALF, 128), BF16)] * 4, V((HALF, STACK), BF16), V((STACK, HALF), BF16),
            V((SLOTS, ROW), BF16), V((PAIR, 128), BF16),
            V((5, n_pass, SLOTS), F32), V((5, n_pass, SLOTS), BF16), V((8, SLOTS), F32),
            *[V((2, 4, 8, 128), F32)] * 4, V((2, 3, 4, 8, 128), F32), V((2, 4, 8, 128), F32),
            V((width, PAIR), BF16), V((SLOTS, width), BF16),
            V((2, 4, BLOCK, width), BF16), V((2, 4, BLOCK, width), BF16), V((2, 4, BLOCK, width), BF16),
            V((2 * BLOCK, width), BF16), V((nq, width), BF16), V((nq // 8, 2 * BLOCK), BF16), V((nq, nq), BF16),
            V((n_pass, width), BF16),
            pltpu.SemaphoreType.DMA((13,)), pltpu.SemaphoreType.DMA((43,)), pltpu.SemaphoreType.DMA((9,)),
        ],
        compiler_params=pltpu.CompilerParams(
            collective_id=0, has_side_effects=True, vmem_limit_bytes=58 * 1024 * 1024),
    )(query_cluster.reshape(1, nq), positive.reshape(1, nq), passage_cluster.reshape(1, n_pass), queries, passages)
    return pl.pallas_call(
        finish,
        out_shape=(jax.ShapeDtypeStruct((nq, width), BF16), jax.ShapeDtypeStruct((n_pass, width), BF16)),
        in_specs=[hbm, hbm, hbm],
        out_specs=(hbm, hbm),
        scratch_shapes=[V((nq, nq), BF16), V((nq, width), BF16), V((nq, width), BF16), V((n_pass, width), BF16),
                        pltpu.SemaphoreType.DMA((4 + 2 * PARTS,))],
        compiler_params=pltpu.CompilerParams(vmem_limit_bytes=58 * 1024 * 1024),
    )(fsel, fg, pg)


def solution(mesh):
    in_specs = (P("dp", None), P(("dp", "tile"), None), P("dp"), P(("dp", "tile")), P("dp"))
    out_specs = (P("dp", None), P(("dp", "tile"), None))
    return jax.shard_map(body, mesh=mesh, in_specs=in_specs, out_specs=out_specs, check_vma=False)
```

```python
import functools
import math

import jax
import jax.numpy as jnp
from jax import lax
from jax.experimental import pallas as pl
from jax.experimental.pallas import tpu as pltpu
from jax.sharding import PartitionSpec as P

F32 = jnp.float32
BF16 = jnp.bfloat16
I32 = jnp.int32

NX, NZ, NY, NC = 4, 8, 4, 2
CL_OWN = 4
CAP = 32
NEGATIVE = -1e30
CUTS = (64, 128, 256, 512, 768)
WIDTH = 768
META = 128
ROW = WIDTH + META
SCALES = tuple(2.0 / math.sqrt(k) for k in CUTS)
LOG2E = math.log2(math.e)
BLOCK = 64
PAIR = 4 * BLOCK
HALF = 8 * BLOCK
SLOTS = 2 * HALF
FAR = NX * NZ
CHUNK = 16
STACK = ROW // 128 * BLOCK

PLACE = ((0, 0), (0, 1), (1, 0), (3, 0), (1, 1), (3, 1), (2, 0), (2, 1))
CHIPS = (0, 1, 3, 2)
MESH = pl.DeviceIdType.MESH
PARTS = 4


def nn(a, b):
    return lax.dot_general(a, b, (((1,), (0,)), ((), ())), preferred_element_type=F32)


def nt(a, b):
    return lax.dot_general(a, b, (((1,), (1,)), ((), ())), preferred_element_type=F32)


def iota(shape, dim):
    return lax.broadcasted_iota(I32, shape, dim)


def onehot(mask):
    return jnp.where(mask, 1.0, 0.0).astype(BF16)


def fold(value, op):
    return op(value.reshape(value.shape[0] // 8, 8, value.shape[1]), axis=0)


def plus(*values):
    return functools.reduce(jnp.add, [v.astype(F32) for v in values])


def shift(a, n):
    return lax.shift_right_logical(a, n)


def kernel(qc_hbm, pos_hbm, pc_hbm, q_hbm, p_hbm, fg_hbm, fsel_hbm, pg_hbm,
           qc_ref, pos_ref, pc_ref, q_ref, p_ref, p0_ref, p1_ref, pt_ref, stack, out_buf, in_buf, back_out, back_in, pack_ref, unpack_ref,
           agb, q0_ref, prob, wt, msc, stat, core_out, core_in, chip_out, chip_in, lse_ref, gt, grad, sib, comb, from_y,
           rows_ref, fg, bsel_ref, fsel_ref, pg_ref,
           ssem, rsem, lsem):
    n_pass = p_ref.shape[0]
    dp = lax.axis_index("dp")
    tile = lax.axis_index("tile")
    x, z = lax.div(dp, NZ), lax.rem(dp, NZ)
    y, core = lax.div(tile, NC), lax.rem(tile, NC)

    def at(dy=0, dc=0):
        return (dp, lax.rem(y + dy, NY) * NC + lax.rem(core + dc, NC))

    places = sorted(((dx, dz) for dx in range(NX) for dz in range(NZ) if dx or dz), key=lambda d: abs(d[1] - NZ // 2))
    x_at = [lax.rem(x + d, NX) * NZ for d in range(NX)]
    z_at = [lax.rem(z + d, NZ) for d in range(NZ)]

    def ahead(dx, dz):
        return (x_at[dx] + z_at[dz], tile)

    def behind(dx, dz):
        return ahead((NX - dx) % NX, (NZ - dz) % NZ)

    groups, received = [], []

    def group(all_sent):
        groups.append(all_sent)
        return len(groups) - 1

    def arrival():
        received.append(None)
        return len(received) - 1

    def remote(src, dst, g, i, where):
        return pltpu.make_async_remote_copy(
            src_ref=src, dst_ref=dst, send_sem=ssem.at[g], recv_sem=rsem.at[i], device_id=where, device_id_type=MESH)

    def send(src, dst, where, g, i=None):
        copy = remote(src, dst, g, arrival() if i is None else i, where)
        copy.start()
        return copy

    def exchange(src, dst, where):
        rest = pl.ds(CHUNK, (FAR - 1) * CHUNK)
        g, n = group(src.at[rest]), arrival()

        for dx, dz in places:
            rows = pl.ds((dx * NZ + dz) * CHUNK, CHUNK)
            remote(src.at[rows], dst.at[rows], g, n, where(dx, dz)).start()
        dst[pl.ds(0, CHUNK)] = src[pl.ds(0, CHUNK)]
        return remote(src.at[rest], dst.at[rest], g, n, at(dc=1)).wait_recv

    barrier = pltpu.get_barrier_semaphore()
    for dx, dz in places:
        pl.semaphore_signal(barrier, inc=1, device_id=ahead(dx, dz), device_id_type=MESH)
    near_by = [(0, 1), (1, 0), (2, 0), (3, 0)]
    for dy, dc in near_by:
        pl.semaphore_signal(barrier, inc=1, device_id=at(dy, dc), device_id_type=MESH)
    small_loads = [pltpu.make_async_copy(src, dst, lsem.at[9 + i]) for i, (src, dst) in
                   enumerate(((qc_hbm, qc_ref), (pos_hbm, pos_ref), (pc_hbm, pc_ref)))]
    for load in small_loads:
        load.start()
    load_q = pltpu.make_async_copy(q_hbm, q_ref, lsem.at[3])
    load_q.start()
    load_p = pltpu.make_async_copy(p_hbm, p_ref, lsem.at[0])
    load_p.start()

    nq = q_ref.shape[0]
    for load in small_loads:
        load.wait()
    cluster = qc_ref[...]
    owner = shift(cluster, 2)
    local = lax.bitwise_and(cluster, 3)
    own = jnp.where(iota((FAR, nq), 0) == owner, 1.0, 0.0)
    before = onehot(iota((nq, nq), 0) < iota((nq, nq), 1))
    rank = jnp.sum(own * nn(own.astype(BF16), before), axis=0, keepdims=True)
    first = jnp.sum(jnp.where(owner < iota((FAR, nq), 0), 1.0, 0.0), axis=1, keepdims=True)
    order = (rank + jnp.sum(own * first, axis=0, keepdims=True)).astype(I32)
    rank = rank.astype(I32)
    carrier = lax.bitwise_and(order, 7)
    line = shift(order, 3)
    dxs = lax.bitwise_and(shift(owner, 3) - x, NX - 1)
    dzs = lax.bitwise_and(lax.bitwise_and(owner, NZ - 1) - z, NZ - 1)
    code = shift(rank, 4) * BLOCK + (dxs * NZ + dzs) * 2 + lax.bitwise_and(shift(rank, 3), 1)
    mine = carrier == tile
    pick = onehot(iota((2 * BLOCK, nq), 0) == jnp.where(mine, code, -1))
    row = iota((META, nq), 0)
    target = lax.bitwise_and(pos_ref[...], 8 * n_pass - 1)
    digits = jnp.where(row == 69, shift(target, 6), jnp.where(row == 70, lax.bitwise_and(target, 63), 0))
    digits = jnp.where((row == local + 64) | (row == 68), 1, digits)
    meta = nt(pick, digits.astype(F32).astype(BF16))
    meta = jnp.where(iota((2 * BLOCK, META), 1) == 68, 1.0 - meta, meta).astype(BF16)
    load_q.wait()
    sent = nn(pick, q_ref[...]).astype(BF16)
    r, c = iota((HALF, STACK), 0), iota((HALF, STACK), 1)
    pack_ref[...] = onehot((shift(lax.bitwise_and(r, CHUNK - 1), 1) == shift(c, 6))
                           & (lax.bitwise_and(c, BLOCK - 1) == shift(r, 4) * 2 + lax.bitwise_and(r, 1)))
    for h in range(2):
        for b in range(WIDTH // 128):
            stack[pl.ds(b * BLOCK, BLOCK)] = sent[h * BLOCK:(h + 1) * BLOCK, b * 128:(b + 1) * 128]
        stack[pl.ds(STACK - BLOCK, BLOCK)] = meta[h * BLOCK:(h + 1) * BLOCK]
        out_buf[h] = nn(pack_ref[...], stack[...]).astype(BF16)

    pl.semaphore_wait(barrier, len(places) + len(near_by))

    arrived = [exchange(out_buf.at[h], in_buf.at[h], ahead) for h in range(2)]

    c, r = iota((STACK, HALF), 0), iota((STACK, HALF), 1)
    unpack_ref[...] = onehot((shift(lax.bitwise_and(r, CHUNK - 1), 1) == shift(c, 6))
                             & (lax.bitwise_and(c, BLOCK - 1) == shift(r, 4) * 2 + lax.bitwise_and(r, 1)))
    clusters = pc_ref[...]
    lane_row = iota((META, n_pass), 0)
    off = jnp.where((lane_row == clusters - CL_OWN * dp + 64) | (lane_row > 68) | (lane_row < 64), 0.0, NEGATIVE)
    load_p.wait()
    lane = iota((n_pass, 128), 1)
    head = p_ref[:, :128].astype(F32)
    p0_ref[...] = jnp.where(lane < 64, head, off.T).astype(BF16)
    p1_ref[...] = jnp.where(lane < 64, 0.0, head).astype(BF16)
    eye = onehot(iota((PAIR, PAIR), 0) == iota((PAIR, PAIR), 1))
    for b in range(WIDTH // PAIR):
        pt_ref[pl.ds(b * PAIR, PAIR)] = nt(eye, p_ref[:, b * PAIR:(b + 1) * PAIR]).astype(BF16)
    lines = nq // 8
    pick_line = onehot(iota((lines, nq), 0) == jnp.where(mine, line, -1))
    bsel_ref[...] = nt(pick_line, pick).astype(BF16)
    cdy = lax.bitwise_and(shift(carrier, 1) - y, NY - 1)
    cdc = lax.bitwise_and(carrier - core, 1)
    place = jnp.where(cdy == 0, cdc, jnp.where(cdy == 2, 6 + cdc, jnp.where(cdy == 1, 2, 3) + 2 * cdc))
    spread = onehot(iota((nq, nq), 0) == place * lines + line)
    fsel_ref[...] = nt(onehot(iota((nq, nq), 0) == iota((nq, nq), 1)), spread).astype(BF16)
    stores = [pltpu.make_async_copy(fsel_ref, fsel_hbm, lsem.at[4])]
    stores[0].start()
    stat[...] = jnp.zeros_like(stat)

    def gather_start(buf, base, rows):
        blk = lambda s: buf.at[pl.ds(base + s * rows, rows)]
        g = group(buf.at[pl.ds(base, 7 * rows)])
        return {0: g, 1: send(blk(0), blk(1), at(dc=1), g), 3: send(blk(0), blk(3), at(dy=1), g),
                2: send(blk(0), blk(2), at(dy=3), g), 6: send(blk(0), blk(6), at(dy=2), g)}

    def gather_pass(buf, base, rows, got, s):
        blk = lambda s: buf.at[pl.ds(base + s * rows, rows)]
        got[s].wait_recv()
        on = {2: 4, 3: 5, 6: 7}[s]
        got[on] = send(blk(s), blk(on), at(dc=1), got[0])

    got = []
    for h in range(2):
        arrived[h]()
        rows = nn(unpack_ref[...], in_buf[h]).astype(BF16)
        for b in range(ROW // 128):
            agb[pl.ds(h * HALF, BLOCK), b * 128:(b + 1) * 128] = rows[b * BLOCK:(b + 1) * BLOCK]
        got.append(gather_start(agb, h * HALF, BLOCK))

    core_group = [group(core_out.at[h]) for h in range(2)]
    core_come = [arrival() for h in range(2)]
    chip_group = [group(chip_in.at[h]) for h in range(2)]
    chip_come = [arrival() for h in range(2)]

    def first_pass(u):
        h, q = u // 2, u % 2
        rows = pl.ds(u * PAIR, PAIR)
        cols = pl.ds(u * PAIR, PAIR)
        q0_ref[...] = jnp.where(iota((PAIR, 128), 1) < 64, agb[rows, 0:128].astype(F32),
                                agb[rows, WIDTH:ROW].astype(F32)).astype(BF16)
        value, tops = None, []
        for m in range(5):
            left = (p0_ref[...], p1_ref[...])[m] if m < 2 else p_ref[:, CUTS[m - 1]:CUTS[m]]
            right = (q0_ref[...], agb[rows, 0:128])[m] if m < 2 else agb[rows, CUTS[m - 1]:CUTS[m]]
            part = nt(left, right)
            value = part if value is None else value + part
            prob[m, :, cols] = value
            tops.append(jnp.max(fold(value, jnp.max), axis=0, keepdims=True))
        small = 128

        def exps(j, sums):
            js = pl.ds(pl.multiple_of(j * small, small), small)
            out = []
            for m in range(5):
                e = jnp.exp2((prob[m, js, cols] - tops[m]) * (SCALES[m] * LOG2E))
                prob[m, js, cols] = e
                out.append(sums[m] + fold(e, jnp.sum))
            return tuple(out)

        sums = lax.fori_loop(0, n_pass // small, exps, (jnp.zeros((8, PAIR), F32),) * 5)
        for m in range(5):
            top = tops[m] * SCALES[m]
            total = jnp.sum(sums[m], axis=0, keepdims=True)
            msc[m:m + 1, cols] = top
            lse = top + jnp.log(total)
            for t in range(2):
                stat[h, 2 * q + t, m:m + 1] = lse[:, t * 128:(t + 1) * 128]

    lower = iota((8, 128), 1) < BLOCK

    def turn(value):
        return pltpu.roll(value, BLOCK, 1)

    def by_chip(a, b):
        return jnp.where(lower, a, turn(b)), jnp.where(lower, turn(a), b)

    def join(values):
        top = functools.reduce(jnp.maximum, values)
        return top + jnp.log(functools.reduce(jnp.add, [jnp.exp(v - top) for v in values]))

    def totals_to_core(h):
        core_out[h, 0] = stat[h, 0]
        core_out[h, 1], core_out[h, 2] = by_chip(stat[h, 1], stat[h, 2])
        core_out[h, 3] = stat[h, 3]
        send(core_out.at[h], core_in.at[h], at(dc=1), core_group[h], core_come[h])

    def totals_to_chips(h):
        remote(core_out.at[h], core_in.at[h], core_group[h], core_come[h], at(dc=1)).wait_recv()
        for t in range(4):
            chip_out[h, t] = join([core_out[h, t], turn(core_in[h, t])])
        for t in (3, 1, 2):
            send(chip_out.at[h], chip_in.at[h, t - 1], at(dy=CHIPS[t]), chip_group[h], chip_come[h])

    def totals(h):
        remote(chip_in.at[h], chip_in.at[h], chip_group[h], chip_come[h], at(dc=1)).wait_recv()
        tiles = []
        for t in range(4):
            values = [chip_out[h, t]]
            for f in (1, 2, 3):
                values.append(chip_in[h, f - 1, CHIPS.index((CHIPS[t] + CHIPS[f]) % NY)])
            tiles.append(join(values))
        lse_ref[h, 0] = tiles[0]
        lse_ref[h, 1], lse_ref[h, 2] = by_chip(tiles[1], tiles[2])
        lse_ref[h, 3] = tiles[3]

    base = tile * n_pass
    pick_digit = jnp.where(iota((8, META), 1) == 69, 64.0,
                           jnp.where(iota((8, META), 1) == 70, 1.0, 0.0)).astype(BF16)

    def second_pass(u, between=None):
        h, q = u // 2, u % 2
        rows = pl.ds(u * PAIR, PAIR)
        cols = pl.ds(u * PAIR, PAIR)
        goal = nt(pick_digit, agb[rows, WIDTH:ROW])[0:1].astype(I32) - base
        lse = jnp.concatenate([lse_ref[h, 2 * q], lse_ref[h, 2 * q + 1]], axis=1)
        factor = [jnp.exp(msc[m:m + 1, cols] - lse[m:m + 1]) * SCALES[m] for m in range(5)]
        small = 64

        def weigh(j, carry):
            start = pl.multiple_of(j * small, small)
            js = pl.ds(start, small)
            hit = iota((small, PAIR), 0) == goal - start
            running = None
            for m in range(4, -1, -1):
                term = prob[m, js, cols] * factor[m]
                running = term if running is None else running + term
                wt[m, js, cols] = jnp.where(hit, running - sum(SCALES[m:]), running).astype(BF16)
            return carry

        lax.fori_loop(0, n_pass // small, weigh, 0)
        if between is not None:
            between()
        for m in range(5):
            lo = CUTS[m - 1] if m else 0
            gt[lo:CUTS[m]] = nn(pt_ref[lo:CUTS[m]], wt[m, :, cols]).astype(BF16)
        grad[rows] = nt(eye, gt[...]).astype(BF16)

    sums_in = {}
    sum_group = [group(grad.at[pl.ds(h * HALF, 7 * BLOCK)]) for h in range(2)]

    def block(h, s):
        return grad.at[pl.ds(h * HALF + s * BLOCK, BLOCK)]

    def to_core(h, s):
        i = {1: 0, 4: 1, 5: 2, 7: 3}[s]
        sums_in[h, i] = send(block(h, s), sib.at[h, i], at(dc=1), sum_group[h])

    def to_chip(h, s):
        i = {2: 1, 3: 2, 6: 3}[s]
        sums_in[h, i].wait_recv()
        comb[h, i] = plus(block(h, s)[...], sib[h, i]).astype(BF16)
        sums_in[h, s, s] = send(comb.at[h, i], from_y.at[h, i], at(dy=PLACE[s][0]), sum_group[h])

    def go_back(h):
        sums_in[h, 0].wait_recv()
        for s in (2, 3, 6):
            sums_in[h, s, s].wait_recv()
        total = plus(block(h, 0)[...], sib[h, 0], from_y[h, 1], from_y[h, 2], from_y[h, 3]).astype(BF16)
        for b in range(WIDTH // 128):
            stack[pl.ds(b * BLOCK, BLOCK)] = total[:, b * 128:(b + 1) * 128]
        used = WIDTH // 128 * BLOCK
        back_out[h] = nn(pack_ref[:, :used], stack[pl.ds(0, used)]).astype(BF16)
        return exchange(back_out.at[h], back_in.at[h], behind)

    wide = n_pass // 2

    def passage_part(j):
        js = slice(j * wide, (j + 1) * wide)
        low = nn(wt[0, js], agb[:, 0:128])
        high = nn(wt[1, js], agb[:, 0:128])
        pg_ref[js, 0:128] = jnp.where(iota((wide, 128), 1) < 64, low, high).astype(BF16)
        for m in range(2, 5):
            pg_ref[js, CUTS[m - 1]:CUTS[m]] = nn(wt[m, js], agb[:, CUTS[m - 1]:CUTS[m]]).astype(BF16)
        store = pltpu.make_async_copy(pg_ref.at[js], pg_hbm.at[js], lsem.at[1 + j])
        store.start()
        return store

    def gather_near(h):
        gather_pass(agb, h * HALF, BLOCK, got[h], 2)
        gather_pass(agb, h * HALF, BLOCK, got[h], 3)
        got[h][1].wait_recv()

    def gather_rest(h):
        gather_pass(agb, h * HALF, BLOCK, got[h], 6)
        for s in (4, 5, 7):
            got[h][s].wait_recv()

    gather_near(0)
    first_pass(0)
    gather_rest(0)
    first_pass(1)
    totals_to_core(0)
    gather_near(1)
    first_pass(2)
    totals_to_chips(0)
    gather_rest(1)
    first_pass(3)
    totals_to_core(1)
    totals(0)

    second_pass(1, lambda: totals_to_chips(1))
    for s in (7, 4, 5):
        to_core(0, s)
    second_pass(0, lambda: to_chip(0, 6))
    to_core(0, 1)
    to_chip(0, 2)
    to_chip(0, 3)
    totals(1)
    second_pass(3)
    for s in (7, 4, 5):
        to_core(1, s)
    second_pass(2, lambda: to_chip(1, 6))
    to_core(1, 1)
    to_chip(1, 2)
    to_chip(1, 3)
    home = [go_back(0)]
    stores.append(passage_part(0))
    home.append(go_back(1))
    stores.append(passage_part(1))

    for h in range(2):
        home[h]()
        used = WIDTH // 128 * BLOCK
        rows = nn(unpack_ref[:used], back_in[h]).astype(BF16)
        for b in range(WIDTH // 128):
            rows_ref[pl.ds(h * BLOCK, BLOCK), b * 128:(b + 1) * 128] = rows[b * BLOCK:(b + 1) * BLOCK]
    fg[pl.ds(0, lines)] = nn(bsel_ref[...], rows_ref[...]).astype(BF16)
    last = gather_start(fg, 0, lines)

    def write_out(s):
        rows = pl.ds(s * lines, 2 * lines)
        stores.append(pltpu.make_async_copy(fg.at[rows], fg_hbm.at[rows], lsem.at[5 + s // 2]))
        stores[-1].start()

    last[1].wait_recv()
    write_out(0)
    gather_pass(fg, 0, lines, last, 2)
    gather_pass(fg, 0, lines, last, 3)
    write_out(2)
    last[4].wait_recv()
    last[5].wait_recv()
    write_out(4)
    gather_pass(fg, 0, lines, last, 6)
    last[7].wait_recv()
    write_out(6)
    assert len(groups) == ssem.shape[0] and len(received) == rsem.shape[0]
    for store in stores:
        store.wait()
    for g, all_sent in enumerate(groups):
        remote(all_sent, all_sent, g, 0, at(dc=1)).wait_send()


def finish(fsel_hbm, fg_hbm, pg_hbm, qg_hbm, out_hbm, fsel_ref, fg_ref, qg_ref, pg_ref, sems):
    loads = [pltpu.make_async_copy(fsel_hbm, fsel_ref, sems.at[0]), pltpu.make_async_copy(fg_hbm, fg_ref, sems.at[1])]
    for load in loads:
        load.start()
    rows = pg_hbm.shape[0] // PARTS
    parts = [pl.ds(i * rows, rows) for i in range(PARTS)]
    reads = [pltpu.make_async_copy(pg_hbm.at[r], pg_ref.at[r], sems.at[2 + i]) for i, r in enumerate(parts)]
    writes = [pltpu.make_async_copy(pg_ref.at[r], out_hbm.at[r], sems.at[2 + PARTS + i]) for i, r in enumerate(parts)]
    for read in reads:
        read.start()
    for load in loads:
        load.wait()
    for read, write in zip(reads, writes):
        read.wait()
        write.start()
    some = qg_ref.shape[0] // 2
    for i in range(2):
        r = pl.ds(i * some, some)
        qg_ref[r] = nn(fsel_ref[r], fg_ref[...]).astype(BF16)
        write = pltpu.make_async_copy(qg_ref.at[r], qg_hbm.at[r], sems.at[2 + 2 * PARTS + i])
        write.start()
        writes.append(write)
    for write in writes:
        write.wait()


def body(queries, passages, query_cluster, passage_cluster, positive):
    nq, width = queries.shape
    n_pass = passages.shape[0]
    hbm = pl.BlockSpec(memory_space=pl.ANY)
    V = pltpu.VMEM
    fg, fsel, pg = pl.pallas_call(
        kernel,
        out_shape=(jax.ShapeDtypeStruct((nq, width), BF16), jax.ShapeDtypeStruct((nq, nq), BF16),
                   jax.ShapeDtypeStruct((n_pass, width), BF16)),
        in_specs=[hbm] * 5,
        out_specs=(hbm, hbm, hbm),
        scratch_shapes=[
            V((1, nq), I32), V((1, nq), I32), V((1, n_pass), I32), V((nq, width), BF16),
            V((n_pass, width), BF16), V((n_pass, 128), BF16), V((n_pass, 128), BF16), V((width, n_pass), BF16),
            V((STACK, 128), BF16), *[V((2, HALF, 128), BF16)] * 4, V((HALF, STACK), BF16), V((STACK, HALF), BF16),
            V((SLOTS, ROW), BF16), V((PAIR, 128), BF16),
            V((5, n_pass, SLOTS), F32), V((5, n_pass, SLOTS), BF16), V((8, SLOTS), F32),
            *[V((2, 4, 8, 128), F32)] * 4, V((2, 3, 4, 8, 128), F32), V((2, 4, 8, 128), F32),
            V((width, PAIR), BF16), V((SLOTS, width), BF16),
            V((2, 4, BLOCK, width), BF16), V((2, 4, BLOCK, width), BF16), V((2, 4, BLOCK, width), BF16),
            V((2 * BLOCK, width), BF16), V((nq, width), BF16), V((nq // 8, 2 * BLOCK), BF16), V((nq, nq), BF16),
            V((n_pass, width), BF16),
            pltpu.SemaphoreType.DMA((13,)), pltpu.SemaphoreType.DMA((43,)), pltpu.SemaphoreType.DMA((12,)),
        ],
        compiler_params=pltpu.CompilerParams(
            collective_id=0, has_side_effects=True, vmem_limit_bytes=58 * 1024 * 1024),
    )(query_cluster.reshape(1, nq), positive.reshape(1, nq), passage_cluster.reshape(1, n_pass), queries, passages)
    return pl.pallas_call(
        finish,
        out_shape=(jax.ShapeDtypeStruct((nq, width), BF16), jax.ShapeDtypeStruct((n_pass, width), BF16)),
        in_specs=[hbm, hbm, hbm],
        out_specs=(hbm, hbm),
        scratch_shapes=[V((nq, nq), BF16), V((nq, width), BF16), V((nq, width), BF16), V((n_pass, width), BF16),
                        pltpu.SemaphoreType.DMA((4 + 2 * PARTS,))],
        compiler_params=pltpu.CompilerParams(vmem_limit_bytes=58 * 1024 * 1024),
    )(fsel, fg, pg)


def solution(mesh):
    in_specs = (P("dp", None), P(("dp", "tile"), None), P("dp"), P(("dp", "tile")), P("dp"))
    out_specs = (P("dp", None), P(("dp", "tile"), None))
    return jax.shard_map(body, mesh=mesh, in_specs=in_specs, out_specs=out_specs, check_vma=False)
```

```python
import functools
import math

import jax
import jax.numpy as jnp
from jax import lax
from jax.experimental import pallas as pl
from jax.experimental.pallas import tpu as pltpu
from jax.sharding import PartitionSpec as P

F32 = jnp.float32
BF16 = jnp.bfloat16
I32 = jnp.int32

NX, NZ, NY, NC = 4, 8, 4, 2
CL_OWN = 4
CAP = 32
NEGATIVE = -1e30
CUTS = (64, 128, 256, 512, 768)
WIDTH = 768
META = 128
ROW = WIDTH + META
SCALES = tuple(2.0 / math.sqrt(k) for k in CUTS)
LOG2E = math.log2(math.e)
BLOCK = 64
PAIR = 4 * BLOCK
HALF = 8 * BLOCK
SLOTS = 2 * HALF
FAR = NX * NZ
CHUNK = 16
STACK = ROW // 128 * BLOCK

PLACE = ((0, 0), (0, 1), (1, 0), (3, 0), (1, 1), (3, 1), (2, 0), (2, 1))
CHIPS = (0, 1, 3, 2)
MESH = pl.DeviceIdType.MESH
PARTS = 4


def nn(a, b):
    return lax.dot_general(a, b, (((1,), (0,)), ((), ())), preferred_element_type=F32)


def nt(a, b):
    return lax.dot_general(a, b, (((1,), (1,)), ((), ())), preferred_element_type=F32)


def iota(shape, dim):
    return lax.broadcasted_iota(I32, shape, dim)


def onehot(mask):
    return jnp.where(mask, 1.0, 0.0).astype(BF16)


def fold(value, op):
    return op(value.reshape(value.shape[0] // 8, 8, value.shape[1]), axis=0)


def plus(*values):
    return functools.reduce(jnp.add, [v.astype(F32) for v in values])


def shift(a, n):
    return lax.shift_right_logical(a, n)


def kernel(qc_ref, pos_ref, pc_ref, q_hbm, p_hbm, fg_hbm, fsel_hbm, pg_hbm,
           q_ref, p_ref, p0_ref, p1_ref, pt_ref, stack, out_buf, in_buf, back_out, back_in, pack_ref, unpack_ref,
           agb, q0_ref, prob, wt, msc, stat, core_out, core_in, chip_out, chip_in, lse_ref, gt, grad, sib, comb, from_y,
           rows_ref, fg, bsel_ref, fsel_ref, pg_ref,
           ssem, rsem, lsem):
    n_pass = p_ref.shape[0]
    dp = lax.axis_index("dp")
    tile = lax.axis_index("tile")
    x, z = lax.div(dp, NZ), lax.rem(dp, NZ)
    y, core = lax.div(tile, NC), lax.rem(tile, NC)

    def at(dy=0, dc=0):
        return (dp, lax.rem(y + dy, NY) * NC + lax.rem(core + dc, NC))

    places = sorted(((dx, dz) for dx in range(NX) for dz in range(NZ) if dx or dz), key=lambda d: abs(d[1] - NZ // 2))
    x_at = [lax.rem(x + d, NX) * NZ for d in range(NX)]
    z_at = [lax.rem(z + d, NZ) for d in range(NZ)]

    def ahead(dx, dz):
        return (x_at[dx] + z_at[dz], tile)

    def behind(dx, dz):
        return ahead((NX - dx) % NX, (NZ - dz) % NZ)

    groups, received = [], []

    def group(all_sent):
        groups.append(all_sent)
        return len(groups) - 1

    def arrival():
        received.append(None)
        return len(received) - 1

    def remote(src, dst, g, i, where):
        return pltpu.make_async_remote_copy(
            src_ref=src, dst_ref=dst, send_sem=ssem.at[g], recv_sem=rsem.at[i], device_id=where, device_id_type=MESH)

    def send(src, dst, where, g, i=None):
        copy = remote(src, dst, g, arrival() if i is None else i, where)
        copy.start()
        return copy

    def exchange(src, dst, where):
        rest = pl.ds(CHUNK, (FAR - 1) * CHUNK)
        g, n = group(src.at[rest]), arrival()

        for dx, dz in places:
            rows = pl.ds((dx * NZ + dz) * CHUNK, CHUNK)
            remote(src.at[rows], dst.at[rows], g, n, where(dx, dz)).start()
        dst[pl.ds(0, CHUNK)] = src[pl.ds(0, CHUNK)]
        return remote(src.at[rest], dst.at[rest], g, n, at(dc=1)).wait_recv

    barrier = pltpu.get_barrier_semaphore()
    for dx, dz in places:
        pl.semaphore_signal(barrier, inc=1, device_id=ahead(dx, dz), device_id_type=MESH)
    near_by = [(0, 1), (1, 0), (2, 0), (3, 0)]
    for dy, dc in near_by:
        pl.semaphore_signal(barrier, inc=1, device_id=at(dy, dc), device_id_type=MESH)
    load_q = pltpu.make_async_copy(q_hbm, q_ref, lsem.at[3])
    load_q.start()
    load_p = pltpu.make_async_copy(p_hbm, p_ref, lsem.at[0])
    load_p.start()

    nq = q_ref.shape[0]
    cluster = qc_ref[...]
    owner = shift(cluster, 2)
    local = lax.bitwise_and(cluster, 3)
    own = jnp.where(iota((FAR, nq), 0) == owner, 1.0, 0.0)
    before = onehot(iota((nq, nq), 0) < iota((nq, nq), 1))
    rank = jnp.sum(own * nn(own.astype(BF16), before), axis=0, keepdims=True)
    first = jnp.sum(jnp.where(owner < iota((FAR, nq), 0), 1.0, 0.0), axis=1, keepdims=True)
    order = (rank + jnp.sum(own * first, axis=0, keepdims=True)).astype(I32)
    rank = rank.astype(I32)
    carrier = lax.bitwise_and(order, 7)
    line = shift(order, 3)
    dxs = lax.bitwise_and(shift(owner, 3) - x, NX - 1)
    dzs = lax.bitwise_and(lax.bitwise_and(owner, NZ - 1) - z, NZ - 1)
    code = shift(rank, 4) * BLOCK + (dxs * NZ + dzs) * 2 + lax.bitwise_and(shift(rank, 3), 1)
    mine = carrier == tile
    pick = onehot(iota((2 * BLOCK, nq), 0) == jnp.where(mine, code, -1))
    row = iota((META, nq), 0)
    target = lax.bitwise_and(pos_ref[...], 8 * n_pass - 1)
    digits = jnp.where(row == 69, shift(target, 6), jnp.where(row == 70, lax.bitwise_and(target, 63), 0))
    digits = jnp.where((row == local + 64) | (row == 68), 1, digits)
    meta = nt(pick, digits.astype(F32).astype(BF16))
    meta = jnp.where(iota((2 * BLOCK, META), 1) == 68, 1.0 - meta, meta).astype(BF16)
    load_q.wait()
    sent = nn(pick, q_ref[...]).astype(BF16)
    r, c = iota((HALF, STACK), 0), iota((HALF, STACK), 1)
    pack_ref[...] = onehot((shift(lax.bitwise_and(r, CHUNK - 1), 1) == shift(c, 6))
                           & (lax.bitwise_and(c, BLOCK - 1) == shift(r, 4) * 2 + lax.bitwise_and(r, 1)))
    c, r = iota((STACK, HALF), 0), iota((STACK, HALF), 1)
    unpack_ref[...] = onehot((shift(lax.bitwise_and(r, CHUNK - 1), 1) == shift(c, 6))
                             & (lax.bitwise_and(c, BLOCK - 1) == shift(r, 4) * 2 + lax.bitwise_and(r, 1)))
    for h in range(2):
        for b in range(WIDTH // 128):
            stack[pl.ds(b * BLOCK, BLOCK)] = sent[h * BLOCK:(h + 1) * BLOCK, b * 128:(b + 1) * 128]
        stack[pl.ds(STACK - BLOCK, BLOCK)] = meta[h * BLOCK:(h + 1) * BLOCK]
        out_buf[h] = nn(pack_ref[...], stack[...]).astype(BF16)

    pl.semaphore_wait(barrier, len(places) + len(near_by))

    arrived = [exchange(out_buf.at[h], in_buf.at[h], ahead) for h in range(2)]

    clusters = pc_ref[...]
    lane_row = iota((META, n_pass), 0)
    off = jnp.where((lane_row == clusters - CL_OWN * dp + 64) | (lane_row > 68) | (lane_row < 64), 0.0, NEGATIVE)
    load_p.wait()
    lane = iota((n_pass, 128), 1)
    head = p_ref[:, :128].astype(F32)
    p0_ref[...] = jnp.where(lane < 64, head, off.T).astype(BF16)
    p1_ref[...] = jnp.where(lane < 64, 0.0, head).astype(BF16)
    eye = onehot(iota((PAIR, PAIR), 0) == iota((PAIR, PAIR), 1))
    for b in range(WIDTH // PAIR):
        pt_ref[pl.ds(b * PAIR, PAIR)] = nt(eye, p_ref[:, b * PAIR:(b + 1) * PAIR]).astype(BF16)
    lines = nq // 8
    pick_line = onehot(iota((lines, nq), 0) == jnp.where(mine, line, -1))
    bsel_ref[...] = nt(pick_line, pick).astype(BF16)
    cdy = lax.bitwise_and(shift(carrier, 1) - y, NY - 1)
    cdc = lax.bitwise_and(carrier - core, 1)
    place = jnp.where(cdy == 0, cdc, jnp.where(cdy == 2, 6 + cdc, jnp.where(cdy == 1, 2, 3) + 2 * cdc))
    spread = onehot(iota((nq, nq), 0) == place * lines + line)
    fsel_ref[...] = nt(onehot(iota((nq, nq), 0) == iota((nq, nq), 1)), spread).astype(BF16)
    stores = [pltpu.make_async_copy(fsel_ref, fsel_hbm, lsem.at[4])]
    stores[0].start()
    stat[...] = jnp.zeros_like(stat)

    def gather_start(buf, base, rows):
        blk = lambda s: buf.at[pl.ds(base + s * rows, rows)]
        g = group(buf.at[pl.ds(base, 7 * rows)])
        return {0: g, 1: send(blk(0), blk(1), at(dc=1), g), 3: send(blk(0), blk(3), at(dy=1), g),
                2: send(blk(0), blk(2), at(dy=3), g), 6: send(blk(0), blk(6), at(dy=2), g)}

    def gather_pass(buf, base, rows, got, s):
        blk = lambda s: buf.at[pl.ds(base + s * rows, rows)]
        got[s].wait_recv()
        on = {2: 4, 3: 5, 6: 7}[s]
        got[on] = send(blk(s), blk(on), at(dc=1), got[0])

    got = []
    for h in range(2):
        arrived[h]()
        rows = nn(unpack_ref[...], in_buf[h]).astype(BF16)
        for b in range(ROW // 128):
            agb[pl.ds(h * HALF, BLOCK), b * 128:(b + 1) * 128] = rows[b * BLOCK:(b + 1) * BLOCK]
        got.append(gather_start(agb, h * HALF, BLOCK))

    core_group = [group(core_out.at[h]) for h in range(2)]
    core_come = [arrival() for h in range(2)]
    chip_group = [group(chip_in.at[h]) for h in range(2)]
    chip_come = [arrival() for h in range(2)]

    def first_pass(u):
        h, q = u // 2, u % 2
        rows = pl.ds(u * PAIR, PAIR)
        cols = pl.ds(u * PAIR, PAIR)
        q0_ref[...] = jnp.where(iota((PAIR, 128), 1) < 64, agb[rows, 0:128].astype(F32),
                                agb[rows, WIDTH:ROW].astype(F32)).astype(BF16)
        value, tops = None, []
        for m in range(5):
            left = (p0_ref[...], p1_ref[...])[m] if m < 2 else p_ref[:, CUTS[m - 1]:CUTS[m]]
            right = (q0_ref[...], agb[rows, 0:128])[m] if m < 2 else agb[rows, CUTS[m - 1]:CUTS[m]]
            part = nt(left, right)
            value = part if value is None else value + part
            prob[m, :, cols] = value
            tops.append(jnp.max(fold(value, jnp.max), axis=0, keepdims=True))
        small = 128

        def exps(j, sums):
            js = pl.ds(pl.multiple_of(j * small, small), small)
            out = []
            for m in range(5):
                e = jnp.exp2((prob[m, js, cols] - tops[m]) * (SCALES[m] * LOG2E))
                prob[m, js, cols] = e
                out.append(sums[m] + fold(e, jnp.sum))
            return tuple(out)

        sums = lax.fori_loop(0, n_pass // small, exps, (jnp.zeros((8, PAIR), F32),) * 5)
        for m in range(5):
            top = tops[m] * SCALES[m]
            total = jnp.sum(sums[m], axis=0, keepdims=True)
            msc[m:m + 1, cols] = top
            lse = top + jnp.log(total)
            for t in range(2):
                stat[h, 2 * q + t, m:m + 1] = lse[:, t * 128:(t + 1) * 128]

    lower = iota((8, 128), 1) < BLOCK

    def turn(value):
        return pltpu.roll(value, BLOCK, 1)

    def by_chip(a, b):
        return jnp.where(lower, a, turn(b)), jnp.where(lower, turn(a), b)

    def join(values):
        top = functools.reduce(jnp.maximum, values)
        return top + jnp.log(functools.reduce(jnp.add, [jnp.exp(v - top) for v in values]))

    def totals_to_core(h):
        core_out[h, 0] = stat[h, 0]
        core_out[h, 1], core_out[h, 2] = by_chip(stat[h, 1], stat[h, 2])
        core_out[h, 3] = stat[h, 3]
        send(core_out.at[h], core_in.at[h], at(dc=1), core_group[h], core_come[h])

    def totals_to_chips(h):
        remote(core_out.at[h], core_in.at[h], core_group[h], core_come[h], at(dc=1)).wait_recv()
        for t in range(4):
            chip_out[h, t] = join([core_out[h, t], turn(core_in[h, t])])
        for t in (3, 1, 2):
            send(chip_out.at[h], chip_in.at[h, t - 1], at(dy=CHIPS[t]), chip_group[h], chip_come[h])

    def totals(h):
        remote(chip_in.at[h], chip_in.at[h], chip_group[h], chip_come[h], at(dc=1)).wait_recv()
        tiles = []
        for t in range(4):
            values = [chip_out[h, t]]
            for f in (1, 2, 3):
                values.append(chip_in[h, f - 1, CHIPS.index((CHIPS[t] + CHIPS[f]) % NY)])
            tiles.append(join(values))
        lse_ref[h, 0] = tiles[0]
        lse_ref[h, 1], lse_ref[h, 2] = by_chip(tiles[1], tiles[2])
        lse_ref[h, 3] = tiles[3]

    base = tile * n_pass
    pick_digit = jnp.where(iota((8, META), 1) == 69, 64.0,
                           jnp.where(iota((8, META), 1) == 70, 1.0, 0.0)).astype(BF16)

    def second_pass(u, between=None, after_upper=None):
        h, q = u // 2, u % 2
        rows = pl.ds(u * PAIR, PAIR)
        cols = pl.ds(u * PAIR, PAIR)
        goal = nt(pick_digit, agb[rows, WIDTH:ROW])[0:1].astype(I32) - base
        lse = jnp.concatenate([lse_ref[h, 2 * q], lse_ref[h, 2 * q + 1]], axis=1)
        factor = [jnp.exp(msc[m:m + 1, cols] - lse[m:m + 1]) * SCALES[m] for m in range(5)]
        small = 64

        def weigh(j, carry):
            start = pl.multiple_of(j * small, small)
            js = pl.ds(start, small)
            hit = iota((small, PAIR), 0) == goal - start
            running = None
            for m in range(4, -1, -1):
                term = prob[m, js, cols] * factor[m]
                running = term if running is None else running + term
                wt[m, js, cols] = jnp.where(hit, running - sum(SCALES[m:]), running).astype(BF16)
            return carry

        lax.fori_loop(0, n_pass // small, weigh, 0)
        if between is not None:
            between()
        width = PAIR if after_upper is None else PAIR // 2
        for start in range(PAIR - width, -1, -width):
            part = slice(start, start + width)
            for m in range(5):
                lo = CUTS[m - 1] if m else 0
                gt[lo:CUTS[m], part] = nn(pt_ref[lo:CUTS[m]], wt[m, :, u * PAIR + start:u * PAIR + start + width]).astype(BF16)
            grad[pl.ds(u * PAIR + start, width)] = nt(eye[:width, :width], gt[:, part]).astype(BF16)
            if start:
                after_upper()

    sums_in = {}
    sum_group = [group(grad.at[pl.ds(h * HALF, 7 * BLOCK)]) for h in range(2)]

    def block(h, s):
        return grad.at[pl.ds(h * HALF + s * BLOCK, BLOCK)]

    def to_core(h, s):
        i = {1: 0, 4: 1, 5: 2, 7: 3}[s]
        sums_in[h, i] = send(block(h, s), sib.at[h, i], at(dc=1), sum_group[h])

    def to_chip(h, s):
        i = {2: 1, 3: 2, 6: 3}[s]
        sums_in[h, i].wait_recv()
        comb[h, i] = plus(block(h, s)[...], sib[h, i]).astype(BF16)
        sums_in[h, s, s] = send(comb.at[h, i], from_y.at[h, i], at(dy=PLACE[s][0]), sum_group[h])

    def go_back(h):
        sums_in[h, 0].wait_recv()
        for s in (2, 3, 6):
            sums_in[h, s, s].wait_recv()
        total = plus(block(h, 0)[...], sib[h, 0], from_y[h, 1], from_y[h, 2], from_y[h, 3]).astype(BF16)
        for b in range(WIDTH // 128):
            stack[pl.ds(b * BLOCK, BLOCK)] = total[:, b * 128:(b + 1) * 128]
        used = WIDTH // 128 * BLOCK
        back_out[h] = nn(pack_ref[:, :used], stack[pl.ds(0, used)]).astype(BF16)
        return exchange(back_out.at[h], back_in.at[h], behind)

    wide = n_pass // 2

    def passage_part(j):
        js = slice(j * wide, (j + 1) * wide)
        low = nn(wt[0, js], agb[:, 0:128])
        high = nn(wt[1, js], agb[:, 0:128])
        pg_ref[js, 0:128] = jnp.where(iota((wide, 128), 1) < 64, low, high).astype(BF16)
        for m in range(2, 5):
            pg_ref[js, CUTS[m - 1]:CUTS[m]] = nn(wt[m, js], agb[:, CUTS[m - 1]:CUTS[m]]).astype(BF16)
        store = pltpu.make_async_copy(pg_ref.at[js], pg_hbm.at[js], lsem.at[1 + j])
        store.start()
        return store

    def gather_near(h):
        gather_pass(agb, h * HALF, BLOCK, got[h], 2)
        gather_pass(agb, h * HALF, BLOCK, got[h], 3)
        got[h][1].wait_recv()

    def gather_rest(h):
        gather_pass(agb, h * HALF, BLOCK, got[h], 6)
        for s in (4, 5, 7):
            got[h][s].wait_recv()

    gather_near(0)
    first_pass(0)
    gather_rest(0)
    first_pass(1)
    totals_to_core(0)
    gather_near(1)
    first_pass(2)
    totals_to_chips(0)
    gather_rest(1)
    first_pass(3)
    totals_to_core(1)
    totals(0)

    second_pass(1, lambda: totals_to_chips(1))
    for s in (7, 4, 5):
        to_core(0, s)
    second_pass(0, lambda: to_chip(0, 6), lambda: (to_chip(0, 2), to_chip(0, 3)))
    to_core(0, 1)
    totals(1)
    second_pass(3)
    for s in (7, 4, 5):
        to_core(1, s)
    second_pass(2, lambda: to_chip(1, 6), lambda: (to_chip(1, 2), to_chip(1, 3)))
    to_core(1, 1)
    home = [go_back(0)]
    stores.append(passage_part(0))
    home.append(go_back(1))
    stores.append(passage_part(1))

    for h in range(2):
        home[h]()
        used = WIDTH // 128 * BLOCK
        rows = nn(unpack_ref[:used], back_in[h]).astype(BF16)
        for b in range(WIDTH // 128):
            rows_ref[pl.ds(h * BLOCK, BLOCK), b * 128:(b + 1) * 128] = rows[b * BLOCK:(b + 1) * BLOCK]
    fg[pl.ds(0, lines)] = nn(bsel_ref[...], rows_ref[...]).astype(BF16)
    last = gather_start(fg, 0, lines)

    def write_out(s):
        rows = pl.ds(s * lines, 2 * lines)
        stores.append(pltpu.make_async_copy(fg.at[rows], fg_hbm.at[rows], lsem.at[5 + s // 2]))
        stores[-1].start()

    last[1].wait_recv()
    write_out(0)
    gather_pass(fg, 0, lines, last, 2)
    gather_pass(fg, 0, lines, last, 3)
    write_out(2)
    last[4].wait_recv()
    last[5].wait_recv()
    write_out(4)
    gather_pass(fg, 0, lines, last, 6)
    last[7].wait_recv()
    write_out(6)
    assert len(groups) == ssem.shape[0] and len(received) == rsem.shape[0]
    for store in stores:
        store.wait()
    for g, all_sent in enumerate(groups):
        remote(all_sent, all_sent, g, 0, at(dc=1)).wait_send()


def finish(fsel_hbm, fg_hbm, pg_hbm, qg_hbm, out_hbm, fsel_ref, fg_ref, qg_ref, pg_ref, sems):
    loads = [pltpu.make_async_copy(fsel_hbm, fsel_ref, sems.at[0]), pltpu.make_async_copy(fg_hbm, fg_ref, sems.at[1])]
    for load in loads:
        load.start()
    rows = pg_hbm.shape[0] // PARTS
    parts = [pl.ds(i * rows, rows) for i in range(PARTS)]
    reads = [pltpu.make_async_copy(pg_hbm.at[r], pg_ref.at[r], sems.at[2 + i]) for i, r in enumerate(parts)]
    writes = [pltpu.make_async_copy(pg_ref.at[r], out_hbm.at[r], sems.at[2 + PARTS + i]) for i, r in enumerate(parts)]
    for read in reads:
        read.start()
    for load in loads:
        load.wait()
    for read, write in zip(reads, writes):
        read.wait()
        write.start()
    some = qg_ref.shape[0] // 2
    for i in range(2):
        r = pl.ds(i * some, some)
        qg_ref[r] = nn(fsel_ref[r], fg_ref[...]).astype(BF16)
        write = pltpu.make_async_copy(qg_ref.at[r], qg_hbm.at[r], sems.at[2 + 2 * PARTS + i])
        write.start()
        writes.append(write)
    for write in writes:
        write.wait()


def body(queries, passages, query_cluster, passage_cluster, positive):
    nq, width = queries.shape
    n_pass = passages.shape[0]
    vmem = pl.BlockSpec(memory_space=pltpu.VMEM)
    hbm = pl.BlockSpec(memory_space=pl.ANY)
    V = pltpu.VMEM
    fg, fsel, pg = pl.pallas_call(
        kernel,
        out_shape=(jax.ShapeDtypeStruct((nq, width), BF16), jax.ShapeDtypeStruct((nq, nq), BF16),
                   jax.ShapeDtypeStruct((n_pass, width), BF16)),
        in_specs=[vmem, vmem, vmem, hbm, hbm],
        out_specs=(hbm, hbm, hbm),
        scratch_shapes=[
            V((nq, width), BF16),
            V((n_pass, width), BF16), V((n_pass, 128), BF16), V((n_pass, 128), BF16), V((width, n_pass), BF16),
            V((STACK, 128), BF16), *[V((2, HALF, 128), BF16)] * 4, V((HALF, STACK), BF16), V((STACK, HALF), BF16),
            V((SLOTS, ROW), BF16), V((PAIR, 128), BF16),
            V((5, n_pass, SLOTS), F32), V((5, n_pass, SLOTS), BF16), V((8, SLOTS), F32),
            *[V((2, 4, 8, 128), F32)] * 4, V((2, 3, 4, 8, 128), F32), V((2, 4, 8, 128), F32),
            V((width, PAIR), BF16), V((SLOTS, width), BF16),
            V((2, 4, BLOCK, width), BF16), V((2, 4, BLOCK, width), BF16), V((2, 4, BLOCK, width), BF16),
            V((2 * BLOCK, width), BF16), V((nq, width), BF16), V((nq // 8, 2 * BLOCK), BF16), V((nq, nq), BF16),
            V((n_pass, width), BF16),
            pltpu.SemaphoreType.DMA((13,)), pltpu.SemaphoreType.DMA((43,)), pltpu.SemaphoreType.DMA((9,)),
        ],
        compiler_params=pltpu.CompilerParams(
            collective_id=0, has_side_effects=True, vmem_limit_bytes=58 * 1024 * 1024),
    )(query_cluster.reshape(1, nq), positive.reshape(1, nq), passage_cluster.reshape(1, n_pass), queries, passages)
    return pl.pallas_call(
        finish,
        out_shape=(jax.ShapeDtypeStruct((nq, width), BF16), jax.ShapeDtypeStruct((n_pass, width), BF16)),
        in_specs=[hbm, hbm, hbm],
        out_specs=(hbm, hbm),
        scratch_shapes=[V((nq, nq), BF16), V((nq, width), BF16), V((nq, width), BF16), V((n_pass, width), BF16),
                        pltpu.SemaphoreType.DMA((4 + 2 * PARTS,))],
        compiler_params=pltpu.CompilerParams(vmem_limit_bytes=58 * 1024 * 1024),
    )(fsel, fg, pg)


def solution(mesh):
    in_specs = (P("dp", None), P(("dp", "tile"), None), P("dp"), P(("dp", "tile")), P("dp"))
    out_specs = (P("dp", None), P(("dp", "tile"), None))
    return jax.shard_map(body, mesh=mesh, in_specs=in_specs, out_specs=out_specs, check_vma=False)
```
